256 devices in a mesh: seg: 64 (over z_hi, x, y, core), det: 4 (over z_lo).
Axes of the slice: x: 4, y: 4, z: 8 (z_hi: 2, z_lo: 4; z = z_hi * 4 + z_lo), core: 2. Of those that a mesh axis runs over, the one named last changes fastest.
Arguments:
- strain: float32 [196608, 1024], P('seg', 'det'), may hold values from -6 to 6
- row_target: int32 [196608], P('seg'), may hold values from -1 to 98303, as said below
- gate_start: int32 [64, 3], P('seg'), may hold values from 0 to 458752
- gate_width: int32 [64, 3], P('seg'), may hold values from 8192 to 65536
- inverse_psd: float32 [3, 512, 512], P(None, 'det'), may hold values from 0.2 to 2
- templates: bfloat16 [256, 512, 2, 512], P('seg', 'det'), may hold values from -6 to 6
- template_shift: int32 [256], P('seg'), may hold values from 0 to 1023
Outputs:
- snr: bfloat16 [64, 4, 3, 256, 2, 1024], P('seg', 'det')
The draws below stay inside these ranges and needn't reach their ends.
Inputs may be any that keep to these rules, and one draw needn't show every extreme that they name: `row_target`: each segment row s * 3 * 512 + r with 0 <= r < 1536 stands in exactly one slot and every other slot holds -1. A reader holds equally many rows of every segment, at most 48, and some reader holds exactly 48 rows of each segment.
All inputs are finite; a program needn't handle non-finite values.
Results may differ from the reference program's by a relative error of at most 0.011.
Values may be sent and summed in bfloat16 or wider, within the bound.
A program may use at most 128 MiB of HBM per device.

```python
import math
import jax
import jax.numpy as jnp
from jax import lax

V = 512
U = 1024
DETECTORS = 3
BLOCK = 4
STEPS = 3
SEGMENTS = 64
SAMPLES = 524288
TEMPLATES = 256
SLOTS = 3072


def draw_row_target(key, part):
    key = jax.random.fold_in(key, 7)
    load_key, order_key, slot_key = jax.random.split(key, 3)
    seg_rows = DETECTORS * V
    unit_rows = seg_rows // (2 * SEGMENTS)
    capacity = 4 * unit_rows
    pattern = jnp.tile(jnp.array([1, 1, 2, 4], jnp.int32), SEGMENTS // 4)
    reader_loads = jax.random.permutation(load_key, pattern)
    offsets = (jnp.cumsum(reader_loads) - reader_loads) * unit_rows
    orders = jax.vmap(lambda subkey: jax.random.permutation(subkey, seg_rows))(jax.random.split(order_key, SEGMENTS))
    position = jnp.arange(capacity, dtype=jnp.int32)
    is_live = position[None, None, :] < (reader_loads * unit_rows)[:, None, None]
    row_index = jnp.minimum(offsets[:, None, None] + position[None, None, :], seg_rows - 1)
    owners = jnp.arange(SEGMENTS, dtype=jnp.int32)[None, :, None]
    picked = orders[owners, row_index]
    target = jnp.where(is_live, owners * seg_rows + picked, -1).reshape(SEGMENTS, SEGMENTS * capacity)
    shuffled = jax.vmap(lambda subkey, target_row: jax.random.permutation(subkey, target_row))(jax.random.split(slot_key, SEGMENTS), target)
    return shuffled.reshape(-1).astype(jnp.int32)


def touch_ends(result, own_key, least, top_value):
    longest = result.shape.index(max(result.shape))
    spots = []
    for shift in (0, 1):
        where = [jax.random.randint(jax.random.fold_in(own_key, axis), (), 0, length) for axis, length in enumerate(result.shape)]
        where[longest] = (where[longest] + shift) % result.shape[longest]
        spots.append(tuple(where))
    return result.at[spots[0]].set(least).at[spots[1]].set(top_value)


def block_levels(stream_key, extent, shards, low, high):
    def one(dim, blocks):
        heights = jax.random.uniform(jax.random.fold_in(jax.random.fold_in(stream_key, 6), dim), (blocks,), jnp.float32, low / len(shards), high / len(shards))
        return jnp.repeat(jnp.exp(heights), extent[dim] // blocks).reshape((-1,) + (1,) * (len(extent) - dim - 1))

    loudness = one(*shards[0])
    for cut in shards[1:]:
        loudness = loudness * one(*cut)
    return loudness


def scatter_about(own_key, dims, scale, reach, cuts=(), held_as=jnp.bfloat16):
    gain = block_levels(own_key, dims, cuts, -0.22, 0.18) if cuts else 1.0
    values = jax.random.normal(own_key, dims, jnp.float32) * scale * gain
    return jnp.minimum(jnp.maximum(values, -reach), reach).astype(held_as)


def setup_inputs(seed: int = 0) -> dict:
    key_list = jax.random.split(jax.random.key(seed), 8)
    return {
        "strain": scatter_about(key_list[0], (SEGMENTS * SLOTS, U), 1.0, 6.0, ((0, 64), (1, 4)), jnp.float32),
        "row_target": draw_row_target(jax.random.fold_in(key_list[7], 71), 0),
        "gate_start": touch_ends(jax.random.randint(key_list[2], (SEGMENTS, DETECTORS), 0, SAMPLES - SAMPLES // 8 + 1), jax.random.fold_in(key_list[2], 1), 0, (SAMPLES - SAMPLES // 8 + 1) - 1).astype(jnp.int32),
        "gate_width": touch_ends(jax.random.randint(key_list[3], (SEGMENTS, DETECTORS), SAMPLES // 64, SAMPLES // 8 + 1), jax.random.fold_in(key_list[3], 1), SAMPLES // 64, (SAMPLES // 8 + 1) - 1).astype(jnp.int32),
        "inverse_psd": jnp.clip(jnp.exp(math.log(2.0) - 2.3025851 * jax.random.uniform(key_list[4], (DETECTORS, V, U // 2), jnp.float32) ** block_levels(key_list[4], (DETECTORS, V, U // 2), ((1, 4),), -0.2, 0.2)), 0.2, 2.0),
        "templates": scatter_about(key_list[5], (TEMPLATES, V, 2, U // 2), 1.0, 6.0, ((0, 64), (1, 4))),
        "template_shift": touch_ends(jax.random.randint(key_list[6], (TEMPLATES,), 0, U), jax.random.fold_in(key_list[6], 1), 0, U - 1).astype(jnp.int32),
    }


def phases(row_index, col_index, modulus, direction):
    residue = row_index[:, None] * col_index[None, :] % modulus
    phase_angle = direction * 2.0 * math.pi / modulus * residue.astype(jnp.float32)
    return (jnp.cos(phase_angle), jnp.sin(phase_angle))

def rotate(real_part, imag_part, cosine, sine_value):
    return (real_part * cosine - imag_part * sine_value, real_part * sine_value + imag_part * cosine)

def rotation_table(row_index, col_index, modulus, direction, scaling):
    cosine, sine_value = phases(row_index, col_index, modulus, direction)
    upper_rows = jnp.concatenate([cosine, sine_value], axis=1)
    lower_rows = jnp.concatenate([-sine_value, cosine], axis=1)
    return (jnp.concatenate([upper_rows, lower_rows], axis=0) * scaling).astype(jnp.bfloat16)

def row_transform(depth, direction):
    depth_index = jnp.arange(depth, dtype=jnp.int32)
    cosine, sine_value = phases(depth_index, depth_index, depth, direction)
    return (jnp.stack([cosine, sine_value], axis=1) / math.sqrt(depth)).astype(jnp.bfloat16)

def output_table(depth):
    middle_rows = jnp.arange(depth // 4, 3 * depth // 4, dtype=jnp.int32)
    cosine, sine_value = phases(middle_rows, jnp.arange(depth, dtype=jnp.int32), depth, 1.0)
    table = jnp.stack([jnp.stack([cosine, -sine_value], axis=1), jnp.stack([sine_value, cosine], axis=1)], axis=1)
    return (table / math.sqrt(depth)).astype(jnp.bfloat16)

def shift_template(template, shift_value, bin_index):
    residue = bin_index * shift_value % SAMPLES
    phase_angle = -2.0 * math.pi / SAMPLES * residue.astype(jnp.float32)
    real_part, imag_part = rotate(template[:, 0].astype(jnp.float32), template[:, 1].astype(jnp.float32), jnp.cos(phase_angle), jnp.sin(phase_angle))
    return jnp.stack([real_part, imag_part], axis=1).astype(jnp.bfloat16)

def correlate(coherent, template):
    real_part = coherent[:, 0] * template[..., 0, :] + coherent[:, 1] * template[..., 1, :]
    imag_part = coherent[:, 1] * template[..., 0, :] - coherent[:, 0] * template[..., 1, :]
    return jnp.stack([real_part, imag_part], axis=-2).astype(jnp.bfloat16)

def reference(strain, row_target, gate_start, gate_width, inverse_psd, templates, template_shift):
    seg_rows = DETECTORS * V
    total_rows = SEGMENTS * seg_rows
    destination = jnp.where(row_target >= 0, row_target, total_rows)
    placed = jnp.zeros((total_rows + 1, U), jnp.float32).at[destination].set(strain)[:total_rows]
    placed = placed.reshape(SEGMENTS, DETECTORS, V, U)
    depth_index = jnp.arange(V, dtype=jnp.int32)
    full_columns = jnp.arange(U, dtype=jnp.int32)
    half_columns = jnp.arange(U // 2, dtype=jnp.int32)
    sample_index = depth_index[:, None] * U + full_columns[None, :]
    forward_rows = row_transform(V, -1.0).astype(jnp.float32)
    twist_cos, twist_sin = phases(depth_index, full_columns, SAMPLES, -1.0)
    forward_columns = rotation_table(full_columns, half_columns, U, -1.0, 1.0 / math.sqrt(U))
    inverse_columns = rotation_table(half_columns, full_columns, U, 1.0, 1.0 / math.sqrt(U))
    back_cos, back_sin = phases(depth_index, full_columns, SAMPLES, 1.0)
    last_rows = output_table(V).astype(jnp.float32)
    bin_index = depth_index[:, None] + V * half_columns[None, :]
    shifted = lax.map(lambda template_pair: shift_template(template_pair[0], template_pair[1], bin_index), (templates, template_shift))
    shifted = shifted.reshape(SEGMENTS, BLOCK, V, 2, U // 2)

    def one_segment(segment):
        segment_rows = placed[segment]
        gate_begin = gate_start[segment][:, None, None]
        gate_end = gate_begin + gate_width[segment][:, None, None]
        inside = (sample_index[None] >= gate_begin) & (sample_index[None] < gate_end)
        gated_rows = jnp.where(inside, 0.0, segment_rows).astype(jnp.bfloat16)
        first_section = jnp.einsum('krv,dvu->dkru', forward_rows, gated_rows.astype(jnp.float32))
        real_first, imag_first = rotate(first_section[:, :, 0], first_section[:, :, 1], twist_cos, twist_sin)
        turned = jnp.stack([real_first, imag_first], axis=2).astype(jnp.bfloat16)
        spectrum = jnp.dot(turned.reshape(DETECTORS * V, 2 * U), forward_columns, preferred_element_type=jnp.float32).reshape(DETECTORS, V, 2, U // 2)
        coherent = lax.optimization_barrier(jnp.sum(inverse_psd[:, :, None, :] * spectrum, axis=0))
        block_ids = (segment + jnp.arange(STEPS, dtype=jnp.int32)) % SEGMENTS
        chosen = jnp.swapaxes(shifted[block_ids], 0, 1).reshape(BLOCK * STEPS, V, 2, U // 2)

        def one_template(template):
            product = correlate(coherent, template)
            series = jnp.dot(product.reshape(V, U), inverse_columns, preferred_element_type=jnp.float32).reshape(V, 2, U)
            real_back, imag_back = rotate(series[:, 0], series[:, 1], back_cos, back_sin)
            turned_back = jnp.stack([real_back, imag_back], axis=1).astype(jnp.bfloat16)
            return jnp.einsum('vpqk,kqu->vpu', last_rows, turned_back.astype(jnp.float32)).astype(jnp.bfloat16)
        return lax.map(one_template, chosen).reshape(BLOCK, STEPS, V // 2, 2, U)
    return lax.map(one_segment, jnp.arange(SEGMENTS, dtype=jnp.int32))
```

```python
import functools
import math

import jax
import jax.numpy as jnp
import numpy as np
from jax import lax
from jax.experimental import pallas as pl
from jax.experimental.pallas import tpu as pltpu
from jax.sharding import PartitionSpec as P

V = 512
U = 1024
DETECTORS = 3
BLOCK = 4
STEPS = 3
SAMPLES = 524288
SEGS = 64
DETS = 4
SLOTS = 3072
CAP = 48
QU = U // DETS
QV = V // DETS
ROWS = DETECTORS * V
HALF = U // 2
MESH = pl.DeviceIdType.MESH
F32 = jnp.float32
BF16 = jnp.bfloat16
LIMIT = 60 * 1024 * 1024
VM = pl.BlockSpec(memory_space=pltpu.VMEM)
SM = pl.BlockSpec(memory_space=pltpu.SMEM)
HB = pl.BlockSpec(memory_space=pl.ANY)


def angles(rows, cols, modulus, direction):
    residue = (rows[:, None].astype(np.int64) * cols[None, :]) % modulus
    angle = np.float32(direction * 2.0 * math.pi / modulus) * residue.astype(np.float32)
    return np.cos(angle), np.sin(angle)


@functools.cache
def tables():
    v, u, m = np.arange(V), np.arange(U), np.arange(HALF)
    bf = np.dtype(jnp.bfloat16)
    c, s = angles(v, v, V, -1.0)
    row = (np.concatenate([c, s], 0) / math.sqrt(V)).astype(bf)
    twist = np.stack([*angles(v, u, SAMPLES, -1.0)])
    twist = twist.reshape(2, V, DETS, QU).transpose(2, 0, 1, 3).astype(np.float32)
    c, s = angles(u, m, U, -1.0)
    col = np.stack([np.concatenate([c, s], 1), np.concatenate([-s, c], 1)])
    col = (col / math.sqrt(U)).reshape(2, DETS, QU, U).transpose(1, 0, 2, 3)
    col = col.reshape(DETS, 2 * QU, U).astype(bf)
    c, s = angles(m, u, U, 1.0)
    back = np.concatenate([np.concatenate([c, s], 1), np.concatenate([-s, c], 1)], 0)
    back = (back / math.sqrt(U)).astype(bf)
    untwist = np.stack([*angles(v, u, SAMPLES, 1.0)]).astype(np.float32)
    c, s = angles(np.arange(V // 4, 3 * V // 4), v, V, 1.0)
    last = np.stack([np.concatenate([c, -s], 1), np.concatenate([s, c], 1)], 1)
    last = (last / math.sqrt(V)).reshape(V, 2 * V).astype(bf)
    return row, twist, col, back, untwist, last


def sort_kernel(me_ref, target_ref, strain_ref, rows_ref, ids_ref, held, dest):
    held[...] = strain_ref[...].astype(BF16)
    block = 256
    count = SLOTS // block
    lane = lax.broadcasted_iota(jnp.int32, (block, block), 1)
    sub = lax.broadcasted_iota(jnp.int32, (block, block), 0)
    upper = jnp.where(sub <= lane, 1.0, 0.0).astype(BF16)
    seg = lax.broadcasted_iota(jnp.int32, (SEGS, block), 0)
    carry = jnp.zeros((SEGS, 1), F32)
    high = jnp.zeros((SEGS, SEGS), F32)
    low = jnp.zeros((SEGS, SEGS), F32)
    for b in range(count):
        t = target_ref[b : b + 1, :]
        owner = ((t >> 9) * 43691) >> 17
        owner = jnp.where(t >= 0, owner, SEGS)
        local = t - owner * ROWS
        mine = jnp.where(seg == owner, 1.0, 0.0)
        before = jnp.dot(mine.astype(BF16), upper, preferred_element_type=F32)
        rank = jnp.sum(mine * (before + carry), axis=0, keepdims=True).astype(jnp.int32) - 1
        carry = carry + jnp.sum(mine, axis=1, keepdims=True)
        dest[b : b + 1, :] = jnp.where(t >= 0, owner * CAP + rank, -1)
        order = jnp.where(seg == rank, 1.0, 0.0).astype(BF16)
        spread = (((1,), (1,)), ((), ()))
        upper_part = (mine * ((local >> 6) + 1).astype(F32)).astype(BF16)
        lower_part = (mine * (local & 63).astype(F32)).astype(BF16)
        high = high + lax.dot_general(upper_part, order, spread, preferred_element_type=F32)
        low = low + lax.dot_general(lower_part, order, spread, preferred_element_type=F32)
    ids = jnp.where(high > 0.5, high * 64.0 + low - 63.0, 0.0).astype(jnp.int32)
    ids = jnp.concatenate([ids, ids], axis=1)
    side = lax.broadcasted_iota(jnp.int32, (SEGS, 128), 1) // 64
    parity = (lax.broadcasted_iota(jnp.int32, (SEGS, 128), 0) + me_ref[0]) & 1
    ids_ref[...] = jnp.where(side == parity, ids, 0)
    step = 512

    def place(i, _):
        want = lax.broadcasted_iota(jnp.int32, (step, block), 0) + i * step
        chosen = [
            jnp.where(want == dest[b : b + 1, :], 1.0, 0.0).astype(BF16) for b in range(count)
        ]
        rows = jnp.dot(jnp.concatenate(chosen, axis=1), held[...], preferred_element_type=F32)
        rows_ref[pl.ds(i * step, step), :] = rows.astype(BF16)
        return 0

    lax.fori_loop(0, SLOTS // step, place, 0)


def sort_rows(me, target, strain):
    return pl.pallas_call(
        sort_kernel,
        out_shape=(
            jax.ShapeDtypeStruct((SLOTS, QU), BF16),
            jax.ShapeDtypeStruct((SEGS, 128), jnp.int32),
        ),
        in_specs=[SM, VM, VM],
        out_specs=(VM, VM),
        scratch_shapes=[
            pltpu.VMEM((SLOTS, QU), BF16),
            pltpu.VMEM((SLOTS // 256, 256), jnp.int32),
        ],
        compiler_params=pltpu.CompilerParams(vmem_limit_bytes=LIMIT),
        cost_estimate=pl.CostEstimate(
            flops=2 * SLOTS * SLOTS * QU, bytes_accessed=SLOTS * QU * 6, transcendentals=0
        ),
        name="sort_rows",
    )(me, target, strain)


GROUP = 16


def route_kernel(
    rows_ref, ids_ref, bank_ref, placed_ref, full_ref,
    arrived, arrived_ids, chosen, total,
    row_send, row_recv, id_send, id_recv, bank_send, bank_recv, own_sem,
):
    me = lax.axis_index("seg")
    det = lax.axis_index("det")
    barrier = pltpu.get_barrier_semaphore()

    def greet(o, _):
        pl.semaphore_signal(
            barrier, inc=1, device_id={"seg": (me + o) % SEGS}, device_id_type=MESH
        )
        return 0

    lax.fori_loop(1, SEGS, greet, 0)
    for o in range(1, DETS):
        pl.semaphore_signal(
            barrier, inc=1, device_id={"det": (det + o) % DETS}, device_id_type=MESH
        )
    own_rows = pltpu.make_async_copy(rows_ref.at[me], arrived.at[0, pl.ds(0, CAP)], own_sem.at[0])
    own_rows.start()
    own_ids = pltpu.make_async_copy(ids_ref.at[me], arrived_ids.at[0], own_sem.at[1])
    own_ids.start()
    own_bank = pltpu.make_async_copy(
        bank_ref.at[det], full_ref.at[pl.ds(det * QV, QV)], own_sem.at[2]
    )
    own_bank.start()
    arrived[:, CAP:, :] = jnp.zeros((SEGS, 64 - CAP, QU), BF16)
    pl.semaphore_wait(barrier, SEGS + DETS - 2)

    def bank_copy(o):
        other = (det + o) % DETS
        return pltpu.make_async_remote_copy(
            src_ref=bank_ref.at[other],
            dst_ref=full_ref.at[pl.ds(det * QV, QV)],
            send_sem=bank_send.at[o],
            recv_sem=bank_recv.at[o],
            device_id={"det": other},
            device_id_type=MESH,
        )

    def row_copy(o):
        other = (me + o) % SEGS
        return pltpu.make_async_remote_copy(
            src_ref=rows_ref.at[other],
            dst_ref=arrived.at[o, pl.ds(0, CAP)],
            send_sem=row_send.at[o],
            recv_sem=row_recv.at[o],
            device_id={"seg": other},
            device_id_type=MESH,
        )

    def id_copy(o):
        other = (me + o) % SEGS
        return pltpu.make_async_remote_copy(
            src_ref=ids_ref.at[other],
            dst_ref=arrived_ids.at[o],
            send_sem=id_send.at[o],
            recv_sem=id_recv.at[o],
            device_id={"seg": other},
            device_id_type=MESH,
        )

    def send(o, _):
        id_copy(o).start()
        row_copy(o).start()
        return 0

    lax.fori_loop(1, SEGS, send, 0)
    for o in range(1, DETS):
        bank_copy(o).start()
    own_rows.wait()
    own_ids.wait()

    def receive(o, _):
        id_copy(o).wait_recv()
        row_copy(o).wait_recv()
        return 0

    wide = GROUP * 64

    for g in range(SEGS // GROUP):
        lax.fori_loop(max(1, g * GROUP), (g + 1) * GROUP, receive, 0)
        idents = [
            arrived_ids[g * GROUP + 2 * p] + arrived_ids[g * GROUP + 2 * p + 1] - 1
            for p in range(GROUP // 2)
        ]
        for p in range(GROUP // 2):
            chosen[:, p * 128 : (p + 1) * 128] = jnp.where(
                lax.broadcasted_iota(jnp.int32, (ROWS, 128), 0) == idents[p], 1.0, 0.0
            ).astype(BF16)
        block = arrived[g * GROUP : (g + 1) * GROUP].reshape(wide, QU)
        part = jnp.dot(chosen[...], block, preferred_element_type=F32)
        if g == 0:
            total[...] = part
        elif g < SEGS // GROUP - 1:
            total[...] += part
        else:
            placed_ref[...] = (total[...] + part).astype(BF16)

    own_bank.wait()
    for o in range(1, DETS):
        bank_copy(o).wait()

    def sent(o, _):
        id_copy(o).wait_send()
        row_copy(o).wait_send()
        return 0

    lax.fori_loop(1, SEGS, sent, 0)


def route_rows(rows, ids, bank):
    return pl.pallas_call(
        route_kernel,
        out_shape=(
            jax.ShapeDtypeStruct((ROWS, QU), BF16),
            jax.ShapeDtypeStruct((V, U), BF16),
        ),
        in_specs=[VM, VM, HB],
        out_specs=(VM, HB),
        scratch_shapes=[
            pltpu.VMEM((SEGS, 64, QU), BF16),
            pltpu.VMEM((SEGS, 1, 128), jnp.int32),
            pltpu.VMEM((ROWS, GROUP * 64), BF16),
            pltpu.VMEM((ROWS, QU), F32),
            pltpu.SemaphoreType.DMA((SEGS,)),
            pltpu.SemaphoreType.DMA((SEGS,)),
            pltpu.SemaphoreType.DMA((SEGS,)),
            pltpu.SemaphoreType.DMA((SEGS,)),
            pltpu.SemaphoreType.DMA((DETS,)),
            pltpu.SemaphoreType.DMA((DETS,)),
            pltpu.SemaphoreType.DMA((3,)),
        ],
        compiler_params=pltpu.CompilerParams(
            vmem_limit_bytes=LIMIT, collective_id=0, has_side_effects=True
        ),
        cost_estimate=pl.CostEstimate(
            flops=2 * ROWS * 4096 * QU, bytes_accessed=SLOTS * QU * 4, transcendentals=0
        ),
        name="route_rows",
    )(rows, ids, bank)


def section_kernel(
    gate_ref, shift_ref, placed_ref, full_ref, row_ref, twist_ref, turned_ref, shifted_ref,
    twist, sem,
):
    det = lax.axis_index("det")
    fetch = pltpu.make_async_copy(twist_ref.at[det], twist, sem)
    fetch.start()
    shift = shift_ref[det]
    k = lax.broadcasted_iota(jnp.int32, (V, 128), 0)
    angle = (-2.0 * math.pi / SAMPLES) * ((k * shift) % SAMPLES).astype(F32)
    row_cos, row_sin = jnp.cos(angle)[:, :1], jnp.sin(angle)[:, :1]
    m = lax.broadcasted_iota(jnp.int32, (8, HALF), 1)
    angle = (-2.0 * math.pi / U) * ((m * shift) % U).astype(F32)
    col_cos, col_sin = jnp.cos(angle)[:1], jnp.sin(angle)[:1]
    real = full_ref[:, :HALF].astype(F32)
    imag = full_ref[:, HALF:].astype(F32)
    cosine = row_cos * col_cos - row_sin * col_sin
    sine = row_cos * col_sin + row_sin * col_cos
    shifted_ref[:, :HALF] = (real * cosine - imag * sine).astype(BF16)
    shifted_ref[:, HALF:] = (real * sine + imag * cosine).astype(BF16)
    sample = lax.broadcasted_iota(jnp.int32, (V, QU), 0) * U
    sample = sample + lax.broadcasted_iota(jnp.int32, (V, QU), 1) + det * QU
    fetch.wait()
    for d in range(DETECTORS):
        begin = gate_ref[0, d]
        end = begin + gate_ref[1, d]
        inside = (sample >= begin) & (sample < end)
        gated = jnp.where(inside, 0.0, placed_ref[d * V : (d + 1) * V].astype(F32)).astype(BF16)
        folded = jnp.dot(row_ref[...], gated, preferred_element_type=F32)
        real, imag = folded[:V], folded[V:]
        cosine, sine = twist[0], twist[1]
        first = (real * cosine - imag * sine).astype(BF16)
        second = (real * sine + imag * cosine).astype(BF16)
        for q in range(DETS):
            turned_ref[q, d * QV : (d + 1) * QV, :QU] = first[q * QV : (q + 1) * QV]
            turned_ref[q, d * QV : (d + 1) * QV, QU:] = second[q * QV : (q + 1) * QV]


def first_section(gates, shift, placed, full, row, twist):
    return pl.pallas_call(
        section_kernel,
        out_shape=(
            jax.ShapeDtypeStruct((DETS, DETECTORS * QV, 2 * QU), BF16),
            jax.ShapeDtypeStruct((V, U), BF16),
        ),
        in_specs=[SM, SM, VM, VM, VM, HB],
        out_specs=(VM, VM),
        scratch_shapes=[pltpu.VMEM((2, V, QU), F32), pltpu.SemaphoreType.DMA],
        compiler_params=pltpu.CompilerParams(vmem_limit_bytes=LIMIT),
        name="first_section",
    )(gates, shift, placed, full, row, twist)


def spectrum_kernel(
    turned_ref, shifted_ref, psd_ref, col_ref, coherent_ref, next_ref, after_ref,
    arrived, mine, total, turn_send, turn_recv, coh_send, coh_recv, pass_send, pass_recv, own_sem,
):
    me = lax.axis_index("seg")
    det = lax.axis_index("det")
    barrier = pltpu.get_barrier_semaphore()
    for o in (1, 2, SEGS - 2, SEGS - 1):
        pl.semaphore_signal(
            barrier, inc=1, device_id={"seg": (me + o) % SEGS}, device_id_type=MESH
        )
    for o in range(1, DETS):
        pl.semaphore_signal(
            barrier, inc=1, device_id={"det": (det + o) % DETS}, device_id_type=MESH
        )
    own = pltpu.make_async_copy(turned_ref.at[det], arrived.at[0], own_sem.at[0])
    own.start()
    pl.semaphore_wait(barrier, 4 + DETS - 1)

    def turn_copy(o):
        other = (det + o) % DETS
        return pltpu.make_async_remote_copy(
            src_ref=turned_ref.at[other],
            dst_ref=arrived.at[o],
            send_sem=turn_send.at[o],
            recv_sem=turn_recv.at[o],
            device_id={"det": other},
            device_id_type=MESH,
        )

    def pass_copy(o, dst_ref):
        return pltpu.make_async_remote_copy(
            src_ref=shifted_ref,
            dst_ref=dst_ref,
            send_sem=pass_send.at[o],
            recv_sem=pass_recv.at[o],
            device_id={"seg": (me + SEGS - o) % SEGS},
            device_id_type=MESH,
        )

    def coherent_copy(o):
        return pltpu.make_async_remote_copy(
            src_ref=mine,
            dst_ref=coherent_ref.at[pl.ds(det * QV, QV)],
            send_sem=coh_send.at[o],
            recv_sem=coh_recv.at[o],
            device_id={"det": (det + o) % DETS},
            device_id_type=MESH,
        )

    for o in (2, 1, 3):
        turn_copy(o).start()
    pass_copy(1, next_ref).start()
    pass_copy(2, after_ref).start()
    own.wait()
    total[...] = jnp.dot(arrived[0], col_ref[det], preferred_element_type=F32)
    for o in (1, 3, 2):
        turn_copy(o).wait_recv()
        part = jnp.dot(
            arrived[o], col_ref[(det + DETS - o) % DETS], preferred_element_type=F32
        )
        total[...] += part
    for half in range(2):
        cols = slice(half * HALF, (half + 1) * HALF)
        value = psd_ref[0] * total[:QV, cols]
        for d in range(1, DETECTORS):
            value = value + psd_ref[d] * total[d * QV : (d + 1) * QV, cols]
        mine[:, cols] = value.astype(BF16)
    for o in (2, 1, 3):
        coherent_copy(o).start()
    keep = pltpu.make_async_copy(mine, coherent_ref.at[pl.ds(det * QV, QV)], own_sem.at[1])
    keep.start()
    for o in (1, 2, 3):
        turn_copy(o).wait_send()
        coherent_copy(o).wait()
    keep.wait()
    pass_copy(1, next_ref).wait()
    pass_copy(2, after_ref).wait()


def spectra(turned, shifted, psd, col):
    bank = jax.ShapeDtypeStruct((V, U), BF16)
    return pl.pallas_call(
        spectrum_kernel,
        out_shape=(bank, bank, bank),
        in_specs=[VM, HB, VM, VM],
        out_specs=(HB, HB, HB),
        scratch_shapes=[
            pltpu.VMEM((DETS, DETECTORS * QV, 2 * QU), BF16),
            pltpu.VMEM((QV, U), BF16),
            pltpu.VMEM((DETECTORS * QV, U), F32),
            pltpu.SemaphoreType.DMA((DETS,)),
            pltpu.SemaphoreType.DMA((DETS,)),
            pltpu.SemaphoreType.DMA((DETS,)),
            pltpu.SemaphoreType.DMA((DETS,)),
            pltpu.SemaphoreType.DMA((STEPS,)),
            pltpu.SemaphoreType.DMA((STEPS,)),
            pltpu.SemaphoreType.DMA((2,)),
        ],
        compiler_params=pltpu.CompilerParams(
            vmem_limit_bytes=LIMIT, collective_id=1, has_side_effects=True
        ),
        cost_estimate=pl.CostEstimate(
            flops=2 * DETECTORS * QV * 2 * U * U, bytes_accessed=8 * V * U, transcendentals=0
        ),
        name="spectra",
    )(turned, shifted, psd, col)


def inverse_kernel(coherent_ref, shifted_ref, back_ref, untwist_ref, last_ref, out_ref, partial):
    real, imag = coherent_ref[:, :HALF].astype(F32), coherent_ref[:, HALF:].astype(F32)
    other_real = shifted_ref[:, :HALF].astype(F32)
    other_imag = shifted_ref[:, HALF:].astype(F32)
    product = jnp.concatenate(
        [
            (real * other_real + imag * other_imag).astype(BF16),
            (imag * other_real - real * other_imag).astype(BF16),
        ],
        axis=1,
    )
    series = jnp.dot(product, back_ref[...], preferred_element_type=F32)
    cosine, sine = untwist_ref[0], untwist_ref[1]
    partial[:V] = (series[:, :U] * cosine - series[:, U:] * sine).astype(BF16)
    partial[V:] = (series[:, :U] * sine + series[:, U:] * cosine).astype(BF16)
    out_ref[...] = jnp.dot(last_ref[...], partial[...], preferred_element_type=F32).astype(BF16)


def inverse_step(coherent, shifted, back, untwist, last):
    return pl.pallas_call(
        inverse_kernel,
        out_shape=jax.ShapeDtypeStruct((V, U), BF16),
        in_specs=[VM] * 5,
        out_specs=VM,
        scratch_shapes=[pltpu.VMEM((2 * V, U), BF16)],
        compiler_params=pltpu.CompilerParams(vmem_limit_bytes=LIMIT),
        name="inverse_step",
    )(coherent, shifted, back, untwist, last)


def body(strain, row_target, gate_start, gate_width, inverse_psd, templates, template_shift):
    row, twist, col, back, untwist, last = (jnp.asarray(t) for t in tables())
    me = lax.axis_index("seg").astype(jnp.int32).reshape(1)
    rows, ids = sort_rows(me, row_target.reshape(SLOTS // 256, 256), strain)
    placed, full = route_rows(
        rows.reshape(SEGS, CAP, QU),
        ids.reshape(SEGS, 1, 128),
        templates.reshape(BLOCK, QV, U),
    )
    gates = jnp.concatenate([gate_start, gate_width], axis=0)
    turned, shifted = first_section(gates, template_shift, placed, full, row, twist)
    coherent, following, after = spectra(turned, shifted, inverse_psd, col)
    results = [
        inverse_step(coherent, bank, back, untwist, last) for bank in (shifted, following, after)
    ]
    return jnp.stack(results, axis=0).reshape(1, 1, STEPS, V // 2, 2, U)


def solution(mesh):
    in_specs = (
        P("seg", "det"),
        P("seg"),
        P("seg", None),
        P("seg", None),
        P(None, "det", None),
        P("seg", "det", None, None),
        P("seg"),
    )
    out_specs = P("seg", "det", None, None, None, None)
    return jax.shard_map(body, mesh=mesh, in_specs=in_specs, out_specs=out_specs, check_vma=False)
```

```python
import functools
import math

import jax
import jax.numpy as jnp
import numpy as np
from jax import lax
from jax.experimental import pallas as pl
from jax.experimental.pallas import tpu as pltpu
from jax.sharding import PartitionSpec as P

V = 512
U = 1024
DETECTORS = 3
BLOCK = 4
STEPS = 3
SAMPLES = 524288
SEGS = 64
DETS = 4
SLOTS = 3072
CAP = 48
QU = U // DETS
QV = V // DETS
ROWS = DETECTORS * V
HALF = U // 2
MESH = pl.DeviceIdType.MESH
F32 = jnp.float32
BF16 = jnp.bfloat16
LIMIT = 60 * 1024 * 1024
VM = pl.BlockSpec(memory_space=pltpu.VMEM)
SM = pl.BlockSpec(memory_space=pltpu.SMEM)
HB = pl.BlockSpec(memory_space=pl.ANY)


def angles(rows, cols, modulus, direction):
    residue = (rows[:, None].astype(np.int64) * cols[None, :]) % modulus
    angle = np.float32(direction * 2.0 * math.pi / modulus) * residue.astype(np.float32)
    return np.cos(angle), np.sin(angle)


@functools.cache
def tables():
    v, u, m = np.arange(V), np.arange(U), np.arange(HALF)
    bf = np.dtype(jnp.bfloat16)
    c, s = angles(v, v, V, -1.0)
    row = (np.concatenate([c, s], 0) / math.sqrt(V)).astype(bf)
    twist = np.stack([*angles(v, u, SAMPLES, -1.0)])
    twist = twist.reshape(2, V, DETS, QU).transpose(2, 0, 1, 3).astype(np.float32)
    c, s = angles(u, m, U, -1.0)
    col = np.stack([np.concatenate([c, s], 1), np.concatenate([-s, c], 1)])
    col = (col / math.sqrt(U)).reshape(2, DETS, QU, U).transpose(1, 0, 2, 3)
    col = col.reshape(DETS, 2 * QU, U).astype(bf)
    c, s = angles(m, u, U, 1.0)
    back = np.concatenate([np.concatenate([c, s], 1), np.concatenate([-s, c], 1)], 0)
    back = (back / math.sqrt(U)).astype(bf)
    untwist = np.stack([*angles(v, u, SAMPLES, 1.0)]).astype(np.float32)
    c, s = angles(np.arange(V // 4, 3 * V // 4), v, V, 1.0)
    last = np.stack([np.concatenate([c, -s], 1), np.concatenate([s, c], 1)], 1)
    last = (last / math.sqrt(V)).reshape(V, 2 * V).astype(bf)
    return row, twist, col, back, untwist, last


GROUP = 16
LANES = 256
COUNT = SLOTS // LANES


def sort_ranks(me, target_ref, dest, ids):
    lane = lax.broadcasted_iota(jnp.int32, (LANES, LANES), 1)
    sub = lax.broadcasted_iota(jnp.int32, (LANES, LANES), 0)
    upper = jnp.where(sub <= lane, 1.0, 0.0).astype(BF16)
    seg = lax.broadcasted_iota(jnp.int32, (SEGS, LANES), 0)
    carry = jnp.zeros((SEGS, 1), F32)
    high = jnp.zeros((SEGS, SEGS), F32)
    low = jnp.zeros((SEGS, SEGS), F32)
    spread = (((1,), (1,)), ((), ()))
    for b in range(COUNT):
        t = target_ref[b : b + 1, :]
        owner = ((t >> 9) * 43691) >> 17
        local = t - owner * ROWS
        owner = jnp.where(t >= 0, (owner + SEGS - me) & (SEGS - 1), SEGS)
        mine = jnp.where(seg == owner, 1.0, 0.0)
        before = jnp.dot(mine.astype(BF16), upper, preferred_element_type=F32)
        rank = jnp.sum(mine * (before + carry), axis=0, keepdims=True).astype(jnp.int32) - 1
        carry = carry + jnp.sum(mine, axis=1, keepdims=True)
        dest[b : b + 1, :] = jnp.where(t >= 0, owner * CAP + rank, -1)
        order = jnp.where(seg == rank, 1.0, 0.0).astype(BF16)
        upper_part = (mine * ((local >> 6) + 1).astype(F32)).astype(BF16)
        lower_part = (mine * (local & 63).astype(F32)).astype(BF16)
        high = high + lax.dot_general(upper_part, order, spread, preferred_element_type=F32)
        low = low + lax.dot_general(lower_part, order, spread, preferred_element_type=F32)
    found = jnp.where(high > 0.5, high * 64.0 + low - 63.0, 0.0).astype(jnp.int32)
    found = jnp.concatenate([found, found], axis=1)
    side = lax.broadcasted_iota(jnp.int32, (SEGS, 128), 1) // 64
    parity = lax.broadcasted_iota(jnp.int32, (SEGS, 128), 0) & 1
    found = jnp.where(side == parity, found, 0)
    for o in range(SEGS):
        ids[o] = found[o : o + 1]


def shift_bank(det, shift_ref, bank_ref, bank):
    split = lax.broadcasted_iota(jnp.int32, (2 * QV, 2 * QV), 0)
    split = 2 * (split % QV) + split // QV
    split = jnp.where(split == lax.broadcasted_iota(jnp.int32, (2 * QV, 2 * QV), 1), 1.0, 0.0)
    split = split.astype(BF16)
    k = lax.broadcasted_iota(jnp.int32, (QV, 128), 0) + det * QV
    m = lax.broadcasted_iota(jnp.int32, (8, HALF), 1)
    for b in range(BLOCK):
        shift = shift_ref[b]
        angle = (-2.0 * math.pi / SAMPLES) * ((k * shift) % SAMPLES).astype(F32)
        row_cos, row_sin = jnp.cos(angle)[:, :1], jnp.sin(angle)[:, :1]
        angle = (-2.0 * math.pi / U) * ((m * shift) % U).astype(F32)
        col_cos, col_sin = jnp.cos(angle)[:1], jnp.sin(angle)[:1]
        pairs = bank_ref[b].reshape(2 * QV, HALF)
        parts = jnp.dot(split, pairs, preferred_element_type=F32)
        real, imag = parts[:QV], parts[QV:]
        cosine = row_cos * col_cos - row_sin * col_sin
        sine = row_cos * col_sin + row_sin * col_cos
        bank[b, :, :HALF] = (real * cosine - imag * sine).astype(BF16)
        bank[b, :, HALF:] = (real * sine + imag * cosine).astype(BF16)


PIECES = 16
PIECE = V // PIECES


def filter_kernel(
    start_ref, width_ref, shift_ref, target_ref, bank_ref, strain_ref, psd_hbm, row_hbm, twist_hbm, col_hbm,
    coherent_ref, full_ref, next_ref, after_ref,
    held, dest, rows, ids, arrived, arrived_ids, chosen, total, bank, relay,
    turned, crossed, sums, mine, psd, row, twist, col,
    row_send, row_recv, id_send, id_recv, bank_send, bank_recv, turn_send, turn_recv,
    coh_send, coh_recv, pass_send, pass_recv, piece_send, relay_recv, table_sem, own_sem,
):
    me = lax.axis_index("seg")
    det = lax.axis_index("det")
    core = me % 2
    place = (me % 32) // 2
    barrier = pltpu.get_barrier_semaphore()

    def greet(o, _):
        pl.semaphore_signal(
            barrier, inc=1, device_id={"seg": (me + o) % SEGS}, device_id_type=MESH
        )
        return 0

    lax.fori_loop(1, SEGS, greet, 0)
    for o in range(1, DETS):
        pl.semaphore_signal(
            barrier, inc=1, device_id={"det": (det + o) % DETS}, device_id_type=MESH
        )
    fetches = [
        pltpu.make_async_copy(source, held_at, table_sem.at[i])
        for i, (source, held_at) in enumerate(
            ((row_hbm, row), (twist_hbm.at[det], twist), (col_hbm, col), (psd_hbm, psd))
        )
    ]
    for fetch in fetches:
        fetch.start()
    shift_bank(det, shift_ref, bank_ref, bank)
    own_bank = pltpu.make_async_copy(
        bank.at[det], full_ref.at[pl.ds(det * QV, QV)], own_sem.at[0]
    )
    own_bank.start()
    pl.semaphore_wait(barrier, SEGS + DETS - 2)

    def bank_copy(o):
        other = (det + o) % DETS
        return pltpu.make_async_remote_copy(
            src_ref=bank.at[other],
            dst_ref=full_ref.at[pl.ds(det * QV, QV)],
            send_sem=bank_send.at[o],
            recv_sem=bank_recv.at[o],
            device_id={"det": other},
            device_id_type=MESH,
        )

    for o in (2, 1, 3):
        bank_copy(o).start()

    def row_copy(o):
        return pltpu.make_async_remote_copy(
            src_ref=rows.at[pl.ds(o * CAP, CAP)],
            dst_ref=arrived.at[o, pl.ds(0, CAP)],
            send_sem=row_send.at[o],
            recv_sem=row_recv.at[o],
            device_id={"seg": (me + o) % SEGS},
            device_id_type=MESH,
        )

    def id_copy(o):
        return pltpu.make_async_remote_copy(
            src_ref=ids.at[o],
            dst_ref=arrived_ids.at[o],
            send_sem=id_send.at[o],
            recv_sem=id_recv.at[o],
            device_id={"seg": (me + o) % SEGS},
            device_id_type=MESH,
        )

    held[...] = strain_ref[...].astype(BF16)
    sort_ranks(me, target_ref, dest, ids)
    step = GROUP * CAP

    def send(o, _):
        id_copy(o).start()
        row_copy(o).start()
        return 0

    for g in range(SEGS // GROUP):
        want = lax.broadcasted_iota(jnp.int32, (step, LANES), 0) + g * step
        picks = [
            jnp.where(want == dest[b : b + 1, :], 1.0, 0.0).astype(BF16) for b in range(COUNT)
        ]
        picked = jnp.dot(jnp.concatenate(picks, axis=1), held[...], preferred_element_type=F32)
        rows[g * step : (g + 1) * step] = picked.astype(BF16)
        lax.fori_loop(max(1, g * GROUP), (g + 1) * GROUP, send, 0)
    own_rows = pltpu.make_async_copy(
        rows.at[pl.ds(0, CAP)], arrived.at[0, pl.ds(0, CAP)], own_sem.at[1]
    )
    own_rows.start()
    own_ids = pltpu.make_async_copy(ids.at[0], arrived_ids.at[0], own_sem.at[2])
    own_ids.start()
    arrived[:, CAP:, :] = jnp.zeros((SEGS, 64 - CAP, QU), BF16)

    own_bank.wait()
    for o in range(1, DETS):
        bank_copy(o).wait_recv()

    def whole_pass(source, target, lane, back):
        return pltpu.make_async_remote_copy(
            src_ref=source,
            dst_ref=target,
            send_sem=pass_send.at[lane],
            recv_sem=pass_recv.at[lane],
            device_id={"seg": (me + SEGS - back) % SEGS},
            device_id_type=MESH,
        )

    hot = (me % 32) < 2
    odd = core == 1
    to_next = whole_pass(full_ref, next_ref, 0, 1)
    to_after = whole_pass(full_ref, after_ref, 1, 2)
    onward = pltpu.make_async_remote_copy(
        src_ref=next_ref,
        dst_ref=after_ref,
        send_sem=pass_send.at[2],
        recv_sem=pass_recv.at[1],
        device_id={"seg": (me + SEGS - 1) % SEGS},
        device_id_type=MESH,
    )
    corner = (me // 32) * 32
    far = (corner + SEGS - 1) % SEGS

    def piece_copy(i):
        return pltpu.make_async_remote_copy(
            src_ref=full_ref.at[pl.ds(i * PIECE, PIECE)],
            dst_ref=relay,
            send_sem=piece_send.at[i],
            recv_sem=relay_recv.at[0],
            device_id={"seg": corner + 2 * i + core},
            device_id_type=MESH,
        )

    def last_hop(source, target, lane, at):
        return pltpu.make_async_remote_copy(
            src_ref=source,
            dst_ref=target.at[pl.ds(at * PIECE, PIECE)],
            send_sem=piece_send.at[0],
            recv_sem=pass_recv.at[lane],
            device_id={"seg": far},
            device_id_type=MESH,
        )

    def pieces(i, _):
        piece_copy(i).start()
        return 0

    def pieces_sent(i, _):
        piece_copy(i).wait_send()
        return 0

    @pl.when(jnp.logical_or(odd, jnp.logical_not(hot)))
    def _():
        to_next.start()

    @pl.when(jnp.logical_and(odd, jnp.logical_not(hot)))
    def _():
        to_after.start()

    @pl.when(hot)
    def _():
        lax.fori_loop(1, PIECES, pieces, 0)

    @pl.when(jnp.logical_and(hot, odd))
    def _():
        last_hop(full_ref.at[pl.ds(0, PIECE)], after_ref, 1, 0).start()

    @pl.when(jnp.logical_and(hot, jnp.logical_not(odd)))
    def _():
        last_hop(full_ref.at[pl.ds(0, PIECE)], next_ref, 0, 0).start()

    own_rows.wait()
    own_ids.wait()

    def receive(o, _):
        id_copy(o).wait_recv()
        row_copy(o).wait_recv()
        return 0

    wide = GROUP * 64
    groups = SEGS // GROUP
    for g in range(groups):
        if g == 1:

            @pl.when(jnp.logical_not(hot))
            def _():
                piece_copy(1).wait_recv()

            @pl.when(jnp.logical_and(jnp.logical_not(hot), odd))
            def _():
                last_hop(relay, after_ref, 1, place).start()

            @pl.when(jnp.logical_and(jnp.logical_not(hot), jnp.logical_not(odd)))
            def _():
                last_hop(relay, next_ref, 0, place).start()

        if g == 3:
            to_next.wait_recv()

            @pl.when(odd)
            def _():
                onward.start()

        lax.fori_loop(max(1, g * GROUP), (g + 1) * GROUP, receive, 0)
        for p in range(GROUP // 2):
            o = g * GROUP + 2 * p
            ident = arrived_ids[o] + arrived_ids[o + 1] - 1
            chosen[:, p * 128 : (p + 1) * 128] = jnp.where(
                lax.broadcasted_iota(jnp.int32, (ROWS, 128), 0) == ident, 1.0, 0.0
            ).astype(BF16)
        block = arrived[g * GROUP : (g + 1) * GROUP].reshape(wide, QU)
        part = jnp.dot(chosen[...], block, preferred_element_type=F32)
        if g == 0:
            total[...] = part
        else:
            total[...] += part

    def turn_copy(o, d):
        other = (det + o) % DETS
        return pltpu.make_async_remote_copy(
            src_ref=turned.at[other, d],
            dst_ref=crossed.at[o, d],
            send_sem=turn_send.at[o, d],
            recv_sem=turn_recv.at[o, d],
            device_id={"det": other},
            device_id_type=MESH,
        )

    sample = lax.broadcasted_iota(jnp.int32, (V, QU), 0) * U
    sample = sample + lax.broadcasted_iota(jnp.int32, (V, QU), 1) + det * QU
    for fetch in fetches:
        fetch.wait()
    for d in range(DETECTORS):
        begin = start_ref[0, d]
        end = begin + width_ref[0, d]
        inside = (sample >= begin) & (sample < end)
        gated = jnp.where(inside, 0.0, total[d * V : (d + 1) * V]).astype(BF16)
        folded = jnp.dot(row[...], gated, preferred_element_type=F32)
        real, imag = folded[:V], folded[V:]
        cosine, sine = twist[0], twist[1]
        first = (real * cosine - imag * sine).astype(BF16)
        second = (real * sine + imag * cosine).astype(BF16)
        for q in range(DETS):
            turned[q, d, :, :QU] = first[q * QV : (q + 1) * QV]
            turned[q, d, :, QU:] = second[q * QV : (q + 1) * QV]
        for o in (2, 1, 3):
            turn_copy(o, d).start()
    for d in range(DETECTORS):
        part = jnp.dot(turned[det, d], col[det], preferred_element_type=F32)
        for o in (1, 3, 2):
            turn_copy(o, d).wait_recv()
            part = part + jnp.dot(
                crossed[o, d], col[(det + DETS - o) % DETS], preferred_element_type=F32
            )
        for half in range(2):
            cols = slice(half * HALF, (half + 1) * HALF)
            value = psd[d] * part[:, cols]
            if d == 0:
                sums[:, cols] = value
            elif d < DETECTORS - 1:
                sums[:, cols] += value
            else:
                mine[:, cols] = (sums[:, cols] + value).astype(BF16)

    def coherent_copy(o):
        return pltpu.make_async_remote_copy(
            src_ref=mine,
            dst_ref=coherent_ref.at[pl.ds(det * QV, QV)],
            send_sem=coh_send.at[o],
            recv_sem=coh_recv.at[o],
            device_id={"det": (det + o) % DETS},
            device_id_type=MESH,
        )

    for o in (2, 1, 3):
        coherent_copy(o).start()
    keep = pltpu.make_async_copy(mine, coherent_ref.at[pl.ds(det * QV, QV)], own_sem.at[3])
    keep.start()

    to_after.wait_recv()

    @pl.when(jnp.logical_or(odd, jnp.logical_not(hot)))
    def _():
        to_next.wait_send()

    @pl.when(jnp.logical_and(odd, jnp.logical_not(hot)))
    def _():
        to_after.wait_send()

    @pl.when(hot)
    def _():
        lax.fori_loop(1, PIECES, pieces_sent, 0)

    last_hop(relay, next_ref, 0, place).wait_send()

    @pl.when(odd)
    def _():
        onward.wait_send()

    def sent(o, _):
        id_copy(o).wait_send()
        row_copy(o).wait_send()
        return 0

    lax.fori_loop(1, SEGS, sent, 0)
    for o in range(1, DETS):
        bank_copy(o).wait_send()
        for d in range(DETECTORS):
            turn_copy(o, d).wait_send()
    for o in (1, 3, 2):
        coherent_copy(o).wait()
    keep.wait()


def filtered(start, width, shift, target, bank, strain, psd, row, twist, col):
    whole = jax.ShapeDtypeStruct((V, U), BF16)
    dma = pltpu.SemaphoreType.DMA
    return pl.pallas_call(
        filter_kernel,
        out_shape=(whole,) * 4,
        in_specs=[SM, SM, SM, VM, VM, VM, HB, HB, HB, HB],
        out_specs=(HB,) * 4,
        scratch_shapes=[
            pltpu.VMEM((SLOTS, QU), BF16),
            pltpu.VMEM((16, LANES), jnp.int32),
            pltpu.VMEM((SLOTS, QU), BF16),
            pltpu.VMEM((SEGS, 1, 128), jnp.int32),
            pltpu.VMEM((SEGS, 64, QU), BF16),
            pltpu.VMEM((SEGS, 1, 128), jnp.int32),
            pltpu.VMEM((ROWS, GROUP * 64), BF16),
            pltpu.VMEM((ROWS, QU), F32),
            pltpu.VMEM((BLOCK, QV, U), BF16),
            pltpu.VMEM((PIECE, U), BF16),
            pltpu.VMEM((DETS, DETECTORS, QV, 2 * QU), BF16),
            pltpu.VMEM((DETS, DETECTORS, QV, 2 * QU), BF16),
            pltpu.VMEM((QV, U), F32),
            pltpu.VMEM((QV, U), BF16),
            pltpu.VMEM((DETECTORS, QV, HALF), F32),
            pltpu.VMEM((2 * V, V), BF16),
            pltpu.VMEM((2, V, QU), F32),
            pltpu.VMEM((DETS, 2 * QU, U), BF16),
            dma((SEGS,)), dma((SEGS,)), dma((SEGS,)), dma((SEGS,)),
            dma((DETS,)), dma((DETS,)),
            dma((DETS, DETECTORS)), dma((DETS, DETECTORS)),
            dma((DETS,)), dma((DETS,)),
            dma((3,)), dma((2,)), dma((PIECES,)), dma((1,)), dma((4,)), dma((4,)),
        ],
        compiler_params=pltpu.CompilerParams(
            vmem_limit_bytes=LIMIT, collective_id=0, has_side_effects=True
        ),
        cost_estimate=pl.CostEstimate(
            flops=12_000_000_000, bytes_accessed=16_000_000, transcendentals=0
        ),
        name="filtered",
    )(start, width, shift, target, bank, strain, psd, row, twist, col)


def inverse_kernel(
    coherent_ref, first_ref, second_ref, third_ref, back_ref, untwist_ref, last_ref, out_ref, partial
):
    real, imag = coherent_ref[:, :HALF].astype(F32), coherent_ref[:, HALF:].astype(F32)
    for r, bank_ref in enumerate((first_ref, second_ref, third_ref)):
        other_real = bank_ref[:, :HALF].astype(F32)
        other_imag = bank_ref[:, HALF:].astype(F32)
        product = jnp.concatenate(
            [
                (real * other_real + imag * other_imag).astype(BF16),
                (imag * other_real - real * other_imag).astype(BF16),
            ],
            axis=1,
        )
        series = jnp.dot(product, back_ref[...], preferred_element_type=F32)
        cosine, sine = untwist_ref[0], untwist_ref[1]
        partial[:V] = (series[:, :U] * cosine - series[:, U:] * sine).astype(BF16)
        partial[V:] = (series[:, :U] * sine + series[:, U:] * cosine).astype(BF16)
        out = jnp.dot(last_ref[...], partial[...], preferred_element_type=F32).astype(BF16)
        out_ref[0, 0, r] = out.reshape(V // 2, 2, U)


def inverse_steps(coherent, banks, back, untwist, last):
    return pl.pallas_call(
        inverse_kernel,
        out_shape=jax.ShapeDtypeStruct((1, 1, STEPS, V // 2, 2, U), BF16),
        in_specs=[VM] * 7,
        out_specs=VM,
        scratch_shapes=[pltpu.VMEM((2 * V, U), BF16)],
        compiler_params=pltpu.CompilerParams(vmem_limit_bytes=LIMIT),
        name="inverse_steps",
    )(coherent, *banks, back, untwist, last)


def body(strain, row_target, gate_start, gate_width, inverse_psd, templates, template_shift):
    row, twist, col, back, untwist, last = (jnp.asarray(t) for t in tables())
    coherent, *banks = filtered(
        gate_start,
        gate_width,
        template_shift,
        row_target.reshape(COUNT, LANES),
        templates,
        strain,
        inverse_psd,
        row,
        twist,
        col,
    )
    return inverse_steps(coherent, banks, back, untwist, last)


def solution(mesh):
    in_specs = (
        P("seg", "det"),
        P("seg"),
        P("seg", None),
        P("seg", None),
        P(None, "det", None),
        P("seg", "det", None, None),
        P("seg"),
    )
    out_specs = P("seg", "det", None, None, None, None)
    return jax.shard_map(body, mesh=mesh, in_specs=in_specs, out_specs=out_specs, check_vma=False)
```

```python
import functools
import math

import jax
import jax.numpy as jnp
import numpy as np
from jax import lax
from jax.experimental import pallas as pl
from jax.experimental.pallas import tpu as pltpu
from jax.sharding import PartitionSpec as P

V = 512
U = 1024
DETECTORS = 3
BLOCK = 4
STEPS = 3
SAMPLES = 524288
SEGS = 64
DETS = 4
SLOTS = 3072
CAP = 48
QU = U // DETS
QV = V // DETS
ROWS = DETECTORS * V
HALF = U // 2
SHARE = V // 8
PLACES = (0, 2, 3, 1)
MIRROR = 32
MESH = pl.DeviceIdType.MESH
F32 = jnp.float32
BF16 = jnp.bfloat16
LIMIT = 60 * 1024 * 1024
VM = pl.BlockSpec(memory_space=pltpu.VMEM)
SM = pl.BlockSpec(memory_space=pltpu.SMEM)
HB = pl.BlockSpec(memory_space=pl.ANY)


def angles(rows, cols, modulus, direction):
    residue = (rows[:, None].astype(np.int64) * cols[None, :]) % modulus
    angle = np.float32(direction * 2.0 * math.pi / modulus) * residue.astype(np.float32)
    return np.cos(angle), np.sin(angle)


@functools.cache
def tables():
    v, u, m = np.arange(V), np.arange(U), np.arange(HALF)
    bf = np.dtype(jnp.bfloat16)
    c, s = angles(v[: V // 2], v, V, -1.0)
    s[0] = np.where(v % 2 == 0, 1.0, -1.0)
    row = (np.concatenate([c, s], 0) / math.sqrt(V)).astype(bf)
    twist = np.stack([*angles(v[: V // 2], u, SAMPLES, -1.0)])
    twist = twist.reshape(2, V // 2, DETS, QU).transpose(2, 0, 1, 3).astype(np.float32)
    edge = np.stack([*angles(v[V // 2 : V // 2 + 1], u, SAMPLES, -1.0)])
    edge = edge.reshape(2, 1, DETS, QU).transpose(2, 1, 0, 3).reshape(DETS, 1, 2 * QU)
    edge = np.tile(edge, (1, 8, 1)).astype(np.float32)

    def by_source(real_rows, imag_rows):
        both = np.stack([real_rows, imag_rows]) / math.sqrt(U)
        both = both.reshape(2, DETS, QU, U).transpose(1, 0, 2, 3)
        return both.reshape(DETS, 2 * QU, U).astype(bf)

    c, s = angles(u, m, U, -1.0)
    direct = by_source(np.concatenate([c, s], 1), np.concatenate([-s, c], 1))
    c, s = angles(u, m + 1, U, -1.0)
    mirrored = by_source(np.concatenate([c, s], 1), np.concatenate([s, -c], 1))
    col = np.stack([direct, mirrored])
    place = np.zeros(V, np.int64)
    for k in range(V):
        low = k if k < V // 2 else (V - k) % (V // 2)
        device = PLACES.index(low // SHARE)
        if k < V // 2:
            place[k] = device * QV + low % SHARE
        else:
            place[k] = device * QV + QV - 1 - low % SHARE
    perm = (place[:, None] == v[None, :]).astype(bf)
    c, s = angles(m, u, U, 1.0)
    back = np.concatenate([np.concatenate([c, s], 1), np.concatenate([-s, c], 1)], 0)
    back = (back / math.sqrt(U)).astype(bf)
    untwist = np.stack([*angles(v, u, SAMPLES, 1.0)]).astype(np.float32)
    c, s = angles(np.arange(V // 4, 3 * V // 4), v, V, 1.0)
    last = np.stack([np.concatenate([c, -s], 1), np.concatenate([s, c], 1)], 1)
    last = (last / math.sqrt(V)).reshape(V, 2 * V).astype(bf)
    return row, twist, edge, col, perm, back, untwist, last


GROUP = 16
LANES = 256
COUNT = SLOTS // LANES


def sort_ranks(me, target_ref, dest, ids):
    lane = lax.broadcasted_iota(jnp.int32, (LANES, LANES), 1)
    sub = lax.broadcasted_iota(jnp.int32, (LANES, LANES), 0)
    upper = jnp.where(sub <= lane, 1.0, 0.0).astype(BF16)
    seg = lax.broadcasted_iota(jnp.int32, (SEGS, LANES), 0)
    carry = jnp.zeros((SEGS, 1), F32)
    high = jnp.zeros((SEGS, SEGS), F32)
    low = jnp.zeros((SEGS, SEGS), F32)
    spread = (((1,), (1,)), ((), ()))
    for b in range(COUNT):
        t = target_ref[b * LANES : (b + 1) * LANES].reshape(1, LANES)
        owner = ((t >> 9) * 43691) >> 17
        local = t - owner * ROWS
        owner = jnp.where(t >= 0, (owner + SEGS - me) & (SEGS - 1), SEGS)
        mine = jnp.where(seg == owner, 1.0, 0.0)
        before = jnp.dot(mine.astype(BF16), upper, preferred_element_type=F32)
        rank = jnp.sum(mine * (before + carry), axis=0, keepdims=True).astype(jnp.int32) - 1
        carry = carry + jnp.sum(mine, axis=1, keepdims=True)
        dest[b : b + 1, :] = jnp.where(t >= 0, owner * CAP + rank, -1)
        order = jnp.where(seg == rank, 1.0, 0.0).astype(BF16)
        upper_part = (mine * ((local >> 6) + 1).astype(F32)).astype(BF16)
        lower_part = (mine * (local & 63).astype(F32)).astype(BF16)
        high = high + lax.dot_general(upper_part, order, spread, preferred_element_type=F32)
        low = low + lax.dot_general(lower_part, order, spread, preferred_element_type=F32)
    found = jnp.where(high > 0.5, high * 64.0 + low - 63.0, 0.0).astype(jnp.int32)
    found = jnp.concatenate([found, found], axis=1)
    side = lax.broadcasted_iota(jnp.int32, (SEGS, 128), 1) // 64
    parity = lax.broadcasted_iota(jnp.int32, (SEGS, 128), 0) & 1
    found = jnp.where(side == parity, found, 0)
    for o in range(SEGS):
        ids[o] = found[o : o + 1]


def shift_bank(det, shift_ref, bank_ref, bank):
    split = lax.broadcasted_iota(jnp.int32, (2 * QV, 2 * QV), 0)
    split = 2 * (split % QV) + split // QV
    split = jnp.where(split == lax.broadcasted_iota(jnp.int32, (2 * QV, 2 * QV), 1), 1.0, 0.0)
    split = split.astype(BF16)
    k = lax.broadcasted_iota(jnp.int32, (QV, 128), 0) + det * QV
    m = lax.broadcasted_iota(jnp.int32, (8, HALF), 1)
    for b in range(BLOCK):
        shift = shift_ref[b]
        angle = (-2.0 * math.pi / SAMPLES) * ((k * shift) % SAMPLES).astype(F32)
        row_cos, row_sin = jnp.cos(angle)[:, :1], jnp.sin(angle)[:, :1]
        angle = (-2.0 * math.pi / U) * ((m * shift) % U).astype(F32)
        col_cos, col_sin = jnp.cos(angle)[:1], jnp.sin(angle)[:1]
        pairs = bank_ref[b].reshape(2 * QV, HALF)
        parts = jnp.dot(split, pairs, preferred_element_type=F32)
        real, imag = parts[:QV], parts[QV:]
        cosine = row_cos * col_cos - row_sin * col_sin
        sine = row_cos * col_sin + row_sin * col_cos
        bank[b, :, :HALF] = (real * cosine - imag * sine).astype(BF16)
        bank[b, :, HALF:] = (real * sine + imag * cosine).astype(BF16)


PIECES = 16
PIECE = V // PIECES


def filter_kernel(
    start_ref, width_ref, shift_ref, target_ref, edge_ref, bank_ref, strain_ref, psd_hbm, row_hbm, twist_hbm, col_hbm,
    coherent_ref, full_ref, next_ref, after_ref,
    held, dest, rows, ids, arrived, arrived_ids, chosen, total, bank, relay,
    turned, crossed, spec, mine, psd_low, psd_high, row, twist, col,
    row_send, row_recv, id_send, id_recv, bank_send, bank_recv, turn_send, turn_recv,
    coh_send, coh_recv, pass_send, pass_recv, piece_send, relay_recv, psd_send, psd_recv, table_sem, own_sem,
):
    me = lax.axis_index("seg")
    det = lax.axis_index("det")
    core = me % 2
    place = (me % 32) // 2
    barrier = pltpu.get_barrier_semaphore()

    def greet(o, _):
        pl.semaphore_signal(
            barrier, inc=1, device_id={"seg": (me + o) % SEGS}, device_id_type=MESH
        )
        return 0

    lax.fori_loop(1, SEGS, greet, 0)
    for o in range(1, DETS):
        pl.semaphore_signal(
            barrier, inc=1, device_id={"det": (det + o) % DETS}, device_id_type=MESH
        )
    across = {"seg": (me + MIRROR) % SEGS, "det": DETS - 1 - det}
    pl.semaphore_signal(barrier, inc=1, device_id=across, device_id_type=MESH)
    fetches = [
        pltpu.make_async_copy(source, held_at, table_sem.at[i])
        for i, (source, held_at) in enumerate(
            ((row_hbm, row), (twist_hbm.at[det], twist), (col_hbm, col))
        )
    ]
    for fetch in fetches:
        fetch.start()
    shift_bank(det, shift_ref, bank_ref, bank)
    own_bank = pltpu.make_async_copy(
        bank.at[det], full_ref.at[pl.ds(det * QV, QV)], own_sem.at[0]
    )
    own_bank.start()
    pl.semaphore_wait(barrier, SEGS + DETS - 1)

    def bank_copy(o):
        other = (det + o) % DETS
        return pltpu.make_async_remote_copy(
            src_ref=bank.at[other],
            dst_ref=full_ref.at[pl.ds(det * QV, QV)],
            send_sem=bank_send.at[o],
            recv_sem=bank_recv.at[o],
            device_id={"det": other},
            device_id_type=MESH,
        )

    for o in (2, 1, 3):
        bank_copy(o).start()

    upper_det = det >= DETS // 2

    def psd_copy(target, lane):
        return pltpu.make_async_remote_copy(
            src_ref=psd_hbm.at[:, pl.ds(SHARE, SHARE)],
            dst_ref=target,
            send_sem=psd_send.at[0],
            recv_sem=psd_recv.at[lane],
            device_id=across,
            device_id_type=MESH,
        )

    to_low = psd_copy(psd_low, 0)
    to_high = psd_copy(psd_high.at[:, pl.ds(0, SHARE)], 0)
    to_rest = pltpu.make_async_remote_copy(
        src_ref=psd_hbm.at[:, pl.ds(0, 8)],
        dst_ref=psd_high.at[:, pl.ds(SHARE, 8)],
        send_sem=psd_send.at[1],
        recv_sem=psd_recv.at[1],
        device_id={"det": (det + 2) % DETS},
        device_id_type=MESH,
    )
    keep_low = pltpu.make_async_copy(psd_hbm.at[:, pl.ds(0, SHARE)], psd_low, own_sem.at[4])
    keep_high = pltpu.make_async_copy(psd_hbm.at[:, pl.ds(0, SHARE + 8)], psd_high, own_sem.at[4])

    @pl.when(upper_det)
    def _():
        to_high.start()
        to_rest.start()
        keep_high.start()

    @pl.when(jnp.logical_not(upper_det))
    def _():
        to_low.start()
        keep_low.start()

    def row_copy(o):
        return pltpu.make_async_remote_copy(
            src_ref=rows.at[pl.ds(o * CAP, CAP)],
            dst_ref=arrived.at[o, pl.ds(0, CAP)],
            send_sem=row_send.at[o],
            recv_sem=row_recv.at[o],
            device_id={"seg": (me + o) % SEGS},
            device_id_type=MESH,
        )

    def id_copy(o):
        return pltpu.make_async_remote_copy(
            src_ref=ids.at[o],
            dst_ref=arrived_ids.at[o],
            send_sem=id_send.at[o],
            recv_sem=id_recv.at[o],
            device_id={"seg": (me + o) % SEGS},
            device_id_type=MESH,
        )

    held[...] = strain_ref[...].astype(BF16)
    sort_ranks(me, target_ref, dest, ids)
    step = GROUP * CAP

    def send(o, _):
        id_copy(o).start()
        row_copy(o).start()
        return 0

    for g in range(SEGS // GROUP):
        want = lax.broadcasted_iota(jnp.int32, (step, LANES), 0) + g * step
        picks = [
            jnp.where(want == dest[b : b + 1, :], 1.0, 0.0).astype(BF16) for b in range(COUNT)
        ]
        picked = jnp.dot(jnp.concatenate(picks, axis=1), held[...], preferred_element_type=F32)
        rows[g * step : (g + 1) * step] = picked.astype(BF16)
        lax.fori_loop(max(1, g * GROUP), (g + 1) * GROUP, send, 0)
    own_rows = pltpu.make_async_copy(
        rows.at[pl.ds(0, CAP)], arrived.at[0, pl.ds(0, CAP)], own_sem.at[1]
    )
    own_rows.start()
    own_ids = pltpu.make_async_copy(ids.at[0], arrived_ids.at[0], own_sem.at[2])
    own_ids.start()
    arrived[:, CAP:, :] = jnp.zeros((SEGS, 64 - CAP, QU), BF16)

    own_bank.wait()
    for o in range(1, DETS):
        bank_copy(o).wait_recv()

    def whole_pass(source, target, lane, back):
        return pltpu.make_async_remote_copy(
            src_ref=source,
            dst_ref=target,
            send_sem=pass_send.at[lane],
            recv_sem=pass_recv.at[lane],
            device_id={"seg": (me + SEGS - back) % SEGS},
            device_id_type=MESH,
        )

    hot = (me % 32) < 2
    odd = core == 1
    to_next = whole_pass(full_ref, next_ref, 0, 1)
    to_after = whole_pass(full_ref, after_ref, 1, 2)
    onward = pltpu.make_async_remote_copy(
        src_ref=next_ref,
        dst_ref=after_ref,
        send_sem=pass_send.at[2],
        recv_sem=pass_recv.at[1],
        device_id={"seg": (me + SEGS - 1) % SEGS},
        device_id_type=MESH,
    )
    corner = (me // 32) * 32
    far = (corner + SEGS - 1) % SEGS

    def piece_copy(i):
        return pltpu.make_async_remote_copy(
            src_ref=full_ref.at[pl.ds(i * PIECE, PIECE)],
            dst_ref=relay,
            send_sem=piece_send.at[i],
            recv_sem=relay_recv.at[0],
            device_id={"seg": corner + 2 * i + core},
            device_id_type=MESH,
        )

    def last_hop(source, target, lane, at):
        return pltpu.make_async_remote_copy(
            src_ref=source,
            dst_ref=target.at[pl.ds(at * PIECE, PIECE)],
            send_sem=piece_send.at[0],
            recv_sem=pass_recv.at[lane],
            device_id={"seg": far},
            device_id_type=MESH,
        )

    def pieces(i, _):
        piece_copy(i).start()
        return 0

    def pieces_sent(i, _):
        piece_copy(i).wait_send()
        return 0

    @pl.when(jnp.logical_or(odd, jnp.logical_not(hot)))
    def _():
        to_next.start()

    @pl.when(jnp.logical_and(odd, jnp.logical_not(hot)))
    def _():
        to_after.start()

    @pl.when(hot)
    def _():
        lax.fori_loop(1, PIECES, pieces, 0)

    @pl.when(jnp.logical_and(hot, odd))
    def _():
        last_hop(full_ref.at[pl.ds(0, PIECE)], after_ref, 1, 0).start()

    @pl.when(jnp.logical_and(hot, jnp.logical_not(odd)))
    def _():
        last_hop(full_ref.at[pl.ds(0, PIECE)], next_ref, 0, 0).start()

    own_rows.wait()
    own_ids.wait()

    def receive(o, _):
        id_copy(o).wait_recv()
        row_copy(o).wait_recv()
        return 0

    wide = GROUP * 64
    groups = SEGS // GROUP
    for g in range(groups):
        lax.fori_loop(max(1, g * GROUP), (g + 1) * GROUP, receive, 0)
        for p in range(GROUP // 2):
            o = g * GROUP + 2 * p
            ident = arrived_ids[o] + arrived_ids[o + 1] - 1
            chosen[:, p * 128 : (p + 1) * 128] = jnp.where(
                lax.broadcasted_iota(jnp.int32, (ROWS, 128), 0) == ident, 1.0, 0.0
            ).astype(BF16)
        block = arrived[g * GROUP : (g + 1) * GROUP].reshape(wide, QU)
        part = jnp.dot(chosen[...], block, preferred_element_type=F32)
        if g == 0:
            total[...] = part
        else:
            total[...] += part

    def turn_copy(o, d):
        other = (det + o) % DETS
        return pltpu.make_async_remote_copy(
            src_ref=turned.at[other, d],
            dst_ref=crossed.at[o, d],
            send_sem=turn_send.at[o, d],
            recv_sem=turn_recv.at[o, d],
            device_id={"det": other},
            device_id_type=MESH,
        )

    sample = lax.broadcasted_iota(jnp.int32, (V, QU), 0) * U
    sample = sample + lax.broadcasted_iota(jnp.int32, (V, QU), 1) + det * QU
    for fetch in fetches:
        fetch.wait()
    for d in range(DETECTORS):
        begin = start_ref[0, d]
        end = begin + width_ref[0, d]
        inside = (sample >= begin) & (sample < end)
        gated = jnp.where(inside, 0.0, total[d * V : (d + 1) * V]).astype(BF16)
        folded = jnp.dot(row[...], gated, preferred_element_type=F32)
        real, imag = folded[: V // 2], folded[V // 2 :]
        cosine, sine = twist[0], twist[1]
        first = (real * cosine - imag * sine).astype(BF16)
        second = (real * sine + imag * cosine).astype(BF16)
        for q in range(DETS):
            at = PLACES[q] * SHARE
            turned[q, d, :, :QU] = first[at : at + SHARE]
            turned[q, d, :, QU:] = second[at : at + SHARE]
        for o in (2, 1, 3):
            turn_copy(o, d).start()

    @pl.when(jnp.logical_not(hot))
    def _():
        piece_copy(1).wait_recv()

    @pl.when(jnp.logical_and(jnp.logical_not(hot), odd))
    def _():
        last_hop(relay, after_ref, 1, place).start()

    @pl.when(jnp.logical_and(jnp.logical_not(hot), jnp.logical_not(odd)))
    def _():
        last_hop(relay, next_ref, 0, place).start()

    high = DETECTORS * SHARE
    row_at = lax.broadcasted_iota(jnp.int32, (high, high), 0)
    col_at = lax.broadcasted_iota(jnp.int32, (high, high), 1)
    flip = (row_at // SHARE == col_at // SHARE) & (row_at % SHARE + col_at % SHARE == SHARE - 1)
    flip = jnp.where(flip, 1.0, 0.0).astype(BF16)
    packed = lax.broadcasted_iota(jnp.int32, (high, 2 * QU), 0) % SHARE + det == 0
    imag_side = lax.broadcasted_iota(jnp.int32, (high, 2 * QU), 1) >= QU
    for o in (0, 1, 3, 2):
        source = (det + DETS - o) % DETS
        if o == 0:
            came = turned[det]
        else:
            for d in range(DETECTORS):
                turn_copy(o, d).wait_recv()
            came = crossed[o]
        came = came.reshape(high, 2 * QU)
        wide_came = came.astype(F32)
        direct = jnp.where(packed & imag_side, 0.0, wide_came).astype(BF16)
        twin = wide_came[:, QU:]
        twin = jnp.concatenate([twin, twin], axis=1) * edge_ref[source][:1]
        mirrored = jnp.where(packed, twin, wide_came).astype(BF16)
        mirrored = jnp.dot(flip, mirrored, preferred_element_type=F32).astype(BF16)
        part = jnp.dot(direct, col[0, source], preferred_element_type=F32)
        other = jnp.dot(mirrored, col[1, source], preferred_element_type=F32)
        if o == 0:
            spec[0], spec[1] = part, other
        else:
            spec[0] += part
            spec[1] += other

    @pl.when(upper_det)
    def _():
        to_low.wait_recv()
        keep_high.wait()

    @pl.when(jnp.logical_not(upper_det))
    def _():
        to_high.wait_recv()
        to_rest.wait_recv()
        keep_low.wait()

    for half in range(2):
        cols = slice(half * HALF, (half + 1) * HALF)
        direct, mirrored = 0.0, 0.0
        for d in range(DETECTORS):
            rows_of = slice(d * SHARE, (d + 1) * SHARE)
            direct = direct + psd_low[d] * spec[0, rows_of, cols]
            mirrored = mirrored + psd_high[d, 1 : SHARE + 1] * spec[1, rows_of, cols]
        mine[:SHARE, cols] = direct.astype(BF16)
        mine[SHARE:, cols] = mirrored.astype(BF16)

    def coherent_copy(o):
        return pltpu.make_async_remote_copy(
            src_ref=mine,
            dst_ref=coherent_ref.at[pl.ds(det * QV, QV)],
            send_sem=coh_send.at[o],
            recv_sem=coh_recv.at[o],
            device_id={"det": (det + o) % DETS},
            device_id_type=MESH,
        )

    for o in (2, 1, 3):
        coherent_copy(o).start()
    keep = pltpu.make_async_copy(mine, coherent_ref.at[pl.ds(det * QV, QV)], own_sem.at[3])
    keep.start()

    to_next.wait_recv()

    @pl.when(odd)
    def _():
        onward.start()

    to_after.wait_recv()

    @pl.when(upper_det)
    def _():
        to_high.wait_send()
        to_rest.wait_send()

    @pl.when(jnp.logical_not(upper_det))
    def _():
        to_low.wait_send()


    @pl.when(jnp.logical_or(odd, jnp.logical_not(hot)))
    def _():
        to_next.wait_send()

    @pl.when(jnp.logical_and(odd, jnp.logical_not(hot)))
    def _():
        to_after.wait_send()

    @pl.when(hot)
    def _():
        lax.fori_loop(1, PIECES, pieces_sent, 0)

    last_hop(relay, next_ref, 0, place).wait_send()

    @pl.when(odd)
    def _():
        onward.wait_send()

    def sent(o, _):
        id_copy(o).wait_send()
        row_copy(o).wait_send()
        return 0

    lax.fori_loop(1, SEGS, sent, 0)
    for o in range(1, DETS):
        bank_copy(o).wait_send()
        for d in range(DETECTORS):
            turn_copy(o, d).wait_send()
    for o in (1, 3, 2):
        coherent_copy(o).wait()
    keep.wait()


def filtered(start, width, shift, target, edge, bank, strain, psd, row, twist, col):
    whole = jax.ShapeDtypeStruct((V, U), BF16)
    dma = pltpu.SemaphoreType.DMA
    return pl.pallas_call(
        filter_kernel,
        out_shape=(whole,) * 4,
        in_specs=[SM, SM, SM, VM, VM, VM, VM, HB, HB, HB, HB],
        out_specs=(HB,) * 4,
        scratch_shapes=[
            pltpu.VMEM((SLOTS, QU), BF16),
            pltpu.VMEM((16, LANES), jnp.int32),
            pltpu.VMEM((SLOTS, QU), BF16),
            pltpu.VMEM((SEGS, 1, 128), jnp.int32),
            pltpu.VMEM((SEGS, 64, QU), BF16),
            pltpu.VMEM((SEGS, 1, 128), jnp.int32),
            pltpu.VMEM((ROWS, GROUP * 64), BF16),
            pltpu.VMEM((ROWS, QU), F32),
            pltpu.VMEM((BLOCK, QV, U), BF16),
            pltpu.VMEM((PIECE, U), BF16),
            pltpu.VMEM((DETS, DETECTORS, SHARE, 2 * QU), BF16),
            pltpu.VMEM((DETS, DETECTORS, SHARE, 2 * QU), BF16),
            pltpu.VMEM((2, DETECTORS * SHARE, U), F32),
            pltpu.VMEM((QV, U), BF16),
            pltpu.VMEM((DETECTORS, SHARE, HALF), F32),
            pltpu.VMEM((DETECTORS, SHARE + 8, HALF), F32),
            pltpu.VMEM((V, V), BF16),
            pltpu.VMEM((2, V // 2, QU), F32),
            pltpu.VMEM((2, DETS, 2 * QU, U), BF16),
            dma((SEGS,)), dma((SEGS,)), dma((SEGS,)), dma((SEGS,)),
            dma((DETS,)), dma((DETS,)),
            dma((DETS, DETECTORS)), dma((DETS, DETECTORS)),
            dma((DETS,)), dma((DETS,)),
            dma((3,)), dma((2,)), dma((PIECES,)), dma((1,)), dma((2,)), dma((2,)), dma((3,)), dma((5,)),
        ],
        compiler_params=pltpu.CompilerParams(
            vmem_limit_bytes=LIMIT, collective_id=0, has_side_effects=True
        ),
        cost_estimate=pl.CostEstimate(
            flops=12_000_000_000, bytes_accessed=16_000_000, transcendentals=0
        ),
        name="filtered",
    )(start, width, shift, target, edge, bank, strain, psd, row, twist, col)


CHUNK = 256


def inverse_kernel(
    coherent_hbm, first_hbm, second_hbm, third_hbm, perm_hbm, back_hbm, untwist_hbm, last_hbm, out_hbm,
    coherent, banks, perm, back, untwist, last, products, partials, outs, load_sem, out_sem,
):
    loads = [
        pltpu.make_async_copy(source, target, load_sem.at[i])
        for i, (source, target) in enumerate(
            (
                (coherent_hbm, coherent),
                (perm_hbm, perm),
                (first_hbm, banks.at[0]),
                (back_hbm, back),
                (untwist_hbm, untwist),
                (last_hbm, last),
                (second_hbm, banks.at[1]),
                (third_hbm, banks.at[2]),
            )
        )
    ]
    for load in loads:
        load.start()
    loads[0].wait()
    loads[1].wait()
    whole = jnp.dot(perm[...], coherent[...], preferred_element_type=F32).astype(BF16)
    coherent[...] = whole
    outgoing = []
    for r in range(STEPS):
        loads[(2, 6, 7)[r]].wait()
        real, imag = coherent[:, :HALF].astype(F32), coherent[:, HALF:].astype(F32)
        other_real = banks[r, :, :HALF].astype(F32)
        other_imag = banks[r, :, HALF:].astype(F32)
        products[r, :, :HALF] = (real * other_real + imag * other_imag).astype(BF16)
        products[r, :, HALF:] = (imag * other_real - real * other_imag).astype(BF16)
        if r == 0:
            for i in (3, 4, 5):
                loads[i].wait()
        for c in range(U // CHUNK):
            lanes = slice(c * CHUNK, (c + 1) * CHUNK)
            upper = slice(U + c * CHUNK, U + (c + 1) * CHUNK)
            first = jnp.dot(products[r], back[:, lanes], preferred_element_type=F32)
            second = jnp.dot(products[r], back[:, upper], preferred_element_type=F32)
            cosine, sine = untwist[0, :, lanes], untwist[1, :, lanes]
            partials[c % 2, :V] = (first * cosine - second * sine).astype(BF16)
            partials[c % 2, V:] = (first * sine + second * cosine).astype(BF16)
            made = jnp.dot(last[...], partials[c % 2], preferred_element_type=F32).astype(BF16)
            outs[r, :, :, lanes] = made.reshape(V // 2, 2, CHUNK)
        outgoing.append(pltpu.make_async_copy(outs.at[r], out_hbm.at[0, 0, r], out_sem.at[r]))
        outgoing[r].start()
    for leaving in outgoing:
        leaving.wait()


def inverse_steps(coherent, banks, perm, back, untwist, last):
    return pl.pallas_call(
        inverse_kernel,
        out_shape=jax.ShapeDtypeStruct((1, 1, STEPS, V // 2, 2, U), BF16),
        in_specs=[HB] * 8,
        out_specs=HB,
        scratch_shapes=[
            pltpu.VMEM((V, U), BF16),
            pltpu.VMEM((STEPS, V, U), BF16),
            pltpu.VMEM((V, V), BF16),
            pltpu.VMEM((U, 2 * U), BF16),
            pltpu.VMEM((2, V, U), F32),
            pltpu.VMEM((V, 2 * V), BF16),
            pltpu.VMEM((STEPS, V, U), BF16),
            pltpu.VMEM((2, 2 * V, CHUNK), BF16),
            pltpu.VMEM((STEPS, V // 2, 2, U), BF16),
            pltpu.SemaphoreType.DMA((8,)),
            pltpu.SemaphoreType.DMA((STEPS,)),
        ],
        compiler_params=pltpu.CompilerParams(vmem_limit_bytes=LIMIT),
        name="inverse_steps",
    )(coherent, *banks, perm, back, untwist, last)


def body(strain, row_target, gate_start, gate_width, inverse_psd, templates, template_shift):
    row, twist, edge, col, perm, back, untwist, last = (jnp.asarray(t) for t in tables())
    coherent, *banks = filtered(
        gate_start,
        gate_width,
        template_shift,
        row_target,
        edge,
        templates,
        strain,
        inverse_psd,
        row,
        twist,
        col,
    )
    return inverse_steps(coherent, banks, perm, back, untwist, last)


def solution(mesh):
    in_specs = (
        P("seg", "det"),
        P("seg"),
        P("seg", None),
        P("seg", None),
        P(None, "det", None),
        P("seg", "det", None, None),
        P("seg"),
    )
    out_specs = P("seg", "det", None, None, None, None)
    return jax.shard_map(body, mesh=mesh, in_specs=in_specs, out_specs=out_specs, check_vma=False)
```

```python
import functools
import math

import jax
import jax.numpy as jnp
import numpy as np
from jax import lax
from jax.experimental import pallas as pl
from jax.experimental.pallas import tpu as pltpu
from jax.sharding import PartitionSpec as P

V = 512
U = 1024
DETECTORS = 3
BLOCK = 4
STEPS = 3
SAMPLES = 524288
SEGS = 64
DETS = 4
SLOTS = 3072
CAP = 48
QU = U // DETS
QV = V // DETS
ROWS = DETECTORS * V
HALF = U // 2
SHARE = V // 8
PLACES = (0, 2, 3, 1)
MIRROR = 32
MESH = pl.DeviceIdType.MESH
F32 = jnp.float32
BF16 = jnp.bfloat16
LIMIT = 60 * 1024 * 1024
VM = pl.BlockSpec(memory_space=pltpu.VMEM)
SM = pl.BlockSpec(memory_space=pltpu.SMEM)
HB = pl.BlockSpec(memory_space=pl.ANY)


def angles(rows, cols, modulus, direction):
    residue = (rows[:, None].astype(np.int64) * cols[None, :]) % modulus
    angle = np.float32(direction * 2.0 * math.pi / modulus) * residue.astype(np.float32)
    return np.cos(angle), np.sin(angle)


@functools.cache
def tables():
    v, u, m = np.arange(V), np.arange(U), np.arange(HALF)
    bf = np.dtype(jnp.bfloat16)
    c, s = angles(v[: V // 2], v, V, -1.0)
    s[0] = np.where(v % 2 == 0, 1.0, -1.0)
    row = (np.concatenate([c, s], 0) / math.sqrt(V)).astype(bf)
    twist = np.stack([*angles(v[: V // 2], u, SAMPLES, -1.0)])
    twist = twist.reshape(2, V // 2, DETS, QU).transpose(2, 0, 1, 3).astype(np.float32)
    edge = np.stack([*angles(v[V // 2 : V // 2 + 1], u, SAMPLES, -1.0)])
    edge = edge.reshape(2, 1, DETS, QU).transpose(2, 1, 0, 3).reshape(DETS, 1, 2 * QU)
    edge = np.tile(edge, (1, 8, 1)).astype(np.float32)

    def by_source(real_rows, imag_rows):
        both = np.stack([real_rows, imag_rows]) / math.sqrt(U)
        both = both.reshape(2, DETS, QU, U).transpose(1, 0, 2, 3)
        return both.reshape(DETS, 2 * QU, U).astype(bf)

    c, s = angles(u, m, U, -1.0)
    direct = by_source(np.concatenate([c, s], 1), np.concatenate([-s, c], 1))
    c, s = angles(u, m + 1, U, -1.0)
    mirrored = by_source(np.concatenate([c, s], 1), np.concatenate([s, -c], 1))
    col = np.stack([direct, mirrored])
    order = np.concatenate(
        [
            np.concatenate([p * SHARE + half, V - p * SHARE - half[::-1]])
            for p, half in ((p, np.arange(SHARE)) for p in PLACES)
        ]
    )
    order[QV - 1] = V // 2
    c, s = angles(m, u, U, 1.0)
    back = np.concatenate([np.concatenate([c, s], 1), np.concatenate([-s, c], 1)], 0)
    back = (back / math.sqrt(U)).astype(bf)
    untwist = np.stack([*angles(order, u, SAMPLES, 1.0)]).astype(np.float32)
    untwist = untwist.reshape(2, DETS, QV, U).transpose(1, 0, 2, 3)
    c, s = angles(np.arange(V // 4, 3 * V // 4), order, V, 1.0)
    last = np.stack([np.concatenate([c, -s], 1), np.concatenate([s, c], 1)], 1)
    last = (last / math.sqrt(V)).reshape(V, 2 * V).astype(bf)
    return row, twist, edge, col, back, untwist, last


GROUP = 16
LANES = 256
COUNT = SLOTS // LANES


def sort_ranks(me, target_ref, dest, ids):
    lane = lax.broadcasted_iota(jnp.int32, (LANES, LANES), 1)
    sub = lax.broadcasted_iota(jnp.int32, (LANES, LANES), 0)
    upper = jnp.where(sub <= lane, 1.0, 0.0).astype(BF16)
    seg = lax.broadcasted_iota(jnp.int32, (SEGS, LANES), 0)
    carry = jnp.zeros((SEGS, 1), F32)
    high = jnp.zeros((SEGS, SEGS), F32)
    low = jnp.zeros((SEGS, SEGS), F32)
    spread = (((1,), (1,)), ((), ()))
    for b in range(COUNT):
        t = target_ref[b * LANES : (b + 1) * LANES].reshape(1, LANES)
        owner = ((t >> 9) * 43691) >> 17
        local = t - owner * ROWS
        owner = jnp.where(t >= 0, (owner + SEGS - me) & (SEGS - 1), SEGS)
        mine = jnp.where(seg == owner, 1.0, 0.0)
        before = jnp.dot(mine.astype(BF16), upper, preferred_element_type=F32)
        rank = jnp.sum(mine * (before + carry), axis=0, keepdims=True).astype(jnp.int32) - 1
        carry = carry + jnp.sum(mine, axis=1, keepdims=True)
        dest[b : b + 1, :] = jnp.where(t >= 0, owner * CAP + rank, -1)
        order = jnp.where(seg == rank, 1.0, 0.0).astype(BF16)
        upper_part = (mine * ((local >> 6) + 1).astype(F32)).astype(BF16)
        lower_part = (mine * (local & 63).astype(F32)).astype(BF16)
        high = high + lax.dot_general(upper_part, order, spread, preferred_element_type=F32)
        low = low + lax.dot_general(lower_part, order, spread, preferred_element_type=F32)
    found = jnp.where(high > 0.5, high * 64.0 + low - 63.0, 0.0).astype(jnp.int32)
    found = jnp.concatenate([found, found], axis=1)
    side = lax.broadcasted_iota(jnp.int32, (SEGS, 128), 1) // 64
    parity = lax.broadcasted_iota(jnp.int32, (SEGS, 128), 0) & 1
    found = jnp.where(side == parity, found, 0)
    for o in range(SEGS):
        ids[o] = found[o : o + 1]


def shift_bank(shift, raw, bank):
    at = lax.broadcasted_iota(jnp.int32, (V, 128), 0)
    block, inner = at // QV, at % QV
    base = jnp.where(block == 0, 0, jnp.where(block == 3, SHARE, block * SHARE + SHARE))
    k = jnp.where(inner < SHARE, base + inner, V - base - (QV - 1) + inner)
    k = jnp.where(at == QV - 1, V // 2, k)
    lane = lax.broadcasted_iota(jnp.int32, (V, 2 * V), 1)
    pairs = raw[...].reshape(2 * V, HALF)
    parts = []
    for part in range(2):
        pick = jnp.where(lane == 2 * k[:, :1] + part, 1.0, 0.0).astype(BF16)
        parts.append(jnp.dot(pick, pairs, preferred_element_type=F32))
    real, imag = parts
    m = lax.broadcasted_iota(jnp.int32, (8, HALF), 1)
    angle = (-2.0 * math.pi / SAMPLES) * ((k * shift) % SAMPLES).astype(F32)
    row_cos, row_sin = jnp.cos(angle)[:, :1], jnp.sin(angle)[:, :1]
    angle = (-2.0 * math.pi / U) * ((m * shift) % U).astype(F32)
    col_cos, col_sin = jnp.cos(angle)[:1], jnp.sin(angle)[:1]
    cosine = row_cos * col_cos - row_sin * col_sin
    sine = row_cos * col_sin + row_sin * col_cos
    bank[0, :, :HALF] = (real * cosine - imag * sine).astype(BF16)
    bank[0, :, HALF:] = (real * sine + imag * cosine).astype(BF16)


PIECES = 16
PIECE = V // PIECES


def filter_kernel(
    start_ref, width_ref, shift_ref, target_ref, edge_ref, bank_ref, strain_ref, psd_hbm,
    row_hbm, twist_hbm, col_hbm, back_hbm, untwist_hbm, last_hbm,
    out_hbm,
    held, dest, rows, ids, arrived, arrived_ids, chosen, total, raw, bank, relay,
    turned, crossed, spec, coherent, psd_low, psd_high, row, twist, col,
    back, untwist, last, products, partials, outs,
    row_send, row_recv, id_send, id_recv, bank_send, bank_recv, turn_send, turn_recv,
    coh_send, coh_recv, out_sem, pass_send, pass_recv, piece_send, relay_recv, psd_send, psd_recv, table_sem, own_sem,
):
    me = lax.axis_index("seg")
    det = lax.axis_index("det")
    core = me % 2
    place = (me % 32) // 2
    barrier = pltpu.get_barrier_semaphore()

    def greet(o, _):
        pl.semaphore_signal(
            barrier, inc=1, device_id={"seg": (me + o) % SEGS}, device_id_type=MESH
        )
        return 0

    lax.fori_loop(1, SEGS, greet, 0)
    for o in range(1, DETS):
        pl.semaphore_signal(
            barrier, inc=1, device_id={"det": (det + o) % DETS}, device_id_type=MESH
        )
    across = {"seg": (me + MIRROR) % SEGS, "det": DETS - 1 - det}
    pl.semaphore_signal(barrier, inc=1, device_id=across, device_id_type=MESH)
    fetches = [
        pltpu.make_async_copy(source, held_at, table_sem.at[i])
        for i, (source, held_at) in enumerate(
            (
                (row_hbm, row),
                (twist_hbm.at[det], twist),
                (col_hbm, col),
                (back_hbm, back),
                (untwist_hbm, untwist),
                (last_hbm, last),
            )
        )
    ]
    own_bank = pltpu.make_async_copy(bank_ref.at[det], raw.at[det], own_sem.at[0])
    own_bank.start()
    pl.semaphore_wait(barrier, SEGS + DETS - 1)

    def bank_copy(o):
        other = (det + o) % DETS
        return pltpu.make_async_remote_copy(
            src_ref=bank_ref.at[other],
            dst_ref=raw.at[det],
            send_sem=bank_send.at[o],
            recv_sem=bank_recv.at[o],
            device_id={"det": other},
            device_id_type=MESH,
        )

    for o in (2, 1, 3):
        bank_copy(o).start()

    upper_det = det >= DETS // 2

    def psd_copy(target, lane):
        return pltpu.make_async_remote_copy(
            src_ref=psd_hbm.at[:, pl.ds(SHARE, SHARE)],
            dst_ref=target,
            send_sem=psd_send.at[0],
            recv_sem=psd_recv.at[lane],
            device_id=across,
            device_id_type=MESH,
        )

    to_low = psd_copy(psd_low, 0)
    to_high = psd_copy(psd_high.at[:, pl.ds(0, SHARE)], 0)
    to_rest = pltpu.make_async_remote_copy(
        src_ref=psd_hbm.at[:, pl.ds(0, 8)],
        dst_ref=psd_high.at[:, pl.ds(SHARE, 8)],
        send_sem=psd_send.at[1],
        recv_sem=psd_recv.at[1],
        device_id={"det": (det + 2) % DETS},
        device_id_type=MESH,
    )
    keep_low = pltpu.make_async_copy(psd_hbm.at[:, pl.ds(0, SHARE)], psd_low, own_sem.at[4])
    keep_high = pltpu.make_async_copy(psd_hbm.at[:, pl.ds(0, SHARE + 8)], psd_high, own_sem.at[4])

    @pl.when(upper_det)
    def _():
        to_high.start()
        to_rest.start()
        keep_high.start()

    @pl.when(jnp.logical_not(upper_det))
    def _():
        to_low.start()
        keep_low.start()

    def row_copy(o):
        return pltpu.make_async_remote_copy(
            src_ref=rows.at[pl.ds(o * CAP, CAP)],
            dst_ref=arrived.at[o, pl.ds(0, CAP)],
            send_sem=row_send.at[o],
            recv_sem=row_recv.at[o],
            device_id={"seg": (me + o) % SEGS},
            device_id_type=MESH,
        )

    def id_copy(o):
        return pltpu.make_async_remote_copy(
            src_ref=ids.at[o],
            dst_ref=arrived_ids.at[o],
            send_sem=id_send.at[o],
            recv_sem=id_recv.at[o],
            device_id={"seg": (me + o) % SEGS},
            device_id_type=MESH,
        )

    for fetch in fetches:
        fetch.start()
    held[...] = strain_ref[...].astype(BF16)
    sort_ranks(me, target_ref, dest, ids)
    step = GROUP * CAP

    def send(o, _):
        id_copy(o).start()
        row_copy(o).start()
        return 0

    for g in range(SEGS // GROUP):
        want = lax.broadcasted_iota(jnp.int32, (step, LANES), 0) + g * step
        picks = [
            jnp.where(want == dest[b : b + 1, :], 1.0, 0.0).astype(BF16) for b in range(COUNT)
        ]
        picked = jnp.dot(jnp.concatenate(picks, axis=1), held[...], preferred_element_type=F32)
        rows[g * step : (g + 1) * step] = picked.astype(BF16)
        lax.fori_loop(max(1, g * GROUP), (g + 1) * GROUP, send, 0)
    own_rows = pltpu.make_async_copy(
        rows.at[pl.ds(0, CAP)], arrived.at[0, pl.ds(0, CAP)], own_sem.at[1]
    )
    own_rows.start()
    own_ids = pltpu.make_async_copy(ids.at[0], arrived_ids.at[0], own_sem.at[2])
    own_ids.start()
    arrived[:, CAP:, :] = jnp.zeros((SEGS, 64 - CAP, QU), BF16)

    own_bank.wait()
    for o in range(1, DETS):
        bank_copy(o).wait_recv()
    shift_bank(shift_ref[det], raw, bank)

    def whole_pass(source, target, lane, back):
        return pltpu.make_async_remote_copy(
            src_ref=source,
            dst_ref=target,
            send_sem=pass_send.at[lane],
            recv_sem=pass_recv.at[lane],
            device_id={"seg": (me + SEGS - back) % SEGS},
            device_id_type=MESH,
        )

    hot = (me % 32) < 2
    odd = core == 1
    to_next = whole_pass(bank.at[0], bank.at[1], 0, 1)
    to_after = whole_pass(bank.at[0], bank.at[2], 1, 2)
    onward = pltpu.make_async_remote_copy(
        src_ref=bank.at[1],
        dst_ref=bank.at[2],
        send_sem=pass_send.at[2],
        recv_sem=pass_recv.at[1],
        device_id={"seg": (me + SEGS - 1) % SEGS},
        device_id_type=MESH,
    )
    corner = (me // 32) * 32
    far = (corner + SEGS - 1) % SEGS

    def piece_copy(i):
        return pltpu.make_async_remote_copy(
            src_ref=bank.at[0, pl.ds(i * PIECE, PIECE)],
            dst_ref=relay,
            send_sem=piece_send.at[i],
            recv_sem=relay_recv.at[0],
            device_id={"seg": corner + 2 * i + core},
            device_id_type=MESH,
        )

    def last_hop(source, lane, at):
        return pltpu.make_async_remote_copy(
            src_ref=source,
            dst_ref=bank.at[1 + lane, pl.ds(at * PIECE, PIECE)],
            send_sem=piece_send.at[0],
            recv_sem=pass_recv.at[lane],
            device_id={"seg": far},
            device_id_type=MESH,
        )

    def pieces(i, _):
        piece_copy(i).start()
        return 0

    def pieces_sent(i, _):
        piece_copy(i).wait_send()
        return 0

    @pl.when(jnp.logical_or(odd, jnp.logical_not(hot)))
    def _():
        to_next.start()

    @pl.when(jnp.logical_and(odd, jnp.logical_not(hot)))
    def _():
        to_after.start()

    @pl.when(hot)
    def _():
        lax.fori_loop(1, PIECES, pieces, 0)

    @pl.when(jnp.logical_and(hot, odd))
    def _():
        last_hop(bank.at[0, pl.ds(0, PIECE)], 1, 0).start()

    @pl.when(jnp.logical_and(hot, jnp.logical_not(odd)))
    def _():
        last_hop(bank.at[0, pl.ds(0, PIECE)], 0, 0).start()

    own_rows.wait()
    own_ids.wait()

    def receive(o, _):
        id_copy(o).wait_recv()
        row_copy(o).wait_recv()
        return 0

    wide = GROUP * 64
    groups = SEGS // GROUP
    for g in range(groups):
        lax.fori_loop(max(1, g * GROUP), (g + 1) * GROUP, receive, 0)
        for p in range(GROUP // 2):
            o = g * GROUP + 2 * p
            ident = arrived_ids[o] + arrived_ids[o + 1] - 1
            chosen[:, p * 128 : (p + 1) * 128] = jnp.where(
                lax.broadcasted_iota(jnp.int32, (ROWS, 128), 0) == ident, 1.0, 0.0
            ).astype(BF16)
        block = arrived[g * GROUP : (g + 1) * GROUP].reshape(wide, QU)
        part = jnp.dot(chosen[...], block, preferred_element_type=F32)
        if g == 0:
            total[...] = part
        else:
            total[...] += part

    def turn_copy(o, d):
        other = (det + o) % DETS
        return pltpu.make_async_remote_copy(
            src_ref=turned.at[other, d],
            dst_ref=crossed.at[o, d],
            send_sem=turn_send.at[o, d],
            recv_sem=turn_recv.at[o, d],
            device_id={"det": other},
            device_id_type=MESH,
        )

    sample = lax.broadcasted_iota(jnp.int32, (V, QU), 0) * U
    sample = sample + lax.broadcasted_iota(jnp.int32, (V, QU), 1) + det * QU
    for fetch in fetches[:3]:
        fetch.wait()
    for d in range(DETECTORS):
        begin = start_ref[0, d]
        end = begin + width_ref[0, d]
        inside = (sample >= begin) & (sample < end)
        gated = jnp.where(inside, 0.0, total[d * V : (d + 1) * V]).astype(BF16)
        folded = jnp.dot(row[...], gated, preferred_element_type=F32)
        real, imag = folded[: V // 2], folded[V // 2 :]
        cosine, sine = twist[0], twist[1]
        first = (real * cosine - imag * sine).astype(BF16)
        second = (real * sine + imag * cosine).astype(BF16)
        for q in range(DETS):
            at = PLACES[q] * SHARE
            turned[q, d, :, :QU] = first[at : at + SHARE]
            turned[q, d, :, QU:] = second[at : at + SHARE]
        for o in (2, 1, 3):
            turn_copy(o, d).start()

    @pl.when(jnp.logical_not(hot))
    def _():
        piece_copy(1).wait_recv()

    @pl.when(jnp.logical_and(jnp.logical_not(hot), odd))
    def _():
        last_hop(relay, 1, place).start()

    @pl.when(jnp.logical_and(jnp.logical_not(hot), jnp.logical_not(odd)))
    def _():
        last_hop(relay, 0, place).start()

    high = DETECTORS * SHARE
    row_at = lax.broadcasted_iota(jnp.int32, (high, high), 0)
    col_at = lax.broadcasted_iota(jnp.int32, (high, high), 1)
    flip = (row_at // SHARE == col_at // SHARE) & (row_at % SHARE + col_at % SHARE == SHARE - 1)
    flip = jnp.where(flip, 1.0, 0.0).astype(BF16)
    packed = lax.broadcasted_iota(jnp.int32, (high, 2 * QU), 0) % SHARE + det == 0
    imag_side = lax.broadcasted_iota(jnp.int32, (high, 2 * QU), 1) >= QU
    for o in (0, 1, 3, 2):
        source = (det + DETS - o) % DETS
        if o == 0:
            came = turned[det]
        else:
            for d in range(DETECTORS):
                turn_copy(o, d).wait_recv()
            came = crossed[o]
        came = came.reshape(high, 2 * QU)
        wide_came = came.astype(F32)
        direct = jnp.where(packed & imag_side, 0.0, wide_came).astype(BF16)
        twin = wide_came[:, QU:]
        twin = jnp.concatenate([twin, twin], axis=1) * edge_ref[source][:1]
        mirrored = jnp.where(packed, twin, wide_came).astype(BF16)
        mirrored = jnp.dot(flip, mirrored, preferred_element_type=F32).astype(BF16)
        part = jnp.dot(direct, col[0, source], preferred_element_type=F32)
        other = jnp.dot(mirrored, col[1, source], preferred_element_type=F32)
        if o == 0:
            spec[0], spec[1] = part, other
        else:
            spec[0] += part
            spec[1] += other

    @pl.when(upper_det)
    def _():
        to_low.wait_recv()
        keep_high.wait()

    @pl.when(jnp.logical_not(upper_det))
    def _():
        to_high.wait_recv()
        to_rest.wait_recv()
        keep_low.wait()

    for half in range(2):
        cols = slice(half * HALF, (half + 1) * HALF)
        direct, mirrored = 0.0, 0.0
        for d in range(DETECTORS):
            rows_of = slice(d * SHARE, (d + 1) * SHARE)
            direct = direct + psd_low[d] * spec[0, rows_of, cols]
            mirrored = mirrored + psd_high[d, 1 : SHARE + 1] * spec[1, rows_of, cols]
        coherent[det, :SHARE, cols] = direct.astype(BF16)
        coherent[det, SHARE:, cols] = mirrored.astype(BF16)

    near = det + 1 - 2 * (det % 2)
    entry = DETS // 2 - det // 2
    beyond = DETS - 1 - det // 2 * (DETS - 1)
    middle = jnp.logical_or(det == 1, det == 2)

    def coherent_copy(block, other, lane):
        return pltpu.make_async_remote_copy(
            src_ref=coherent.at[block],
            dst_ref=coherent.at[block],
            send_sem=coh_send.at[lane],
            recv_sem=coh_recv.at[block],
            device_id={"det": other},
            device_id_type=MESH,
        )

    coherent_copy(det, entry, 0).start()
    coherent_copy(det, near, 1).start()
    to_next.wait_recv()

    @pl.when(odd)
    def _():
        onward.start()

    for fetch in fetches[3:]:
        fetch.wait()

    def multiply(block, r):
        real = coherent[block, :, :HALF].astype(F32)
        imag = coherent[block, :, HALF:].astype(F32)
        at = pl.ds(pl.multiple_of(block * QV, QV), QV)
        other_real = bank[r, at, :HALF].astype(F32)
        other_imag = bank[r, at, HALF:].astype(F32)
        into = slice(r * QV, (r + 1) * QV)
        products[into, :HALF] = (real * other_real + imag * other_imag).astype(BF16)
        products[into, HALF:] = (imag * other_real - real * other_imag).astype(BF16)

    def invert(block):
        for r in range(STEPS):
            multiply(block, r)
        for half in range(2):
            lanes = slice(half * HALF, (half + 1) * HALF)
            upper = slice(U + half * HALF, U + (half + 1) * HALF)
            first = jnp.dot(products[...], back[:, lanes], preferred_element_type=F32)
            second = jnp.dot(products[...], back[:, upper], preferred_element_type=F32)
            cosine, sine = untwist[block, 0, :, lanes], untwist[block, 1, :, lanes]
            for r in range(STEPS):
                real, imag = first[r * QV : (r + 1) * QV], second[r * QV : (r + 1) * QV]
                partials[r, 0, block, :, lanes] = (real * cosine - imag * sine).astype(BF16)
                partials[r, 1, block, :, lanes] = (real * sine + imag * cosine).astype(BF16)

    to_after.wait_recv()
    invert(det)
    coherent_copy(near, det, 1).wait_recv()
    invert(near)
    coherent_copy(entry, det, 0).wait_recv()

    @pl.when(middle)
    def _():
        coherent_copy(entry, near, 2).start()
        coherent_copy(beyond, det, 0).wait_recv()
        coherent_copy(beyond, near, 3).start()

    invert(entry)

    @pl.when(jnp.logical_not(middle))
    def _():
        coherent_copy(beyond, det, 0).wait_recv()

    invert(beyond)
    outgoing = []
    for r in range(STEPS):
        made = jnp.dot(last[...], partials[r].reshape(2 * V, U), preferred_element_type=F32)
        outs[r] = made.astype(BF16).reshape(V // 2, 2, U)
        outgoing.append(pltpu.make_async_copy(outs.at[r], out_hbm.at[0, 0, r], out_sem.at[r]))
        outgoing[r].start()

    @pl.when(upper_det)
    def _():
        to_high.wait_send()
        to_rest.wait_send()

    @pl.when(jnp.logical_not(upper_det))
    def _():
        to_low.wait_send()

    @pl.when(jnp.logical_or(odd, jnp.logical_not(hot)))
    def _():
        to_next.wait_send()

    @pl.when(jnp.logical_and(odd, jnp.logical_not(hot)))
    def _():
        to_after.wait_send()

    @pl.when(hot)
    def _():
        lax.fori_loop(1, PIECES, pieces_sent, 0)

    last_hop(relay, 0, place).wait_send()

    @pl.when(odd)
    def _():
        onward.wait_send()

    def sent(o, _):
        id_copy(o).wait_send()
        row_copy(o).wait_send()
        return 0

    lax.fori_loop(1, SEGS, sent, 0)
    for o in range(1, DETS):
        bank_copy(o).wait_send()
        for d in range(DETECTORS):
            turn_copy(o, d).wait_send()
    coherent_copy(det, entry, 0).wait_send()
    coherent_copy(det, near, 1).wait_send()

    @pl.when(middle)
    def _():
        coherent_copy(entry, near, 2).wait_send()
        coherent_copy(beyond, near, 3).wait_send()

    for leaving in outgoing:
        leaving.wait()


def filtered(*operands):
    dma = pltpu.SemaphoreType.DMA
    return pl.pallas_call(
        filter_kernel,
        out_shape=jax.ShapeDtypeStruct((1, 1, STEPS, V // 2, 2, U), BF16),
        in_specs=[SM, SM, SM, VM, VM, HB, VM] + [HB] * 7,
        out_specs=HB,
        scratch_shapes=[
            pltpu.VMEM((SLOTS, QU), BF16),
            pltpu.VMEM((16, LANES), jnp.int32),
            pltpu.VMEM((SLOTS, QU), BF16),
            pltpu.VMEM((SEGS, 1, 128), jnp.int32),
            pltpu.VMEM((SEGS, 64, QU), BF16),
            pltpu.VMEM((SEGS, 1, 128), jnp.int32),
            pltpu.VMEM((ROWS, GROUP * 64), BF16),
            pltpu.VMEM((ROWS, QU), F32),
            pltpu.VMEM((DETS, QV, 2, HALF), BF16),
            pltpu.VMEM((STEPS, V, U), BF16),
            pltpu.VMEM((PIECE, U), BF16),
            pltpu.VMEM((DETS, DETECTORS, SHARE, 2 * QU), BF16),
            pltpu.VMEM((DETS, DETECTORS, SHARE, 2 * QU), BF16),
            pltpu.VMEM((2, DETECTORS * SHARE, U), F32),
            pltpu.VMEM((DETS, QV, U), BF16),
            pltpu.VMEM((DETECTORS, SHARE, HALF), F32),
            pltpu.VMEM((DETECTORS, SHARE + 8, HALF), F32),
            pltpu.VMEM((V, V), BF16),
            pltpu.VMEM((2, V // 2, QU), F32),
            pltpu.VMEM((2, DETS, 2 * QU, U), BF16),
            pltpu.VMEM((U, 2 * U), BF16),
            pltpu.VMEM((DETS, 2, QV, U), F32),
            pltpu.VMEM((V, 2 * V), BF16),
            pltpu.VMEM((STEPS * QV, U), BF16),
            pltpu.VMEM((STEPS, 2, DETS, QV, U), BF16),
            pltpu.VMEM((STEPS, V // 2, 2, U), BF16),
            dma((SEGS,)), dma((SEGS,)), dma((SEGS,)), dma((SEGS,)),
            dma((DETS,)), dma((DETS,)),
            dma((DETS, DETECTORS)), dma((DETS, DETECTORS)),
            dma((4,)), dma((DETS,)), dma((STEPS,)),
            dma((3,)), dma((2,)), dma((PIECES,)), dma((1,)), dma((2,)), dma((2,)), dma((6,)), dma((5,)),
        ],
        compiler_params=pltpu.CompilerParams(
            vmem_limit_bytes=LIMIT, collective_id=0, has_side_effects=True
        ),
        cost_estimate=pl.CostEstimate(
            flops=12_000_000_000, bytes_accessed=16_000_000, transcendentals=0
        ),
        name="filtered",
    )(*operands)


def body(strain, row_target, gate_start, gate_width, inverse_psd, templates, template_shift):
    row, twist, edge, col, back, untwist, last = (jnp.asarray(t) for t in tables())
    return filtered(
        gate_start,
        gate_width,
        template_shift,
        row_target,
        edge,
        templates,
        strain,
        inverse_psd,
        row,
        twist,
        col,
        back,
        untwist,
        last,
    )


def solution(mesh):
    in_specs = (
        P("seg", "det"),
        P("seg"),
        P("seg", None),
        P("seg", None),
        P(None, "det", None),
        P("seg", "det", None, None),
        P("seg"),
    )
    out_specs = P("seg", "det", None, None, None, None)
    return jax.shard_map(body, mesh=mesh, in_specs=in_specs, out_specs=out_specs, check_vma=False)
```

```python
import functools
import math

import jax
import jax.numpy as jnp
import numpy as np
from jax import lax
from jax.experimental import pallas as pl
from jax.experimental.pallas import tpu as pltpu
from jax.sharding import PartitionSpec as P

V = 512
U = 1024
DETECTORS = 3
BLOCK = 4
STEPS = 3
SAMPLES = 524288
SEGS = 64
DETS = 4
SLOTS = 3072
CAP = 48
QU = U // DETS
QV = V // DETS
ROWS = DETECTORS * V
HALF = U // 2
SHARE = V // 8
PLACES = (0, 2, 3, 1)
MIRROR = 32
MESH = pl.DeviceIdType.MESH
F32 = jnp.float32
BF16 = jnp.bfloat16
LIMIT = 60 * 1024 * 1024
VM = pl.BlockSpec(memory_space=pltpu.VMEM)
SM = pl.BlockSpec(memory_space=pltpu.SMEM)
HB = pl.BlockSpec(memory_space=pl.ANY)


def angles(rows, cols, modulus, direction):
    residue = (rows[:, None].astype(np.int64) * cols[None, :]) % modulus
    angle = np.float32(direction * 2.0 * math.pi / modulus) * residue.astype(np.float32)
    return np.cos(angle), np.sin(angle)


@functools.cache
def tables():
    v, u, m = np.arange(V), np.arange(U), np.arange(HALF)
    bf = np.dtype(jnp.bfloat16)
    c, s = angles(v[: V // 2], v, V, -1.0)
    s[0] = np.where(v % 2 == 0, 1.0, -1.0)
    row = (np.concatenate([c, s], 0) / math.sqrt(V)).astype(bf)
    twist = np.stack([*angles(v[: V // 2], u, SAMPLES, -1.0)])
    twist = twist.reshape(2, V // 2, DETS, QU).transpose(2, 0, 1, 3).astype(np.float32)
    edge = np.stack([*angles(v[V // 2 : V // 2 + 1], u, SAMPLES, -1.0)])
    edge = edge.reshape(2, 1, DETS, QU).transpose(2, 1, 0, 3).reshape(DETS, 1, 2 * QU)
    edge = np.tile(edge, (1, 8, 1)).astype(np.float32)

    def by_source(real_rows, imag_rows):
        both = np.stack([real_rows, imag_rows]) / math.sqrt(U)
        both = both.reshape(2, DETS, QU, U).transpose(1, 0, 2, 3)
        return both.reshape(DETS, 2 * QU, U).astype(bf)

    c, s = angles(u, m, U, -1.0)
    direct = by_source(np.concatenate([c, s], 1), np.concatenate([-s, c], 1))
    c, s = angles(u, m + 1, U, -1.0)
    mirrored = by_source(np.concatenate([c, s], 1), np.concatenate([s, -c], 1))
    col = np.stack([direct, mirrored])
    order = np.concatenate(
        [
            np.concatenate([p * SHARE + half, V - p * SHARE - half[::-1]])
            for p, half in ((p, np.arange(SHARE)) for p in PLACES)
        ]
    )
    order[QV - 1] = V // 2
    c, s = angles(m, u, U, 1.0)
    back = np.concatenate([np.concatenate([c, s], 1), np.concatenate([-s, c], 1)], 0)
    back = (back / math.sqrt(U)).astype(bf)
    untwist = np.stack([*angles(order, u, SAMPLES, 1.0)]).astype(np.float32)
    untwist = untwist.reshape(2, DETS, QV, U).transpose(1, 0, 2, 3)
    c, s = angles(np.arange(V // 4, 3 * V // 4), order, V, 1.0)
    last = np.stack([np.concatenate([c, -s], 1), np.concatenate([s, c], 1)], 1)
    last = (last / math.sqrt(V)).reshape(V, 2 * V).astype(bf)
    return row, twist, edge, col, back, untwist, last


GROUP = 16
BATCH = 8
LANES = 256
COUNT = SLOTS // LANES


def sort_ranks(me, target_ref, dest, ids):
    lane = lax.broadcasted_iota(jnp.int32, (LANES, LANES), 1)
    sub = lax.broadcasted_iota(jnp.int32, (LANES, LANES), 0)
    upper = jnp.where(sub <= lane, 1.0, 0.0).astype(BF16)
    seg = lax.broadcasted_iota(jnp.int32, (SEGS, LANES), 0)
    carry = jnp.zeros((SEGS, 1), F32)
    high = jnp.zeros((SEGS, SEGS), F32)
    low = jnp.zeros((SEGS, SEGS), F32)
    spread = (((1,), (1,)), ((), ()))
    for b in range(COUNT):
        t = target_ref[b * LANES : (b + 1) * LANES].reshape(1, LANES)
        owner = ((t >> 9) * 43691) >> 17
        local = t - owner * ROWS
        owner = jnp.where(t >= 0, (owner + SEGS - me) & (SEGS - 1), SEGS)
        mine = jnp.where(seg == owner, 1.0, 0.0)
        before = jnp.dot(mine.astype(BF16), upper, preferred_element_type=F32)
        rank = jnp.sum(mine * (before + carry), axis=0, keepdims=True).astype(jnp.int32) - 1
        carry = carry + jnp.sum(mine, axis=1, keepdims=True)
        dest[b : b + 1, :] = jnp.where(t >= 0, owner * CAP + rank, -1)
        order = jnp.where(seg == rank, 1.0, 0.0).astype(BF16)
        upper_part = (mine * ((local >> 6) + 1).astype(F32)).astype(BF16)
        lower_part = (mine * (local & 63).astype(F32)).astype(BF16)
        high = high + lax.dot_general(upper_part, order, spread, preferred_element_type=F32)
        low = low + lax.dot_general(lower_part, order, spread, preferred_element_type=F32)
    found = jnp.where(high > 0.5, high * 64.0 + low - 63.0, 0.0).astype(jnp.int32)
    found = jnp.concatenate([found, found], axis=1)
    side = lax.broadcasted_iota(jnp.int32, (SEGS, 128), 1) // 64
    parity = lax.broadcasted_iota(jnp.int32, (SEGS, 128), 0) & 1
    found = jnp.where(side == parity, found, 0)
    for o in range(SEGS):
        ids[o] = found[o : o + 1]


def shift_bank(shift, raw, bank):
    at = lax.broadcasted_iota(jnp.int32, (V, 128), 0)
    block, inner = at // QV, at % QV
    base = jnp.where(block == 0, 0, jnp.where(block == 3, SHARE, block * SHARE + SHARE))
    k = jnp.where(inner < SHARE, base + inner, V - base - (QV - 1) + inner)
    k = jnp.where(at == QV - 1, V // 2, k)
    lane = lax.broadcasted_iota(jnp.int32, (V, 2 * V), 1)
    pairs = raw[...].reshape(2 * V, HALF)
    parts = []
    for part in range(2):
        pick = jnp.where(lane == 2 * k[:, :1] + part, 1.0, 0.0).astype(BF16)
        parts.append(jnp.dot(pick, pairs, preferred_element_type=F32))
    real, imag = parts
    m = lax.broadcasted_iota(jnp.int32, (8, HALF), 1)
    angle = (-2.0 * math.pi / SAMPLES) * ((k * shift) % SAMPLES).astype(F32)
    row_cos, row_sin = jnp.cos(angle)[:, :1], jnp.sin(angle)[:, :1]
    angle = (-2.0 * math.pi / U) * ((m * shift) % U).astype(F32)
    col_cos, col_sin = jnp.cos(angle)[:1], jnp.sin(angle)[:1]
    cosine = row_cos * col_cos - row_sin * col_sin
    sine = row_cos * col_sin + row_sin * col_cos
    bank[0, :, :HALF] = (real * cosine - imag * sine).astype(BF16)
    bank[0, :, HALF:] = (real * sine + imag * cosine).astype(BF16)


PIECES = 16
PART = 32
PARTS = QV // PART
PIECE = V // PIECES


def filter_kernel(
    start_ref, width_ref, shift_ref, target_ref, edge_ref, bank_ref, strain_hbm, psd_hbm,
    row_hbm, twist_hbm, col_hbm, back_hbm, untwist_hbm,
    out_hbm,
    strain, held, dest, rows, ids, arrived, arrived_ids, chosen, total, raw, bank, relay,
    turned, crossed, spec, coherent, psd_low, psd_high, row, twist, col,
    back, untwist, products, partials,
    row_send, row_recv, id_send, id_recv, bank_send, bank_recv, turn_send, turn_recv,
    coh_send, coh_recv, out_sem, pass_send, pass_recv, piece_send, relay_recv, psd_send, psd_recv, table_sem, own_sem,
):
    me = lax.axis_index("seg")
    det = lax.axis_index("det")
    core = me % 2
    place = (me % 32) // 2
    barrier = pltpu.get_barrier_semaphore()
    own_strain = pltpu.make_async_copy(strain_hbm, strain, own_sem.at[3])
    own_strain.start()

    def greet(o, _):
        pl.semaphore_signal(
            barrier, inc=1, device_id={"seg": (me + o) % SEGS}, device_id_type=MESH
        )
        return 0

    lax.fori_loop(1, SEGS, greet, 0)
    for o in range(1, DETS):
        pl.semaphore_signal(
            barrier, inc=1, device_id={"det": (det + o) % DETS}, device_id_type=MESH
        )
    across = {"seg": (me + MIRROR) % SEGS, "det": DETS - 1 - det}
    pl.semaphore_signal(barrier, inc=1, device_id=across, device_id_type=MESH)
    fetches = [
        pltpu.make_async_copy(source, held_at, table_sem.at[i])
        for i, (source, held_at) in enumerate(
            (
                (row_hbm, row),
                (twist_hbm.at[det], twist),
                (col_hbm, col),
                (back_hbm, back),
                (untwist_hbm, untwist),
            )
        )
    ]
    own_bank = pltpu.make_async_copy(bank_ref.at[det], raw.at[det], own_sem.at[0])
    own_bank.start()
    pl.semaphore_wait(barrier, SEGS + DETS - 1)

    def bank_copy(o):
        other = (det + o) % DETS
        return pltpu.make_async_remote_copy(
            src_ref=bank_ref.at[other],
            dst_ref=raw.at[det],
            send_sem=bank_send.at[o],
            recv_sem=bank_recv.at[o],
            device_id={"det": other},
            device_id_type=MESH,
        )

    for o in (2, 1, 3):
        bank_copy(o).start()

    upper_det = det >= DETS // 2

    def psd_copy(target, lane):
        return pltpu.make_async_remote_copy(
            src_ref=psd_hbm.at[:, pl.ds(SHARE, SHARE)],
            dst_ref=target,
            send_sem=psd_send.at[0],
            recv_sem=psd_recv.at[lane],
            device_id=across,
            device_id_type=MESH,
        )

    to_low = psd_copy(psd_low, 0)
    to_high = psd_copy(psd_high.at[:, pl.ds(0, SHARE)], 0)
    to_rest = pltpu.make_async_remote_copy(
        src_ref=psd_hbm.at[:, pl.ds(0, 8)],
        dst_ref=psd_high.at[:, pl.ds(SHARE, 8)],
        send_sem=psd_send.at[1],
        recv_sem=psd_recv.at[1],
        device_id={"det": (det + 2) % DETS},
        device_id_type=MESH,
    )
    keep_low = pltpu.make_async_copy(psd_hbm.at[:, pl.ds(0, SHARE)], psd_low, own_sem.at[4])
    keep_high = pltpu.make_async_copy(psd_hbm.at[:, pl.ds(0, SHARE + 8)], psd_high, own_sem.at[4])

    @pl.when(upper_det)
    def _():
        to_high.start()
        to_rest.start()
        keep_high.start()

    @pl.when(jnp.logical_not(upper_det))
    def _():
        to_low.start()
        keep_low.start()

    def row_copy(o):
        return pltpu.make_async_remote_copy(
            src_ref=rows.at[pl.ds(o * CAP, CAP)],
            dst_ref=arrived.at[o, pl.ds(0, CAP)],
            send_sem=row_send.at[o],
            recv_sem=row_recv.at[o],
            device_id={"seg": (me + o) % SEGS},
            device_id_type=MESH,
        )

    def id_copy(o):
        return pltpu.make_async_remote_copy(
            src_ref=ids.at[o],
            dst_ref=arrived_ids.at[o],
            send_sem=id_send.at[o],
            recv_sem=id_recv.at[o],
            device_id={"seg": (me + o) % SEGS},
            device_id_type=MESH,
        )

    for fetch in fetches:
        fetch.start()
    own_strain.wait()
    held[...] = strain[...].astype(BF16)
    sort_ranks(me, target_ref, dest, ids)
    step = GROUP * CAP

    def send(o, _):
        id_copy(o).start()
        row_copy(o).start()
        return 0

    for g in range(SEGS // GROUP):
        want = lax.broadcasted_iota(jnp.int32, (step, LANES), 0) + g * step
        picks = [
            jnp.where(want == dest[b : b + 1, :], 1.0, 0.0).astype(BF16) for b in range(COUNT)
        ]
        picked = jnp.dot(jnp.concatenate(picks, axis=1), held[...], preferred_element_type=F32)
        rows[g * step : (g + 1) * step] = picked.astype(BF16)
        lax.fori_loop(max(1, g * GROUP), (g + 1) * GROUP, send, 0)
    own_rows = pltpu.make_async_copy(
        rows.at[pl.ds(0, CAP)], arrived.at[0, pl.ds(0, CAP)], own_sem.at[1]
    )
    own_rows.start()
    own_ids = pltpu.make_async_copy(ids.at[0], arrived_ids.at[0], own_sem.at[2])
    own_ids.start()
    arrived[:, CAP:, :] = jnp.zeros((SEGS, 64 - CAP, QU), BF16)

    own_bank.wait()
    for o in range(1, DETS):
        bank_copy(o).wait_recv()
    shift_bank(shift_ref[det], raw, bank)

    def whole_pass(source, target, lane, back):
        return pltpu.make_async_remote_copy(
            src_ref=source,
            dst_ref=target,
            send_sem=pass_send.at[lane],
            recv_sem=pass_recv.at[lane],
            device_id={"seg": (me + SEGS - back) % SEGS},
            device_id_type=MESH,
        )

    hot = (me % 32) < 2
    odd = core == 1
    to_next = whole_pass(bank.at[0], bank.at[1], 0, 1)
    to_after = whole_pass(bank.at[0], bank.at[2], 1, 2)
    onward = pltpu.make_async_remote_copy(
        src_ref=bank.at[1],
        dst_ref=bank.at[2],
        send_sem=pass_send.at[2],
        recv_sem=pass_recv.at[1],
        device_id={"seg": (me + SEGS - 1) % SEGS},
        device_id_type=MESH,
    )
    corner = (me // 32) * 32
    far = (corner + SEGS - 1) % SEGS

    def piece_copy(i):
        return pltpu.make_async_remote_copy(
            src_ref=bank.at[0, pl.ds(i * PIECE, PIECE)],
            dst_ref=relay,
            send_sem=piece_send.at[i],
            recv_sem=relay_recv.at[0],
            device_id={"seg": corner + 2 * i + core},
            device_id_type=MESH,
        )

    def last_hop(source, lane, at):
        return pltpu.make_async_remote_copy(
            src_ref=source,
            dst_ref=bank.at[1 + lane, pl.ds(at * PIECE, PIECE)],
            send_sem=piece_send.at[0],
            recv_sem=pass_recv.at[lane],
            device_id={"seg": far},
            device_id_type=MESH,
        )

    def pieces(i, _):
        piece_copy(i).start()
        return 0

    def pieces_sent(i, _):
        piece_copy(i).wait_send()
        return 0

    @pl.when(jnp.logical_or(odd, jnp.logical_not(hot)))
    def _():
        to_next.start()

    @pl.when(jnp.logical_and(odd, jnp.logical_not(hot)))
    def _():
        to_after.start()

    @pl.when(hot)
    def _():
        lax.fori_loop(1, PIECES, pieces, 0)

    @pl.when(jnp.logical_and(hot, odd))
    def _():
        last_hop(bank.at[0, pl.ds(0, PIECE)], 1, 0).start()

    @pl.when(jnp.logical_and(hot, jnp.logical_not(odd)))
    def _():
        last_hop(bank.at[0, pl.ds(0, PIECE)], 0, 0).start()

    own_rows.wait()
    own_ids.wait()

    def receive(o, _):
        id_copy(o).wait_recv()
        row_copy(o).wait_recv()
        return 0

    wide = BATCH * 64
    groups = SEGS // BATCH
    for g in range(groups):
        lax.fori_loop(max(1, g * BATCH), (g + 1) * BATCH, receive, 0)
        for p in range(BATCH // 2):
            o = g * BATCH + 2 * p
            ident = arrived_ids[o] + arrived_ids[o + 1] - 1
            chosen[:, p * 128 : (p + 1) * 128] = jnp.where(
                lax.broadcasted_iota(jnp.int32, (ROWS, 128), 0) == ident, 1.0, 0.0
            ).astype(BF16)
        block = arrived[g * BATCH : (g + 1) * BATCH].reshape(wide, QU)
        part = jnp.dot(chosen[...], block, preferred_element_type=F32)
        if g == 0:
            total[...] = part
        else:
            total[...] += part

    def turn_copy(o, d):
        other = (det + o) % DETS
        return pltpu.make_async_remote_copy(
            src_ref=turned.at[other, d],
            dst_ref=crossed.at[o, d],
            send_sem=turn_send.at[o, d],
            recv_sem=turn_recv.at[o, d],
            device_id={"det": other},
            device_id_type=MESH,
        )

    sample = lax.broadcasted_iota(jnp.int32, (V, QU), 0) * U
    sample = sample + lax.broadcasted_iota(jnp.int32, (V, QU), 1) + det * QU
    for fetch in fetches[:3]:
        fetch.wait()
    for d in range(DETECTORS):
        begin = start_ref[0, d]
        end = begin + width_ref[0, d]
        inside = (sample >= begin) & (sample < end)
        gated = jnp.where(inside, 0.0, total[d * V : (d + 1) * V]).astype(BF16)
        folded = jnp.dot(row[...], gated, preferred_element_type=F32)
        real, imag = folded[: V // 2], folded[V // 2 :]
        cosine, sine = twist[0], twist[1]
        first = (real * cosine - imag * sine).astype(BF16)
        second = (real * sine + imag * cosine).astype(BF16)
        for q in range(DETS):
            at = PLACES[q] * SHARE
            turned[q, d, :, :QU] = first[at : at + SHARE]
            turned[q, d, :, QU:] = second[at : at + SHARE]
        for o in (2, 1, 3):
            turn_copy(o, d).start()

    @pl.when(jnp.logical_not(hot))
    def _():
        piece_copy(1).wait_recv()

    @pl.when(jnp.logical_and(jnp.logical_not(hot), odd))
    def _():
        last_hop(relay, 1, place).start()

    @pl.when(jnp.logical_and(jnp.logical_not(hot), jnp.logical_not(odd)))
    def _():
        last_hop(relay, 0, place).start()

    near = det + 1 - 2 * (det % 2)
    entry = DETS // 2 - det // 2
    beyond = DETS - 1 - det // 2 * (DETS - 1)
    middle = jnp.logical_or(det == 1, det == 2)

    def coherent_copy(block, other, lane, part):
        rows_of = pl.ds(part * PART, PART)
        return pltpu.make_async_remote_copy(
            src_ref=coherent.at[block, rows_of],
            dst_ref=coherent.at[block, rows_of],
            send_sem=coh_send.at[lane, part],
            recv_sem=coh_recv.at[block, part],
            device_id={"det": other},
            device_id_type=MESH,
        )

    def gather_rows(which, scale, shift, first_row):
        for half in range(2):
            cols = slice(half * HALF, (half + 1) * HALF)
            value = 0.0
            for d in range(DETECTORS):
                held_rows = spec[which, d * SHARE : (d + 1) * SHARE, cols]
                value = value + scale[d, shift : shift + SHARE] * held_rows
            coherent[det, first_row : first_row + SHARE, cols] = value.astype(BF16)
        for part in range(first_row // PART, (first_row + SHARE) // PART):
            coherent_copy(det, entry, 0, part).start()
            coherent_copy(det, near, 1, part).start()

    high = DETECTORS * SHARE
    row_at = lax.broadcasted_iota(jnp.int32, (high, high), 0)
    col_at = lax.broadcasted_iota(jnp.int32, (high, high), 1)
    flip = (row_at // SHARE == col_at // SHARE) & (row_at % SHARE + col_at % SHARE == SHARE - 1)
    flip = jnp.where(flip, 1.0, 0.0).astype(BF16)
    packed = lax.broadcasted_iota(jnp.int32, (high, 2 * QU), 0) % SHARE + det == 0
    imag_side = lax.broadcasted_iota(jnp.int32, (high, 2 * QU), 1) >= QU
    for o in (0, 1, 3, 2):
        source = (det + DETS - o) % DETS
        if o == 0:
            came = turned[det]
        else:
            for d in range(DETECTORS):
                turn_copy(o, d).wait_recv()
            came = crossed[o]
        came = came.reshape(high, 2 * QU)
        wide_came = came.astype(F32)
        direct = jnp.where(packed & imag_side, 0.0, wide_came).astype(BF16)
        twin = wide_came[:, QU:]
        twin = jnp.concatenate([twin, twin], axis=1) * edge_ref[source][:1]
        mirrored = jnp.where(packed, twin, wide_came).astype(BF16)
        mirrored = jnp.dot(flip, mirrored, preferred_element_type=F32).astype(BF16)
        if o == 2:

            @pl.when(upper_det)
            def _():
                to_low.wait_recv()
                keep_high.wait()

            @pl.when(jnp.logical_not(upper_det))
            def _():
                to_high.wait_recv()
                to_rest.wait_recv()
                keep_low.wait()

        part = jnp.dot(direct, col[0, source], preferred_element_type=F32)
        if o == 0:
            spec[0] = part
        else:
            spec[0] += part
        if o == 2:
            gather_rows(0, psd_low, 0, 0)
        other = jnp.dot(mirrored, col[1, source], preferred_element_type=F32)
        if o == 0:
            spec[1] = other
        else:
            spec[1] += other
    gather_rows(1, psd_high, 1, SHARE)
    to_next.wait_recv()

    @pl.when(odd)
    def _():
        onward.start()

    for fetch in fetches[3:]:
        fetch.wait()

    def multiply(block, r):
        real = coherent[block, :, :HALF].astype(F32)
        imag = coherent[block, :, HALF:].astype(F32)
        at = pl.ds(pl.multiple_of(block * QV, QV), QV)
        other_real = bank[r, at, :HALF].astype(F32)
        other_imag = bank[r, at, HALF:].astype(F32)
        into = slice(r * QV, (r + 1) * QV)
        products[into, :HALF] = (real * other_real + imag * other_imag).astype(BF16)
        products[into, HALF:] = (imag * other_real - real * other_imag).astype(BF16)

    def leave(block):
        return pltpu.make_async_copy(
            partials.at[:, :, block], out_hbm.at[:, :, block], out_sem.at[block]
        )

    def invert(block):
        for r in range(STEPS):
            multiply(block, r)
        for half in range(2):
            lanes = slice(half * HALF, (half + 1) * HALF)
            upper = slice(U + half * HALF, U + (half + 1) * HALF)
            first = jnp.dot(products[...], back[:, lanes], preferred_element_type=F32)
            second = jnp.dot(products[...], back[:, upper], preferred_element_type=F32)
            cosine, sine = untwist[block, 0, :, lanes], untwist[block, 1, :, lanes]
            for r in range(STEPS):
                real, imag = first[r * QV : (r + 1) * QV], second[r * QV : (r + 1) * QV]
                partials[r, 0, block, :, lanes] = (real * cosine - imag * sine).astype(BF16)
                partials[r, 1, block, :, lanes] = (real * sine + imag * cosine).astype(BF16)
        leave(block).start()

    def arrive(block):
        for part in range(PARTS):
            coherent_copy(block, det, 0, part).wait_recv()

    to_after.wait_recv()
    invert(det)

    @pl.when(middle)
    def _():
        for part in range(PARTS):
            coherent_copy(entry, det, 0, part).wait_recv()
            coherent_copy(entry, near, 2, part).start()
            coherent_copy(beyond, det, 0, part).wait_recv()
            coherent_copy(beyond, near, 3, part).start()

    arrive(near)
    invert(near)

    @pl.when(jnp.logical_not(middle))
    def _():
        arrive(entry)

    invert(entry)

    @pl.when(jnp.logical_not(middle))
    def _():
        arrive(beyond)

    invert(beyond)

    @pl.when(upper_det)
    def _():
        to_high.wait_send()
        to_rest.wait_send()

    @pl.when(jnp.logical_not(upper_det))
    def _():
        to_low.wait_send()

    @pl.when(jnp.logical_or(odd, jnp.logical_not(hot)))
    def _():
        to_next.wait_send()

    @pl.when(jnp.logical_and(odd, jnp.logical_not(hot)))
    def _():
        to_after.wait_send()

    @pl.when(hot)
    def _():
        lax.fori_loop(1, PIECES, pieces_sent, 0)

    last_hop(relay, 0, place).wait_send()

    @pl.when(odd)
    def _():
        onward.wait_send()

    def sent(o, _):
        id_copy(o).wait_send()
        row_copy(o).wait_send()
        return 0

    lax.fori_loop(1, SEGS, sent, 0)
    for o in range(1, DETS):
        bank_copy(o).wait_send()
        for d in range(DETECTORS):
            turn_copy(o, d).wait_send()
    for part in range(PARTS):
        coherent_copy(det, entry, 0, part).wait_send()
        coherent_copy(det, near, 1, part).wait_send()

    @pl.when(middle)
    def _():
        for part in range(PARTS):
            coherent_copy(entry, near, 2, part).wait_send()
            coherent_copy(beyond, near, 3, part).wait_send()

    for block in range(DETS):
        leave(block).wait()


def filtered(*operands):
    dma = pltpu.SemaphoreType.DMA
    return pl.pallas_call(
        filter_kernel,
        out_shape=jax.ShapeDtypeStruct((STEPS, 2, DETS, QV, U), BF16),
        in_specs=[SM, SM, SM, VM, VM] + [HB] * 8,
        out_specs=HB,
        scratch_shapes=[
            pltpu.VMEM((SLOTS, QU), F32),
            pltpu.VMEM((SLOTS, QU), BF16),
            pltpu.VMEM((16, LANES), jnp.int32),
            pltpu.VMEM((SLOTS, QU), BF16),
            pltpu.VMEM((SEGS, 1, 128), jnp.int32),
            pltpu.VMEM((SEGS, 64, QU), BF16),
            pltpu.VMEM((SEGS, 1, 128), jnp.int32),
            pltpu.VMEM((ROWS, BATCH * 64), BF16),
            pltpu.VMEM((ROWS, QU), F32),
            pltpu.VMEM((DETS, QV, 2, HALF), BF16),
            pltpu.VMEM((STEPS, V, U), BF16),
            pltpu.VMEM((PIECE, U), BF16),
            pltpu.VMEM((DETS, DETECTORS, SHARE, 2 * QU), BF16),
            pltpu.VMEM((DETS, DETECTORS, SHARE, 2 * QU), BF16),
            pltpu.VMEM((2, DETECTORS * SHARE, U), F32),
            pltpu.VMEM((DETS, QV, U), BF16),
            pltpu.VMEM((DETECTORS, SHARE, HALF), F32),
            pltpu.VMEM((DETECTORS, SHARE + 8, HALF), F32),
            pltpu.VMEM((V, V), BF16),
            pltpu.VMEM((2, V // 2, QU), F32),
            pltpu.VMEM((2, DETS, 2 * QU, U), BF16),
            pltpu.VMEM((U, 2 * U), BF16),
            pltpu.VMEM((DETS, 2, QV, U), F32),
            pltpu.VMEM((STEPS * QV, U), BF16),
            pltpu.VMEM((STEPS, 2, DETS, QV, U), BF16),
            dma((SEGS,)), dma((SEGS,)), dma((SEGS,)), dma((SEGS,)),
            dma((DETS,)), dma((DETS,)),
            dma((DETS, DETECTORS)), dma((DETS, DETECTORS)),
            dma((4, PARTS)), dma((DETS, PARTS)), dma((DETS,)),
            dma((3,)), dma((2,)), dma((PIECES,)), dma((1,)), dma((2,)), dma((2,)), dma((5,)), dma((5,)),
        ],
        compiler_params=pltpu.CompilerParams(
            vmem_limit_bytes=LIMIT, collective_id=0, has_side_effects=True
        ),
        cost_estimate=pl.CostEstimate(
            flops=12_000_000_000, bytes_accessed=16_000_000, transcendentals=0
        ),
        name="filtered",
    )(*operands)


COLUMNS = 512


def last_kernel(partial_ref, last_ref, out_ref):
    made = jnp.dot(last_ref[...], partial_ref[0], preferred_element_type=F32)
    out_ref[0, 0, 0] = made.astype(BF16).reshape(V // 2, 2, COLUMNS)


def last_rows(partials, last):
    return pl.pallas_call(
        last_kernel,
        grid=(STEPS, U // COLUMNS),
        out_shape=jax.ShapeDtypeStruct((1, 1, STEPS, V // 2, 2, U), BF16),
        in_specs=[
            pl.BlockSpec((1, 2 * V, COLUMNS), lambda r, c: (r, 0, c)),
            pl.BlockSpec((V, 2 * V), lambda r, c: (0, 0)),
        ],
        out_specs=pl.BlockSpec((1, 1, 1, V // 2, 2, COLUMNS), lambda r, c: (0, 0, r, 0, 0, c)),
        compiler_params=pltpu.CompilerParams(vmem_limit_bytes=LIMIT),
        name="last_rows",
    )(partials, last)


def body(strain, row_target, gate_start, gate_width, inverse_psd, templates, template_shift):
    row, twist, edge, col, back, untwist, last = (jnp.asarray(t) for t in tables())
    partials = filtered(
        gate_start,
        gate_width,
        template_shift,
        row_target,
        edge,
        templates,
        strain,
        inverse_psd,
        row,
        twist,
        col,
        back,
        untwist,
    )
    return last_rows(partials.reshape(STEPS, 2 * V, U), last)


def solution(mesh):
    in_specs = (
        P("seg", "det"),
        P("seg"),
        P("seg", None),
        P("seg", None),
        P(None, "det", None),
        P("seg", "det", None, None),
        P("seg"),
    )
    out_specs = P("seg", "det", None, None, None, None)
    return jax.shard_map(body, mesh=mesh, in_specs=in_specs, out_specs=out_specs, check_vma=False)
```

```python
import functools
import math

import jax
import jax.numpy as jnp
import numpy as np
from jax import lax
from jax.experimental import pallas as pl
from jax.experimental.pallas import tpu as pltpu
from jax.sharding import PartitionSpec as P

V = 512
U = 1024
DETECTORS = 3
BLOCK = 4
STEPS = 3
SAMPLES = 524288
SEGS = 64
DETS = 4
SLOTS = 3072
CAP = 48
QU = U // DETS
QV = V // DETS
ROWS = DETECTORS * V
HALF = U // 2
SHARE = V // 8
PLACES = (0, 2, 3, 1)
MIRROR = 32
MESH = pl.DeviceIdType.MESH
F32 = jnp.float32
BF16 = jnp.bfloat16
LIMIT = 60 * 1024 * 1024
VM = pl.BlockSpec(memory_space=pltpu.VMEM)
SM = pl.BlockSpec(memory_space=pltpu.SMEM)
HB = pl.BlockSpec(memory_space=pl.ANY)


def angles(rows, cols, modulus, direction):
    residue = (rows[:, None].astype(np.int64) * cols[None, :]) % modulus
    angle = np.float32(direction * 2.0 * math.pi / modulus) * residue.astype(np.float32)
    return np.cos(angle), np.sin(angle)


@functools.cache
def tables():
    v, u, m = np.arange(V), np.arange(U), np.arange(HALF)
    bf = np.dtype(jnp.bfloat16)
    c, s = angles(v[: V // 2], v, V, -1.0)
    s[0] = np.where(v % 2 == 0, 1.0, -1.0)
    row = (np.concatenate([c, s], 0) / math.sqrt(V)).astype(bf)
    twist = np.stack([*angles(v[: V // 2], u, SAMPLES, -1.0)])
    twist = twist.reshape(2, V // 2, DETS, QU).transpose(2, 0, 1, 3).astype(np.float32)
    edge = np.stack([*angles(v[V // 2 : V // 2 + 1], u, SAMPLES, -1.0)])
    edge = edge.reshape(2, 1, DETS, QU).transpose(2, 1, 0, 3).reshape(DETS, 1, 2 * QU)
    edge = np.tile(edge, (1, 8, 1)).astype(np.float32)

    def by_source(real_rows, imag_rows):
        both = np.stack([real_rows, imag_rows]) / math.sqrt(U)
        both = both.reshape(2, DETS, QU, U).transpose(1, 0, 2, 3)
        return both.reshape(DETS, 2 * QU, U).astype(bf)

    c, s = angles(u, m, U, -1.0)
    direct = by_source(np.concatenate([c, s], 1), np.concatenate([-s, c], 1))
    c, s = angles(u, m + 1, U, -1.0)
    mirrored = by_source(np.concatenate([c, s], 1), np.concatenate([s, -c], 1))
    col = np.stack([direct, mirrored])
    order = np.concatenate(
        [
            np.concatenate([p * SHARE + half, V - p * SHARE - half[::-1]])
            for p, half in ((p, np.arange(SHARE)) for p in PLACES)
        ]
    )
    order[QV - 1] = V // 2
    c, s = angles(m, u, U, 1.0)
    back = np.concatenate([np.concatenate([c, s], 1), np.concatenate([-s, c], 1)], 0)
    back = (back / math.sqrt(U)).astype(bf)
    untwist = np.stack([*angles(order, u, SAMPLES, 1.0)]).astype(np.float32)
    untwist = untwist.reshape(2, DETS, QV, U).transpose(1, 0, 2, 3)
    c, s = angles(np.arange(V // 4, 3 * V // 4), order, V, 1.0)
    last = np.stack([np.concatenate([c, -s], 1), np.concatenate([s, c], 1)], 1)
    last = (last / math.sqrt(V)).reshape(V, 2 * V).astype(bf)
    return row, twist, edge, col, back, untwist, last


GROUP = 16
BATCH = 8
LANES = 256
HOME = SEGS // 2
COUNT = SLOTS // LANES


def sort_ranks(me, target_ref, dest, ids):
    lane = lax.broadcasted_iota(jnp.int32, (LANES, LANES), 1)
    sub = lax.broadcasted_iota(jnp.int32, (LANES, LANES), 0)
    upper = jnp.where(sub <= lane, 1.0, 0.0).astype(BF16)
    seg = lax.broadcasted_iota(jnp.int32, (SEGS, LANES), 0)
    carry = jnp.zeros((SEGS, 1), F32)
    high = jnp.zeros((SEGS, SEGS), F32)
    low = jnp.zeros((SEGS, SEGS), F32)
    spread = (((1,), (1,)), ((), ()))
    for b in range(COUNT):
        t = target_ref[b * LANES : (b + 1) * LANES].reshape(1, LANES)
        owner = ((t >> 9) * 43691) >> 17
        local = t - owner * ROWS
        flips = ((owner >> 5) + me // HOME) & 1
        slot = ((owner + SEGS - me) & (HOME - 1)) + HOME - HOME * flips
        owner = jnp.where(t >= 0, slot, SEGS)
        mine = jnp.where(seg == owner, 1.0, 0.0)
        before = jnp.dot(mine.astype(BF16), upper, preferred_element_type=F32)
        rank = jnp.sum(mine * (before + carry), axis=0, keepdims=True).astype(jnp.int32) - 1
        carry = carry + jnp.sum(mine, axis=1, keepdims=True)
        dest[b : b + 1, :] = jnp.where(t >= 0, owner * CAP + rank, -1)
        order = jnp.where(seg == rank, 1.0, 0.0).astype(BF16)
        upper_part = (mine * ((local >> 6) + 1).astype(F32)).astype(BF16)
        lower_part = (mine * (local & 63).astype(F32)).astype(BF16)
        high = high + lax.dot_general(upper_part, order, spread, preferred_element_type=F32)
        low = low + lax.dot_general(lower_part, order, spread, preferred_element_type=F32)
    found = jnp.where(high > 0.5, high * 64.0 + low - 63.0, 0.0).astype(jnp.int32)
    found = jnp.concatenate([found, found], axis=1)
    side = lax.broadcasted_iota(jnp.int32, (SEGS, 128), 1) // 64
    parity = lax.broadcasted_iota(jnp.int32, (SEGS, 128), 0) & 1
    found = jnp.where(side == parity, found, 0)
    for o in range(SEGS):
        ids[o] = found[o : o + 1]


def shift_bank(shift, raw, bank):
    at = lax.broadcasted_iota(jnp.int32, (V, 128), 0)
    block, inner = at // QV, at % QV
    base = jnp.where(block == 0, 0, jnp.where(block == 3, SHARE, block * SHARE + SHARE))
    k = jnp.where(inner < SHARE, base + inner, V - base - (QV - 1) + inner)
    k = jnp.where(at == QV - 1, V // 2, k)
    lane = lax.broadcasted_iota(jnp.int32, (V, 2 * V), 1)
    pairs = raw[...].reshape(2 * V, HALF)
    parts = []
    for part in range(2):
        pick = jnp.where(lane == 2 * k[:, :1] + part, 1.0, 0.0).astype(BF16)
        parts.append(jnp.dot(pick, pairs, preferred_element_type=F32))
    real, imag = parts
    m = lax.broadcasted_iota(jnp.int32, (8, HALF), 1)
    angle = (-2.0 * math.pi / SAMPLES) * ((k * shift) % SAMPLES).astype(F32)
    row_cos, row_sin = jnp.cos(angle)[:, :1], jnp.sin(angle)[:, :1]
    angle = (-2.0 * math.pi / U) * ((m * shift) % U).astype(F32)
    col_cos, col_sin = jnp.cos(angle)[:1], jnp.sin(angle)[:1]
    cosine = row_cos * col_cos - row_sin * col_sin
    sine = row_cos * col_sin + row_sin * col_cos
    bank[0, :, :HALF] = (real * cosine - imag * sine).astype(BF16)
    bank[0, :, HALF:] = (real * sine + imag * cosine).astype(BF16)


PIECES = 16
PART = 32
PARTS = QV // PART
PIECE = V // PIECES


def filter_kernel(
    start_ref, width_ref, shift_ref, target_ref, edge_ref, bank_ref, strain_hbm, psd_hbm,
    row_hbm, twist_hbm, col_hbm, back_hbm, untwist_hbm,
    out_hbm,
    strain, held, dest, rows, ids, arrived, arrived_ids, chosen, total, raw, bank, relay,
    turned, crossed, spec, coherent, psd_low, psd_high, row, twist, col,
    back, untwist, products, partials,
    row_send, row_recv, id_send, id_recv, bank_send, bank_recv, turn_send, turn_recv,
    coh_send, coh_recv, out_sem, pass_send, pass_recv, piece_send, relay_recv, psd_send, psd_recv, table_sem, own_sem,
):
    me = lax.axis_index("seg")
    det = lax.axis_index("det")
    core = me % 2
    place = (me % 32) // 2
    barrier = pltpu.get_barrier_semaphore()
    own_strain = pltpu.make_async_copy(strain_hbm, strain, own_sem.at[3])
    own_strain.start()

    def greet(o, _):
        pl.semaphore_signal(
            barrier, inc=1, device_id={"seg": (me + o) % SEGS}, device_id_type=MESH
        )
        return 0

    lax.fori_loop(1, SEGS, greet, 0)
    for o in range(1, DETS):
        pl.semaphore_signal(
            barrier, inc=1, device_id={"det": (det + o) % DETS}, device_id_type=MESH
        )
    across = {"seg": (me + MIRROR) % SEGS, "det": DETS - 1 - det}
    pl.semaphore_signal(barrier, inc=1, device_id=across, device_id_type=MESH)
    fetches = [
        pltpu.make_async_copy(source, held_at, table_sem.at[i])
        for i, (source, held_at) in enumerate(
            (
                (row_hbm, row),
                (twist_hbm.at[det], twist),
                (col_hbm, col),
                (back_hbm, back),
                (untwist_hbm, untwist),
            )
        )
    ]
    own_bank = pltpu.make_async_copy(bank_ref.at[det], raw.at[det], own_sem.at[0])
    own_bank.start()
    pl.semaphore_wait(barrier, SEGS + DETS - 1)

    def bank_copy(o):
        other = (det + o) % DETS
        return pltpu.make_async_remote_copy(
            src_ref=bank_ref.at[other],
            dst_ref=raw.at[det],
            send_sem=bank_send.at[o],
            recv_sem=bank_recv.at[o],
            device_id={"det": other},
            device_id_type=MESH,
        )

    for o in (2, 1, 3):
        bank_copy(o).start()

    upper_det = det >= DETS // 2

    def psd_copy(target, lane):
        return pltpu.make_async_remote_copy(
            src_ref=psd_hbm.at[:, pl.ds(SHARE, SHARE)],
            dst_ref=target,
            send_sem=psd_send.at[0],
            recv_sem=psd_recv.at[lane],
            device_id=across,
            device_id_type=MESH,
        )

    to_low = psd_copy(psd_low, 0)
    to_high = psd_copy(psd_high.at[:, pl.ds(0, SHARE)], 0)
    to_rest = pltpu.make_async_remote_copy(
        src_ref=psd_hbm.at[:, pl.ds(0, 8)],
        dst_ref=psd_high.at[:, pl.ds(SHARE, 8)],
        send_sem=psd_send.at[1],
        recv_sem=psd_recv.at[1],
        device_id={"det": (det + 2) % DETS},
        device_id_type=MESH,
    )
    keep_low = pltpu.make_async_copy(psd_hbm.at[:, pl.ds(0, SHARE)], psd_low, own_sem.at[4])
    keep_high = pltpu.make_async_copy(psd_hbm.at[:, pl.ds(0, SHARE + 8)], psd_high, own_sem.at[4])

    @pl.when(upper_det)
    def _():
        to_high.start()
        to_rest.start()
        keep_high.start()

    @pl.when(jnp.logical_not(upper_det))
    def _():
        to_low.start()
        keep_low.start()

    def partner(o):
        return (me // HOME + 1 + o // HOME) % 2 * HOME + (me % HOME + o) % HOME

    def row_copy(o):
        return pltpu.make_async_remote_copy(
            src_ref=rows.at[pl.ds(o * CAP, CAP)],
            dst_ref=arrived.at[o, pl.ds(0, CAP)],
            send_sem=row_send.at[o],
            recv_sem=row_recv.at[o],
            device_id={"seg": partner(o)},
            device_id_type=MESH,
        )

    def id_copy(o):
        return pltpu.make_async_remote_copy(
            src_ref=ids.at[o],
            dst_ref=arrived_ids.at[o],
            send_sem=id_send.at[o],
            recv_sem=id_recv.at[o],
            device_id={"seg": partner(o)},
            device_id_type=MESH,
        )

    for fetch in fetches:
        fetch.start()
    own_strain.wait()
    held[...] = strain[...].astype(BF16)
    sort_ranks(me, target_ref, dest, ids)
    step = GROUP * CAP

    def send(o, _):
        id_copy(o).start()
        row_copy(o).start()
        return 0

    for g in range(SEGS // GROUP):
        want = lax.broadcasted_iota(jnp.int32, (step, LANES), 0) + g * step
        picks = [
            jnp.where(want == dest[b : b + 1, :], 1.0, 0.0).astype(BF16) for b in range(COUNT)
        ]
        picked = jnp.dot(jnp.concatenate(picks, axis=1), held[...], preferred_element_type=F32)
        rows[g * step : (g + 1) * step] = picked.astype(BF16)
        lax.fori_loop(g * GROUP + (g * GROUP == HOME), (g + 1) * GROUP, send, 0)
    own_rows = pltpu.make_async_copy(
        rows.at[pl.ds(HOME * CAP, CAP)], arrived.at[HOME, pl.ds(0, CAP)], own_sem.at[1]
    )
    own_rows.start()
    own_ids = pltpu.make_async_copy(ids.at[HOME], arrived_ids.at[HOME], own_sem.at[2])
    own_ids.start()
    arrived[:, CAP:, :] = jnp.zeros((SEGS, 64 - CAP, QU), BF16)

    own_bank.wait()
    for o in range(1, DETS):
        bank_copy(o).wait_recv()
    shift_bank(shift_ref[det], raw, bank)

    def whole_pass(source, target, lane, back):
        return pltpu.make_async_remote_copy(
            src_ref=source,
            dst_ref=target,
            send_sem=pass_send.at[lane],
            recv_sem=pass_recv.at[lane],
            device_id={"seg": (me + SEGS - back) % SEGS},
            device_id_type=MESH,
        )

    hot = (me % 32) < 2
    odd = core == 1
    to_next = whole_pass(bank.at[0], bank.at[1], 0, 1)
    to_after = whole_pass(bank.at[0], bank.at[2], 1, 2)
    onward = pltpu.make_async_remote_copy(
        src_ref=bank.at[1],
        dst_ref=bank.at[2],
        send_sem=pass_send.at[2],
        recv_sem=pass_recv.at[1],
        device_id={"seg": (me + SEGS - 1) % SEGS},
        device_id_type=MESH,
    )
    corner = (me // 32) * 32
    far = (corner + SEGS - 1) % SEGS

    def piece_copy(i):
        return pltpu.make_async_remote_copy(
            src_ref=bank.at[0, pl.ds(i * PIECE, PIECE)],
            dst_ref=relay,
            send_sem=piece_send.at[i],
            recv_sem=relay_recv.at[0],
            device_id={"seg": corner + 2 * i + core},
            device_id_type=MESH,
        )

    def last_hop(source, lane, at):
        return pltpu.make_async_remote_copy(
            src_ref=source,
            dst_ref=bank.at[1 + lane, pl.ds(at * PIECE, PIECE)],
            send_sem=piece_send.at[0],
            recv_sem=pass_recv.at[lane],
            device_id={"seg": far},
            device_id_type=MESH,
        )

    def pieces(i, _):
        piece_copy(i).start()
        return 0

    def pieces_sent(i, _):
        piece_copy(i).wait_send()
        return 0

    @pl.when(jnp.logical_or(odd, jnp.logical_not(hot)))
    def _():
        to_next.start()

    @pl.when(jnp.logical_and(odd, jnp.logical_not(hot)))
    def _():
        to_after.start()

    @pl.when(hot)
    def _():
        lax.fori_loop(1, PIECES, pieces, 0)

    @pl.when(jnp.logical_and(hot, odd))
    def _():
        last_hop(bank.at[0, pl.ds(0, PIECE)], 1, 0).start()

    @pl.when(jnp.logical_and(hot, jnp.logical_not(odd)))
    def _():
        last_hop(bank.at[0, pl.ds(0, PIECE)], 0, 0).start()

    own_rows.wait()
    own_ids.wait()

    def receive(o, _):
        id_copy(o).wait_recv()
        row_copy(o).wait_recv()
        return 0

    wide = BATCH * 64
    groups = SEGS // BATCH
    for g in (*range(groups // 2, groups), *range(groups // 2)):
        lax.fori_loop(g * BATCH + (g * BATCH == HOME), (g + 1) * BATCH, receive, 0)
        for p in range(BATCH // 2):
            o = g * BATCH + 2 * p
            ident = arrived_ids[o] + arrived_ids[o + 1] - 1
            chosen[:, p * 128 : (p + 1) * 128] = jnp.where(
                lax.broadcasted_iota(jnp.int32, (ROWS, 128), 0) == ident, 1.0, 0.0
            ).astype(BF16)
        block = arrived[g * BATCH : (g + 1) * BATCH].reshape(wide, QU)
        part = jnp.dot(chosen[...], block, preferred_element_type=F32)
        if g == groups // 2:
            total[...] = part
        else:
            total[...] += part

    def turn_copy(o, d):
        other = (det + o) % DETS
        return pltpu.make_async_remote_copy(
            src_ref=turned.at[other, d],
            dst_ref=crossed.at[o, d],
            send_sem=turn_send.at[o, d],
            recv_sem=turn_recv.at[o, d],
            device_id={"det": other},
            device_id_type=MESH,
        )

    sample = lax.broadcasted_iota(jnp.int32, (V, QU), 0) * U
    sample = sample + lax.broadcasted_iota(jnp.int32, (V, QU), 1) + det * QU
    for fetch in fetches[:3]:
        fetch.wait()
    for d in range(DETECTORS):
        begin = start_ref[0, d]
        end = begin + width_ref[0, d]
        inside = (sample >= begin) & (sample < end)
        gated = jnp.where(inside, 0.0, total[d * V : (d + 1) * V]).astype(BF16)
        folded = jnp.dot(row[...], gated, preferred_element_type=F32)
        real, imag = folded[: V // 2], folded[V // 2 :]
        cosine, sine = twist[0], twist[1]
        first = (real * cosine - imag * sine).astype(BF16)
        second = (real * sine + imag * cosine).astype(BF16)
        for q in range(DETS):
            at = PLACES[q] * SHARE
            turned[q, d, :, :QU] = first[at : at + SHARE]
            turned[q, d, :, QU:] = second[at : at + SHARE]
        for o in (2, 1, 3):
            turn_copy(o, d).start()

    @pl.when(jnp.logical_not(hot))
    def _():
        piece_copy(1).wait_recv()

    @pl.when(jnp.logical_and(jnp.logical_not(hot), odd))
    def _():
        last_hop(relay, 1, place).start()

    @pl.when(jnp.logical_and(jnp.logical_not(hot), jnp.logical_not(odd)))
    def _():
        last_hop(relay, 0, place).start()

    near = det + 1 - 2 * (det % 2)
    entry = DETS // 2 - det // 2
    beyond = DETS - 1 - det // 2 * (DETS - 1)
    middle = jnp.logical_or(det == 1, det == 2)

    def coherent_copy(block, other, lane, part):
        rows_of = pl.ds(part * PART, PART)
        return pltpu.make_async_remote_copy(
            src_ref=coherent.at[block, rows_of],
            dst_ref=coherent.at[block, rows_of],
            send_sem=coh_send.at[lane, part],
            recv_sem=coh_recv.at[block, part],
            device_id={"det": other},
            device_id_type=MESH,
        )

    def gather_rows(which, scale, shift, first_row):
        for half in range(2):
            cols = slice(half * HALF, (half + 1) * HALF)
            value = 0.0
            for d in range(DETECTORS):
                held_rows = spec[which, d * SHARE : (d + 1) * SHARE, cols]
                value = value + scale[d, shift : shift + SHARE] * held_rows
            coherent[det, first_row : first_row + SHARE, cols] = value.astype(BF16)
        for part in range(first_row // PART, (first_row + SHARE) // PART):
            coherent_copy(det, entry, 0, part).start()
            coherent_copy(det, near, 1, part).start()

    high = DETECTORS * SHARE
    row_at = lax.broadcasted_iota(jnp.int32, (high, high), 0)
    col_at = lax.broadcasted_iota(jnp.int32, (high, high), 1)
    flip = (row_at // SHARE == col_at // SHARE) & (row_at % SHARE + col_at % SHARE == SHARE - 1)
    flip = jnp.where(flip, 1.0, 0.0).astype(BF16)
    packed = lax.broadcasted_iota(jnp.int32, (high, 2 * QU), 0) % SHARE + det == 0
    imag_side = lax.broadcasted_iota(jnp.int32, (high, 2 * QU), 1) >= QU
    for o in (0, 1, 3, 2):
        source = (det + DETS - o) % DETS
        if o == 0:
            came = turned[det]
        else:
            for d in range(DETECTORS):
                turn_copy(o, d).wait_recv()
            came = crossed[o]
        came = came.reshape(high, 2 * QU)
        wide_came = came.astype(F32)
        direct = jnp.where(packed & imag_side, 0.0, wide_came).astype(BF16)
        twin = wide_came[:, QU:]
        twin = jnp.concatenate([twin, twin], axis=1) * edge_ref[source][:1]
        mirrored = jnp.where(packed, twin, wide_came).astype(BF16)
        mirrored = jnp.dot(flip, mirrored, preferred_element_type=F32).astype(BF16)
        if o == 2:

            @pl.when(upper_det)
            def _():
                to_low.wait_recv()
                keep_high.wait()

            @pl.when(jnp.logical_not(upper_det))
            def _():
                to_high.wait_recv()
                to_rest.wait_recv()
                keep_low.wait()

        part = jnp.dot(direct, col[0, source], preferred_element_type=F32)
        if o == 0:
            spec[0] = part
        else:
            spec[0] += part
        if o == 2:
            gather_rows(0, psd_low, 0, 0)
        other = jnp.dot(mirrored, col[1, source], preferred_element_type=F32)
        if o == 0:
            spec[1] = other
        else:
            spec[1] += other
    gather_rows(1, psd_high, 1, SHARE)
    to_next.wait_recv()

    @pl.when(odd)
    def _():
        onward.start()

    for fetch in fetches[3:]:
        fetch.wait()

    def multiply(block, r):
        real = coherent[block, :, :HALF].astype(F32)
        imag = coherent[block, :, HALF:].astype(F32)
        at = pl.ds(pl.multiple_of(block * QV, QV), QV)
        other_real = bank[r, at, :HALF].astype(F32)
        other_imag = bank[r, at, HALF:].astype(F32)
        into = slice(r * QV, (r + 1) * QV)
        products[into, :HALF] = (real * other_real + imag * other_imag).astype(BF16)
        products[into, HALF:] = (imag * other_real - real * other_imag).astype(BF16)

    def leave(block):
        return pltpu.make_async_copy(
            partials.at[:, :, block], out_hbm.at[:, :, block], out_sem.at[block]
        )

    def invert(block):
        for r in range(STEPS):
            multiply(block, r)
        for half in range(2):
            lanes = slice(half * HALF, (half + 1) * HALF)
            upper = slice(U + half * HALF, U + (half + 1) * HALF)
            first = jnp.dot(products[...], back[:, lanes], preferred_element_type=F32)
            second = jnp.dot(products[...], back[:, upper], preferred_element_type=F32)
            cosine, sine = untwist[block, 0, :, lanes], untwist[block, 1, :, lanes]
            for r in range(STEPS):
                real, imag = first[r * QV : (r + 1) * QV], second[r * QV : (r + 1) * QV]
                partials[r, 0, block, :, lanes] = (real * cosine - imag * sine).astype(BF16)
                partials[r, 1, block, :, lanes] = (real * sine + imag * cosine).astype(BF16)
        leave(block).start()

    def arrive(block):
        for part in range(PARTS):
            coherent_copy(block, det, 0, part).wait_recv()

    to_after.wait_recv()
    invert(det)

    @pl.when(middle)
    def _():
        for part in range(PARTS):
            coherent_copy(entry, det, 0, part).wait_recv()
            coherent_copy(entry, near, 2, part).start()
            coherent_copy(beyond, det, 0, part).wait_recv()
            coherent_copy(beyond, near, 3, part).start()

    arrive(near)
    invert(near)

    @pl.when(jnp.logical_not(middle))
    def _():
        arrive(entry)

    invert(entry)

    @pl.when(jnp.logical_not(middle))
    def _():
        arrive(beyond)

    invert(beyond)

    @pl.when(upper_det)
    def _():
        to_high.wait_send()
        to_rest.wait_send()

    @pl.when(jnp.logical_not(upper_det))
    def _():
        to_low.wait_send()

    @pl.when(jnp.logical_or(odd, jnp.logical_not(hot)))
    def _():
        to_next.wait_send()

    @pl.when(jnp.logical_and(odd, jnp.logical_not(hot)))
    def _():
        to_after.wait_send()

    @pl.when(hot)
    def _():
        lax.fori_loop(1, PIECES, pieces_sent, 0)

    last_hop(relay, 0, place).wait_send()

    @pl.when(odd)
    def _():
        onward.wait_send()

    def sent(o, _):
        id_copy(o).wait_send()
        row_copy(o).wait_send()
        return 0

    lax.fori_loop(0, HOME, sent, 0)
    lax.fori_loop(HOME + 1, SEGS, sent, 0)
    for o in range(1, DETS):
        bank_copy(o).wait_send()
        for d in range(DETECTORS):
            turn_copy(o, d).wait_send()
    for part in range(PARTS):
        coherent_copy(det, entry, 0, part).wait_send()
        coherent_copy(det, near, 1, part).wait_send()

    @pl.when(middle)
    def _():
        for part in range(PARTS):
            coherent_copy(entry, near, 2, part).wait_send()
            coherent_copy(beyond, near, 3, part).wait_send()

    for block in range(DETS):
        leave(block).wait()


def filtered(*operands):
    dma = pltpu.SemaphoreType.DMA
    return pl.pallas_call(
        filter_kernel,
        out_shape=jax.ShapeDtypeStruct((STEPS, 2, DETS, QV, U), BF16),
        in_specs=[SM, SM, SM, VM, VM] + [HB] * 8,
        out_specs=HB,
        scratch_shapes=[
            pltpu.VMEM((SLOTS, QU), F32),
            pltpu.VMEM((SLOTS, QU), BF16),
            pltpu.VMEM((16, LANES), jnp.int32),
            pltpu.VMEM((SLOTS, QU), BF16),
            pltpu.VMEM((SEGS, 1, 128), jnp.int32),
            pltpu.VMEM((SEGS, 64, QU), BF16),
            pltpu.VMEM((SEGS, 1, 128), jnp.int32),
            pltpu.VMEM((ROWS, BATCH * 64), BF16),
            pltpu.VMEM((ROWS, QU), F32),
            pltpu.VMEM((DETS, QV, 2, HALF), BF16),
            pltpu.VMEM((STEPS, V, U), BF16),
            pltpu.VMEM((PIECE, U), BF16),
            pltpu.VMEM((DETS, DETECTORS, SHARE, 2 * QU), BF16),
            pltpu.VMEM((DETS, DETECTORS, SHARE, 2 * QU), BF16),
            pltpu.VMEM((2, DETECTORS * SHARE, U), F32),
            pltpu.VMEM((DETS, QV, U), BF16),
            pltpu.VMEM((DETECTORS, SHARE, HALF), F32),
            pltpu.VMEM((DETECTORS, SHARE + 8, HALF), F32),
            pltpu.VMEM((V, V), BF16),
            pltpu.VMEM((2, V // 2, QU), F32),
            pltpu.VMEM((2, DETS, 2 * QU, U), BF16),
            pltpu.VMEM((U, 2 * U), BF16),
            pltpu.VMEM((DETS, 2, QV, U), F32),
            pltpu.VMEM((STEPS * QV, U), BF16),
            pltpu.VMEM((STEPS, 2, DETS, QV, U), BF16),
            dma((SEGS,)), dma((SEGS,)), dma((SEGS,)), dma((SEGS,)),
            dma((DETS,)), dma((DETS,)),
            dma((DETS, DETECTORS)), dma((DETS, DETECTORS)),
            dma((4, PARTS)), dma((DETS, PARTS)), dma((DETS,)),
            dma((3,)), dma((2,)), dma((PIECES,)), dma((1,)), dma((2,)), dma((2,)), dma((5,)), dma((5,)),
        ],
        compiler_params=pltpu.CompilerParams(
            vmem_limit_bytes=LIMIT, collective_id=0, has_side_effects=True
        ),
        cost_estimate=pl.CostEstimate(
            flops=12_000_000_000, bytes_accessed=16_000_000, transcendentals=0
        ),
        name="filtered",
    )(*operands)


COLUMNS = 512


def last_kernel(partial_ref, last_ref, out_ref):
    made = jnp.dot(last_ref[...], partial_ref[0], preferred_element_type=F32)
    out_ref[0, 0, 0] = made.astype(BF16).reshape(V // 2, 2, COLUMNS)


def last_rows(partials, last):
    return pl.pallas_call(
        last_kernel,
        grid=(STEPS, U // COLUMNS),
        out_shape=jax.ShapeDtypeStruct((1, 1, STEPS, V // 2, 2, U), BF16),
        in_specs=[
            pl.BlockSpec((1, 2 * V, COLUMNS), lambda r, c: (r, 0, c)),
            pl.BlockSpec((V, 2 * V), lambda r, c: (0, 0)),
        ],
        out_specs=pl.BlockSpec((1, 1, 1, V // 2, 2, COLUMNS), lambda r, c: (0, 0, r, 0, 0, c)),
        compiler_params=pltpu.CompilerParams(vmem_limit_bytes=LIMIT),
        name="last_rows",
    )(partials, last)


def body(strain, row_target, gate_start, gate_width, inverse_psd, templates, template_shift):
    row, twist, edge, col, back, untwist, last = (jnp.asarray(t) for t in tables())
    partials = filtered(
        gate_start,
        gate_width,
        template_shift,
        row_target,
        edge,
        templates,
        strain,
        inverse_psd,
        row,
        twist,
        col,
        back,
        untwist,
    )
    return last_rows(partials.reshape(STEPS, 2 * V, U), last)


def solution(mesh):
    in_specs = (
        P("seg", "det"),
        P("seg"),
        P("seg", None),
        P("seg", None),
        P(None, "det", None),
        P("seg", "det", None, None),
        P("seg"),
    )
    out_specs = P("seg", "det", None, None, None, None)
    return jax.shard_map(body, mesh=mesh, in_specs=in_specs, out_specs=out_specs, check_vma=False)
```

```python
import functools
import math

import jax
import jax.numpy as jnp
import numpy as np
from jax import lax
from jax.experimental import pallas as pl
from jax.experimental.pallas import tpu as pltpu
from jax.sharding import PartitionSpec as P

V = 512
U = 1024
DETECTORS = 3
BLOCK = 4
STEPS = 3
SAMPLES = 524288
SEGS = 64
DETS = 4
SLOTS = 3072
CAP = 48
QU = U // DETS
QV = V // DETS
ROWS = DETECTORS * V
HALF = U // 2
SHARE = V // 8
PLACES = (0, 2, 3, 1)
MIRROR = 32
MESH = pl.DeviceIdType.MESH
F32 = jnp.float32
BF16 = jnp.bfloat16
LIMIT = 60 * 1024 * 1024
VM = pl.BlockSpec(memory_space=pltpu.VMEM)
SM = pl.BlockSpec(memory_space=pltpu.SMEM)
HB = pl.BlockSpec(memory_space=pl.ANY)


def angles(rows, cols, modulus, direction):
    residue = (rows[:, None].astype(np.int64) * cols[None, :]) % modulus
    angle = np.float32(direction * 2.0 * math.pi / modulus) * residue.astype(np.float32)
    return np.cos(angle), np.sin(angle)


@functools.cache
def tables():
    v, u, m = np.arange(V), np.arange(U), np.arange(HALF)
    bf = np.dtype(jnp.bfloat16)
    c, s = angles(v[: V // 2], v, V, -1.0)
    s[0] = np.where(v % 2 == 0, 1.0, -1.0)
    row = (np.concatenate([c, s], 0) / math.sqrt(V)).astype(bf)
    twist = np.stack([*angles(v[: V // 2], u, SAMPLES, -1.0)])
    twist = twist.reshape(2, V // 2, DETS, QU).transpose(2, 0, 1, 3).astype(np.float32)
    edge = np.stack([*angles(v[V // 2 : V // 2 + 1], u, SAMPLES, -1.0)])
    edge = edge.reshape(2, 1, DETS, QU).transpose(2, 1, 0, 3).reshape(DETS, 1, 2 * QU)
    edge = np.tile(edge, (1, 8, 1)).astype(np.float32)

    def by_source(real_rows, imag_rows):
        both = np.stack([real_rows, imag_rows]) / math.sqrt(U)
        both = both.reshape(2, DETS, QU, U).transpose(1, 0, 2, 3)
        return both.reshape(DETS, 2 * QU, U).astype(bf)

    c, s = angles(u, m, U, -1.0)
    direct = by_source(np.concatenate([c, s], 1), np.concatenate([-s, c], 1))
    c, s = angles(u, m + 1, U, -1.0)
    mirrored = by_source(np.concatenate([c, s], 1), np.concatenate([s, -c], 1))
    col = np.stack([direct, mirrored])
    order = np.concatenate(
        [
            np.concatenate([p * SHARE + half, V - p * SHARE - half[::-1]])
            for p, half in ((p, np.arange(SHARE)) for p in PLACES)
        ]
    )
    order[QV - 1] = V // 2
    c, s = angles(m, u, U, 1.0)
    back = np.concatenate([np.concatenate([c, s], 1), np.concatenate([-s, c], 1)], 0)
    back = (back / math.sqrt(U)).astype(bf)
    untwist = np.stack([*angles(order, u, SAMPLES, 1.0)]).astype(np.float32)
    untwist = untwist.reshape(2, DETS, QV, U).transpose(1, 0, 2, 3)
    c, s = angles(np.arange(V // 4, 3 * V // 4), order, V, 1.0)
    last = np.stack([np.concatenate([c, -s], 1), np.concatenate([s, c], 1)], 1)
    last = (last / math.sqrt(V)).reshape(V, 2 * V).astype(bf)
    return row, twist, edge, col, back, untwist, last


GROUP = 16
BATCH = 8
LANES = 256
HOME = SEGS // 2
COUNT = SLOTS // LANES


def sort_ranks(me, target_ref, dest, ids):
    lane = lax.broadcasted_iota(jnp.int32, (LANES, LANES), 1)
    sub = lax.broadcasted_iota(jnp.int32, (LANES, LANES), 0)
    upper = jnp.where(sub <= lane, 1.0, 0.0).astype(BF16)
    seg = lax.broadcasted_iota(jnp.int32, (SEGS, LANES), 0)
    carry = jnp.zeros((SEGS, 1), F32)
    high = jnp.zeros((SEGS, SEGS), F32)
    low = jnp.zeros((SEGS, SEGS), F32)
    spread = (((1,), (1,)), ((), ()))
    for b in range(COUNT):
        t = target_ref[b * LANES : (b + 1) * LANES].reshape(1, LANES)
        owner = ((t >> 9) * 43691) >> 17
        local = t - owner * ROWS
        flips = ((owner >> 5) + me // HOME) & 1
        slot = ((owner + SEGS - me) & (HOME - 1)) + HOME - HOME * flips
        owner = jnp.where(t >= 0, slot, SEGS)
        mine = jnp.where(seg == owner, 1.0, 0.0)
        before = jnp.dot(mine.astype(BF16), upper, preferred_element_type=F32)
        rank = jnp.sum(mine * (before + carry), axis=0, keepdims=True).astype(jnp.int32) - 1
        carry = carry + jnp.sum(mine, axis=1, keepdims=True)
        dest[b : b + 1, :] = jnp.where(t >= 0, owner * CAP + rank, -1)
        order = jnp.where(seg == rank, 1.0, 0.0).astype(BF16)
        upper_part = (mine * ((local >> 6) + 1).astype(F32)).astype(BF16)
        lower_part = (mine * (local & 63).astype(F32)).astype(BF16)
        high = high + lax.dot_general(upper_part, order, spread, preferred_element_type=F32)
        low = low + lax.dot_general(lower_part, order, spread, preferred_element_type=F32)
    found = jnp.where(high > 0.5, high * 64.0 + low - 63.0, 0.0).astype(jnp.int32)
    found = jnp.concatenate([found, found], axis=1)
    side = lax.broadcasted_iota(jnp.int32, (SEGS, 128), 1) // 64
    parity = lax.broadcasted_iota(jnp.int32, (SEGS, 128), 0) & 1
    found = jnp.where(side == parity, found, 0)
    for o in range(SEGS):
        ids[o] = found[o : o + 1]


def shift_bank(shift, raw, bank):
    at = lax.broadcasted_iota(jnp.int32, (V, 128), 0)
    block, inner = at // QV, at % QV
    base = jnp.where(block == 0, 0, jnp.where(block == 3, SHARE, block * SHARE + SHARE))
    k = jnp.where(inner < SHARE, base + inner, V - base - (QV - 1) + inner)
    k = jnp.where(at == QV - 1, V // 2, k)
    lane = lax.broadcasted_iota(jnp.int32, (V, 2 * V), 1)
    pairs = raw[...].reshape(2 * V, HALF)
    parts = []
    for part in range(2):
        pick = jnp.where(lane == 2 * k[:, :1] + part, 1.0, 0.0).astype(BF16)
        parts.append(jnp.dot(pick, pairs, preferred_element_type=F32))
    real, imag = parts
    m = lax.broadcasted_iota(jnp.int32, (8, HALF), 1)
    angle = (-2.0 * math.pi / SAMPLES) * ((k * shift) % SAMPLES).astype(F32)
    row_cos, row_sin = jnp.cos(angle)[:, :1], jnp.sin(angle)[:, :1]
    angle = (-2.0 * math.pi / U) * ((m * shift) % U).astype(F32)
    col_cos, col_sin = jnp.cos(angle)[:1], jnp.sin(angle)[:1]
    cosine = row_cos * col_cos - row_sin * col_sin
    sine = row_cos * col_sin + row_sin * col_cos
    bank[0, :, :HALF] = (real * cosine - imag * sine).astype(BF16)
    bank[0, :, HALF:] = (real * sine + imag * cosine).astype(BF16)


PIECES = 16
PART = 32
PARTS = QV // PART
PIECE = V // PIECES


def filter_kernel(
    start_ref, width_ref, shift_ref, target_ref, edge_ref, bank_ref, strain_hbm, psd_hbm,
    row_hbm, twist_hbm, col_hbm, back_hbm, untwist_hbm,
    out_hbm,
    strain, held, dest, rows, ids, arrived, arrived_ids, chosen, total, raw, bank, relay,
    turned, crossed, spec, coherent, psd_low, psd_high, row, twist, col,
    back, untwist, products, partials,
    row_send, row_recv, id_send, id_recv, bank_send, bank_recv, turn_send, turn_recv,
    coh_send, coh_recv, out_sem, pass_send, pass_recv, piece_send, relay_recv, psd_send, psd_recv, table_sem, own_sem,
):
    me = lax.axis_index("seg")
    det = lax.axis_index("det")
    core = me % 2
    place = (me % 32) // 2
    barrier = pltpu.get_barrier_semaphore()
    own_strain = pltpu.make_async_copy(strain_hbm, strain, own_sem.at[3])
    own_strain.start()

    def greet(o, _):
        pl.semaphore_signal(
            barrier, inc=1, device_id={"seg": (me + o) % SEGS}, device_id_type=MESH
        )
        return 0

    lax.fori_loop(1, SEGS, greet, 0)
    for o in range(1, DETS):
        pl.semaphore_signal(
            barrier, inc=1, device_id={"det": (det + o) % DETS}, device_id_type=MESH
        )
    across = {"seg": (me + MIRROR) % SEGS, "det": DETS - 1 - det}
    pl.semaphore_signal(barrier, inc=1, device_id=across, device_id_type=MESH)
    fetches = [
        pltpu.make_async_copy(source, held_at, table_sem.at[i])
        for i, (source, held_at) in enumerate(
            (
                (row_hbm, row),
                (twist_hbm.at[det], twist),
                (col_hbm, col),
                (back_hbm, back),
                (untwist_hbm, untwist),
            )
        )
    ]
    own_bank = pltpu.make_async_copy(bank_ref.at[det], raw.at[det], own_sem.at[0])
    own_bank.start()
    pl.semaphore_wait(barrier, SEGS + DETS - 1)

    def bank_copy(o):
        other = (det + o) % DETS
        return pltpu.make_async_remote_copy(
            src_ref=bank_ref.at[other],
            dst_ref=raw.at[det],
            send_sem=bank_send.at[o],
            recv_sem=bank_recv.at[o],
            device_id={"det": other},
            device_id_type=MESH,
        )

    for o in (2, 1, 3):
        bank_copy(o).start()

    upper_det = det >= DETS // 2

    def psd_copy(target, lane):
        return pltpu.make_async_remote_copy(
            src_ref=psd_hbm.at[:, pl.ds(SHARE, SHARE)],
            dst_ref=target,
            send_sem=psd_send.at[0],
            recv_sem=psd_recv.at[lane],
            device_id=across,
            device_id_type=MESH,
        )

    to_low = psd_copy(psd_low, 0)
    to_high = psd_copy(psd_high.at[:, pl.ds(0, SHARE)], 0)
    to_rest = pltpu.make_async_remote_copy(
        src_ref=psd_hbm.at[:, pl.ds(0, 8)],
        dst_ref=psd_high.at[:, pl.ds(SHARE, 8)],
        send_sem=psd_send.at[1],
        recv_sem=psd_recv.at[1],
        device_id={"det": (det + 2) % DETS},
        device_id_type=MESH,
    )
    keep_low = pltpu.make_async_copy(psd_hbm.at[:, pl.ds(0, SHARE)], psd_low, own_sem.at[4])
    keep_high = pltpu.make_async_copy(psd_hbm.at[:, pl.ds(0, SHARE + 8)], psd_high, own_sem.at[4])

    @pl.when(upper_det)
    def _():
        to_high.start()
        to_rest.start()
        keep_high.start()

    @pl.when(jnp.logical_not(upper_det))
    def _():
        to_low.start()
        keep_low.start()

    def partner(o):
        return (me // HOME + 1 + o // HOME) % 2 * HOME + (me % HOME + o) % HOME

    def row_copy(o):
        return pltpu.make_async_remote_copy(
            src_ref=rows.at[pl.ds(o * CAP, CAP)],
            dst_ref=arrived.at[o, pl.ds(0, CAP)],
            send_sem=row_send.at[o],
            recv_sem=row_recv.at[o],
            device_id={"seg": partner(o)},
            device_id_type=MESH,
        )

    def id_copy(o):
        return pltpu.make_async_remote_copy(
            src_ref=ids.at[o],
            dst_ref=arrived_ids.at[o],
            send_sem=id_send.at[o],
            recv_sem=id_recv.at[o],
            device_id={"seg": partner(o)},
            device_id_type=MESH,
        )

    for fetch in fetches:
        fetch.start()
    own_strain.wait()
    held[...] = strain[...].astype(BF16)
    sort_ranks(me, target_ref, dest, ids)
    step = GROUP * CAP

    def send(o, _):
        id_copy(o).start()
        row_copy(o).start()
        return 0

    for g in range(SEGS // GROUP):
        want = lax.broadcasted_iota(jnp.int32, (step, LANES), 0) + g * step
        picks = [
            jnp.where(want == dest[b : b + 1, :], 1.0, 0.0).astype(BF16) for b in range(COUNT)
        ]
        picked = jnp.dot(jnp.concatenate(picks, axis=1), held[...], preferred_element_type=F32)
        rows[g * step : (g + 1) * step] = picked.astype(BF16)
        lax.fori_loop(g * GROUP + (g * GROUP == HOME), (g + 1) * GROUP, send, 0)
    own_rows = pltpu.make_async_copy(
        rows.at[pl.ds(HOME * CAP, CAP)], arrived.at[HOME, pl.ds(0, CAP)], own_sem.at[1]
    )
    own_rows.start()
    own_ids = pltpu.make_async_copy(ids.at[HOME], arrived_ids.at[HOME], own_sem.at[2])
    own_ids.start()
    arrived[:, CAP:, :] = jnp.zeros((SEGS, 64 - CAP, QU), BF16)

    own_bank.wait()
    for o in range(1, DETS):
        bank_copy(o).wait_recv()
    shift_bank(shift_ref[det], raw, bank)

    def whole_pass(source, target, lane, back):
        return pltpu.make_async_remote_copy(
            src_ref=source,
            dst_ref=target,
            send_sem=pass_send.at[lane],
            recv_sem=pass_recv.at[lane],
            device_id={"seg": (me + SEGS - back) % SEGS},
            device_id_type=MESH,
        )

    hot = (me % 32) < 2
    odd = core == 1
    to_next = whole_pass(bank.at[0], bank.at[1], 0, 1)
    to_after = whole_pass(bank.at[0], bank.at[2], 1, 2)
    onward = pltpu.make_async_remote_copy(
        src_ref=bank.at[1],
        dst_ref=bank.at[2],
        send_sem=pass_send.at[2],
        recv_sem=pass_recv.at[1],
        device_id={"seg": (me + SEGS - 1) % SEGS},
        device_id_type=MESH,
    )
    corner = (me // 32) * 32
    far = (corner + SEGS - 1) % SEGS

    def piece_copy(i):
        return pltpu.make_async_remote_copy(
            src_ref=bank.at[0, pl.ds(i * PIECE, PIECE)],
            dst_ref=relay,
            send_sem=piece_send.at[i],
            recv_sem=relay_recv.at[0],
            device_id={"seg": corner + 2 * i + core},
            device_id_type=MESH,
        )

    def last_hop(source, lane, at):
        return pltpu.make_async_remote_copy(
            src_ref=source,
            dst_ref=bank.at[1 + lane, pl.ds(at * PIECE, PIECE)],
            send_sem=piece_send.at[0],
            recv_sem=pass_recv.at[lane],
            device_id={"seg": far},
            device_id_type=MESH,
        )

    def pieces(i, _):
        piece_copy(i).start()
        return 0

    def pieces_sent(i, _):
        piece_copy(i).wait_send()
        return 0

    @pl.when(jnp.logical_or(odd, jnp.logical_not(hot)))
    def _():
        to_next.start()

    @pl.when(jnp.logical_and(odd, jnp.logical_not(hot)))
    def _():
        to_after.start()

    @pl.when(hot)
    def _():
        lax.fori_loop(1, PIECES, pieces, 0)

    @pl.when(jnp.logical_and(hot, odd))
    def _():
        last_hop(bank.at[0, pl.ds(0, PIECE)], 1, 0).start()

    @pl.when(jnp.logical_and(hot, jnp.logical_not(odd)))
    def _():
        last_hop(bank.at[0, pl.ds(0, PIECE)], 0, 0).start()

    own_rows.wait()
    own_ids.wait()

    def receive(o, _):
        id_copy(o).wait_recv()
        row_copy(o).wait_recv()
        return 0

    wide = BATCH * 64
    groups = SEGS // BATCH
    for g in (*range(groups // 2, groups), *range(groups // 2)):
        lax.fori_loop(g * BATCH + (g * BATCH == HOME), (g + 1) * BATCH, receive, 0)
        for p in range(BATCH // 2):
            o = g * BATCH + 2 * p
            ident = arrived_ids[o] + arrived_ids[o + 1] - 1
            chosen[:, p * 128 : (p + 1) * 128] = jnp.where(
                lax.broadcasted_iota(jnp.int32, (ROWS, 128), 0) == ident, 1.0, 0.0
            ).astype(BF16)
        block = arrived[g * BATCH : (g + 1) * BATCH].reshape(wide, QU)
        part = jnp.dot(chosen[...], block, preferred_element_type=F32)
        if g == groups // 2:
            total[...] = part
        else:
            total[...] += part

    def turn_copy(o, d):
        other = (det + o) % DETS
        return pltpu.make_async_remote_copy(
            src_ref=turned.at[other, d],
            dst_ref=crossed.at[o, d],
            send_sem=turn_send.at[o, d],
            recv_sem=turn_recv.at[o, d],
            device_id={"det": other},
            device_id_type=MESH,
        )

    sample = lax.broadcasted_iota(jnp.int32, (V, QU), 0) * U
    sample = sample + lax.broadcasted_iota(jnp.int32, (V, QU), 1) + det * QU
    for fetch in fetches[:3]:
        fetch.wait()
    for d in range(DETECTORS):
        begin = start_ref[0, d]
        end = begin + width_ref[0, d]
        inside = (sample >= begin) & (sample < end)
        gated = jnp.where(inside, 0.0, total[d * V : (d + 1) * V]).astype(BF16)
        folded = jnp.dot(row[...], gated, preferred_element_type=F32)
        real, imag = folded[: V // 2], folded[V // 2 :]
        cosine, sine = twist[0], twist[1]
        first = (real * cosine - imag * sine).astype(BF16)
        second = (real * sine + imag * cosine).astype(BF16)
        for q in range(DETS):
            at = PLACES[q] * SHARE
            turned[q, d, :, :QU] = first[at : at + SHARE]
            turned[q, d, :, QU:] = second[at : at + SHARE]
        for o in (2, 1, 3):
            turn_copy(o, d).start()

    @pl.when(jnp.logical_not(hot))
    def _():
        piece_copy(1).wait_recv()

    @pl.when(jnp.logical_and(jnp.logical_not(hot), odd))
    def _():
        last_hop(relay, 1, place).start()

    @pl.when(jnp.logical_and(jnp.logical_not(hot), jnp.logical_not(odd)))
    def _():
        last_hop(relay, 0, place).start()

    near = det + 1 - 2 * (det % 2)
    entry = DETS // 2 - det // 2
    beyond = DETS - 1 - det // 2 * (DETS - 1)
    middle = jnp.logical_or(det == 1, det == 2)

    def coherent_copy(block, other, lane, part):
        rows_of = pl.ds(part * PART, PART)
        return pltpu.make_async_remote_copy(
            src_ref=coherent.at[block, rows_of],
            dst_ref=coherent.at[block, rows_of],
            send_sem=coh_send.at[lane, part],
            recv_sem=coh_recv.at[block, part],
            device_id={"det": other},
            device_id_type=MESH,
        )

    def gather_rows(which, scale, shift, first_row):
        for half in range(2):
            cols = slice(half * HALF, (half + 1) * HALF)
            value = 0.0
            for d in range(DETECTORS):
                held_rows = spec[which, d * SHARE : (d + 1) * SHARE, cols]
                value = value + scale[d, shift : shift + SHARE] * held_rows
            coherent[det, first_row : first_row + SHARE, cols] = value.astype(BF16)
        for part in range(first_row // PART, (first_row + SHARE) // PART):
            coherent_copy(det, entry, 0, part).start()
            coherent_copy(det, near, 1, part).start()

    high = DETECTORS * SHARE
    row_at = lax.broadcasted_iota(jnp.int32, (high, high), 0)
    col_at = lax.broadcasted_iota(jnp.int32, (high, high), 1)
    flip = (row_at // SHARE == col_at // SHARE) & (row_at % SHARE + col_at % SHARE == SHARE - 1)
    flip = jnp.where(flip, 1.0, 0.0).astype(BF16)
    packed = lax.broadcasted_iota(jnp.int32, (high, 2 * QU), 0) % SHARE + det == 0
    imag_side = lax.broadcasted_iota(jnp.int32, (high, 2 * QU), 1) >= QU
    beside = 3 - 2 * (det % 2)
    for turn, o in enumerate((0, beside, DETS - beside, 2)):
        source = (det + DETS - o) % DETS
        if turn == 0:
            came = turned[det]
        else:
            for d in range(DETECTORS):
                turn_copy(o, d).wait_recv()
            came = crossed[o]
        came = came.reshape(high, 2 * QU)
        wide_came = came.astype(F32)
        direct = jnp.where(packed & imag_side, 0.0, wide_came).astype(BF16)
        twin = wide_came[:, QU:]
        twin = jnp.concatenate([twin, twin], axis=1) * edge_ref[source][:1]
        mirrored = jnp.where(packed, twin, wide_came).astype(BF16)
        mirrored = jnp.dot(flip, mirrored, preferred_element_type=F32).astype(BF16)
        if turn == 3:

            @pl.when(upper_det)
            def _():
                to_low.wait_recv()
                keep_high.wait()

            @pl.when(jnp.logical_not(upper_det))
            def _():
                to_high.wait_recv()
                to_rest.wait_recv()
                keep_low.wait()

        part = jnp.dot(direct, col[0, source], preferred_element_type=F32)
        if turn == 0:
            spec[0] = part
        else:
            spec[0] += part
        if turn == 3:
            gather_rows(0, psd_low, 0, 0)
        other = jnp.dot(mirrored, col[1, source], preferred_element_type=F32)
        if turn == 0:
            spec[1] = other
        else:
            spec[1] += other
    gather_rows(1, psd_high, 1, SHARE)
    to_next.wait_recv()

    @pl.when(odd)
    def _():
        onward.start()

    for fetch in fetches[3:]:
        fetch.wait()

    def multiply(block, r):
        real = coherent[block, :, :HALF].astype(F32)
        imag = coherent[block, :, HALF:].astype(F32)
        at = pl.ds(pl.multiple_of(block * QV, QV), QV)
        other_real = bank[r, at, :HALF].astype(F32)
        other_imag = bank[r, at, HALF:].astype(F32)
        into = slice(r * QV, (r + 1) * QV)
        products[into, :HALF] = (real * other_real + imag * other_imag).astype(BF16)
        products[into, HALF:] = (imag * other_real - real * other_imag).astype(BF16)

    def leave(block):
        return pltpu.make_async_copy(
            partials.at[:, :, block], out_hbm.at[:, :, block], out_sem.at[block]
        )

    def invert(block):
        for r in range(STEPS):
            multiply(block, r)
        for half in range(2):
            lanes = slice(half * HALF, (half + 1) * HALF)
            upper = slice(U + half * HALF, U + (half + 1) * HALF)
            first = jnp.dot(products[...], back[:, lanes], preferred_element_type=F32)
            second = jnp.dot(products[...], back[:, upper], preferred_element_type=F32)
            cosine, sine = untwist[block, 0, :, lanes], untwist[block, 1, :, lanes]
            for r in range(STEPS):
                real, imag = first[r * QV : (r + 1) * QV], second[r * QV : (r + 1) * QV]
                partials[r, 0, block, :, lanes] = (real * cosine - imag * sine).astype(BF16)
                partials[r, 1, block, :, lanes] = (real * sine + imag * cosine).astype(BF16)
        leave(block).start()

    def arrive(block):
        for part in range(PARTS):
            coherent_copy(block, det, 0, part).wait_recv()

    to_after.wait_recv()
    invert(det)

    @pl.when(middle)
    def _():
        for part in range(PARTS + 1):
            if part < PARTS:
                coherent_copy(entry, det, 0, part).wait_recv()
                coherent_copy(entry, near, 2, part).start()
            if part > 0:
                coherent_copy(beyond, det, 0, part - 1).wait_recv()
                coherent_copy(beyond, near, 3, part - 1).start()

    arrive(near)
    invert(near)

    @pl.when(jnp.logical_not(middle))
    def _():
        arrive(entry)

    invert(entry)

    @pl.when(jnp.logical_not(middle))
    def _():
        arrive(beyond)

    invert(beyond)

    @pl.when(upper_det)
    def _():
        to_high.wait_send()
        to_rest.wait_send()

    @pl.when(jnp.logical_not(upper_det))
    def _():
        to_low.wait_send()

    @pl.when(jnp.logical_or(odd, jnp.logical_not(hot)))
    def _():
        to_next.wait_send()

    @pl.when(jnp.logical_and(odd, jnp.logical_not(hot)))
    def _():
        to_after.wait_send()

    @pl.when(hot)
    def _():
        lax.fori_loop(1, PIECES, pieces_sent, 0)

    last_hop(relay, 0, place).wait_send()

    @pl.when(odd)
    def _():
        onward.wait_send()

    def sent(o, _):
        id_copy(o).wait_send()
        row_copy(o).wait_send()
        return 0

    lax.fori_loop(0, HOME, sent, 0)
    lax.fori_loop(HOME + 1, SEGS, sent, 0)
    for o in range(1, DETS):
        bank_copy(o).wait_send()
        for d in range(DETECTORS):
            turn_copy(o, d).wait_send()
    for part in range(PARTS):
        coherent_copy(det, entry, 0, part).wait_send()
        coherent_copy(det, near, 1, part).wait_send()

    @pl.when(middle)
    def _():
        for part in range(PARTS):
            coherent_copy(entry, near, 2, part).wait_send()
            coherent_copy(beyond, near, 3, part).wait_send()

    for block in range(DETS):
        leave(block).wait()


def filtered(*operands):
    dma = pltpu.SemaphoreType.DMA
    return pl.pallas_call(
        filter_kernel,
        out_shape=jax.ShapeDtypeStruct((STEPS, 2, DETS, QV, U), BF16),
        in_specs=[SM, SM, SM, VM, VM] + [HB] * 8,
        out_specs=HB,
        scratch_shapes=[
            pltpu.VMEM((SLOTS, QU), F32),
            pltpu.VMEM((SLOTS, QU), BF16),
            pltpu.VMEM((16, LANES), jnp.int32),
            pltpu.VMEM((SLOTS, QU), BF16),
            pltpu.VMEM((SEGS, 1, 128), jnp.int32),
            pltpu.VMEM((SEGS, 64, QU), BF16),
            pltpu.VMEM((SEGS, 1, 128), jnp.int32),
            pltpu.VMEM((ROWS, BATCH * 64), BF16),
            pltpu.VMEM((ROWS, QU), F32),
            pltpu.VMEM((DETS, QV, 2, HALF), BF16),
            pltpu.VMEM((STEPS, V, U), BF16),
            pltpu.VMEM((PIECE, U), BF16),
            pltpu.VMEM((DETS, DETECTORS, SHARE, 2 * QU), BF16),
            pltpu.VMEM((DETS, DETECTORS, SHARE, 2 * QU), BF16),
            pltpu.VMEM((2, DETECTORS * SHARE, U), F32),
            pltpu.VMEM((DETS, QV, U), BF16),
            pltpu.VMEM((DETECTORS, SHARE, HALF), F32),
            pltpu.VMEM((DETECTORS, SHARE + 8, HALF), F32),
            pltpu.VMEM((V, V), BF16),
            pltpu.VMEM((2, V // 2, QU), F32),
            pltpu.VMEM((2, DETS, 2 * QU, U), BF16),
            pltpu.VMEM((U, 2 * U), BF16),
            pltpu.VMEM((DETS, 2, QV, U), F32),
            pltpu.VMEM((STEPS * QV, U), BF16),
            pltpu.VMEM((STEPS, 2, DETS, QV, U), BF16),
            dma((SEGS,)), dma((SEGS,)), dma((SEGS,)), dma((SEGS,)),
            dma((DETS,)), dma((DETS,)),
            dma((DETS, DETECTORS)), dma((DETS, DETECTORS)),
            dma((4, PARTS)), dma((DETS, PARTS)), dma((DETS,)),
            dma((3,)), dma((2,)), dma((PIECES,)), dma((1,)), dma((2,)), dma((2,)), dma((5,)), dma((5,)),
        ],
        compiler_params=pltpu.CompilerParams(
            vmem_limit_bytes=LIMIT, collective_id=0, has_side_effects=True
        ),
        cost_estimate=pl.CostEstimate(
            flops=12_000_000_000, bytes_accessed=16_000_000, transcendentals=0
        ),
        name="filtered",
    )(*operands)


COLUMNS = 1024


def last_kernel(partial_ref, last_ref, out_ref):
    made = jnp.dot(last_ref[...], partial_ref[0], preferred_element_type=F32)
    out_ref[0, 0, 0] = made.astype(BF16).reshape(V // 2, 2, COLUMNS)


def last_rows(partials, last):
    return pl.pallas_call(
        last_kernel,
        grid=(STEPS, U // COLUMNS),
        out_shape=jax.ShapeDtypeStruct((1, 1, STEPS, V // 2, 2, U), BF16),
        in_specs=[
            pl.BlockSpec((1, 2 * V, COLUMNS), lambda r, c: (r, 0, c)),
            pl.BlockSpec((V, 2 * V), lambda r, c: (0, 0)),
        ],
        out_specs=pl.BlockSpec((1, 1, 1, V // 2, 2, COLUMNS), lambda r, c: (0, 0, r, 0, 0, c)),
        compiler_params=pltpu.CompilerParams(vmem_limit_bytes=LIMIT),
        name="last_rows",
    )(partials, last)


def body(strain, row_target, gate_start, gate_width, inverse_psd, templates, template_shift):
    row, twist, edge, col, back, untwist, last = (jnp.asarray(t) for t in tables())
    partials = filtered(
        gate_start,
        gate_width,
        template_shift,
        row_target,
        edge,
        templates,
        strain,
        inverse_psd,
        row,
        twist,
        col,
        back,
        untwist,
    )
    return last_rows(partials.reshape(STEPS, 2 * V, U), last)


def solution(mesh):
    in_specs = (
        P("seg", "det"),
        P("seg"),
        P("seg", None),
        P("seg", None),
        P(None, "det", None),
        P("seg", "det", None, None),
        P("seg"),
    )
    out_specs = P("seg", "det", None, None, None, None)
    return jax.shard_map(body, mesh=mesh, in_specs=in_specs, out_specs=out_specs, check_vma=False)
```
